32 devices in a mesh: batch: 8 (over y, x, core), seq: 4 (over z).
Axes of the slice: x: 2, y: 2, z: 4, core: 2. Of those that a mesh axis runs over, the one named last changes fastest.
Arguments:
- patches: bfloat16 [16, 1024, 1152], P('batch', 'seq'), may hold values from -6 to 6
- timesteps: int32 [16], P('batch'), may hold values from 0 to 999
- labels: int32 [16], P('batch'), may hold values from 0 to 1000
- next_grad: bfloat16 [16, 1024, 1152], P('batch', 'seq'), may hold values from -6 to 6
- skip_grad: bfloat16 [16, 1024, 1152], P('batch', 'seq'), may hold values from -6 to 6
- next_extra: bfloat16 [16, 2, 1152], P('batch'), may hold values from -6 to 6
- skip_extra: bfloat16 [16, 2, 1152], P('batch'), may hold values from -6 to 6
- w_qkv: float32 [1152, 3456], P(None, ('batch', 'seq')), may hold values from -0.1875 to 0.1875
- w_proj: float32 [1152, 1152], P(None, ('batch', 'seq')), may hold values from -1.25 to 1.25
- w_up: float32 [1152, 4608], P(None, ('batch', 'seq')), may hold values from -0.1875 to 0.1875
- w_down: float32 [4608, 1152], P(('batch', 'seq')), may hold values from -0.09375 to 0.09375
- mom_qkv: float32 [1152, 3456], P(None, ('batch', 'seq'))
- mom_proj: float32 [1152, 1152], P(None, ('batch', 'seq'))
- mom_up: float32 [1152, 4608], P(None, ('batch', 'seq'))
- mom_down: float32 [4608, 1152], P(('batch', 'seq'))
- vectors: float32 [10, 1152], P(None, ('batch', 'seq'))
- vec_first: float32 [10, 1152], P(None, ('batch', 'seq')), may hold values from -64 to 64
- vec_second: float32 [10, 1152], P(None, ('batch', 'seq')), may hold values from 19.6992 to 73.872
- table: float32 [1001, 1152], P(None, ('batch', 'seq')), may hold values from -6 to 6
- table_first: float32 [1001, 1152], P(None, ('batch', 'seq')), may hold values from -2.5 to 2.5
- table_second: float32 [1001, 1152], P(None, ('batch', 'seq')), may hold values from 0.0022 to 0.009
Outputs:
- y_patches: bfloat16 [16, 1024, 1152], P('batch', 'seq')
- y_extras: bfloat16 [16, 2, 1152], P('batch')
- dx_patches: bfloat16 [16, 1024, 1152], P('batch', 'seq')
- w_qkv_new: float32 [1152, 3456], P(None, ('batch', 'seq'))
- w_proj_new: float32 [1152, 1152], P(None, ('batch', 'seq'))
- w_up_new: float32 [1152, 4608], P(None, ('batch', 'seq'))
- w_down_new: float32 [4608, 1152], P(('batch', 'seq'))
- mom_qkv_new: float32 [1152, 3456], P(None, ('batch', 'seq'))
- mom_proj_new: float32 [1152, 1152], P(None, ('batch', 'seq'))
- mom_up_new: float32 [1152, 4608], P(None, ('batch', 'seq'))
- mom_down_new: float32 [4608, 1152], P(('batch', 'seq'))
- vec_first_new: float32 [10, 1152], P(None, ('batch', 'seq'))
- vec_second_new: float32 [10, 1152], P(None, ('batch', 'seq'))
- vectors_new: float32 [10, 1152], P(None, ('batch', 'seq'))
- table_first_new: float32 [1001, 1152], P(None, ('batch', 'seq'))
- table_second_new: float32 [1001, 1152], P(None, ('batch', 'seq'))
- table_new: float32 [1001, 1152], P(None, ('batch', 'seq'))
The draws below stay inside these ranges and needn't reach their ends.
All inputs are finite; a program needn't handle non-finite values.
Results may differ from the reference program's by a relative error of at most 0.02.
Values may be sent and summed in bfloat16 or wider, within the bound.
No kernel may reach another device: no remote copies, remote signals or barrier semaphores. Data moves between devices by JAX's collectives and lax.ppermute only.
A program may use at most 384 MiB of HBM per device.

```python
import math
import jax
import jax.numpy as jnp
from jax import lax

D = 1152
HEADS = 16
HEAD_DIM = 72
FF = 4608
PATCHES = 1024
CLASSES = 1001
EXTRA = 2
NS_STEPS = 5
STEP = 10
IMAGES = 16
SEQ_LEN = 1026
N_BATCH = 8
N_SEQ = 4


def rising_scale(extent, long_axis, growth, coefficient):
    length = extent[long_axis]
    position = lax.broadcasted_iota(jnp.int32, extent, long_axis)
    block_index = position // (length // (N_BATCH * N_SEQ))
    seq_rank = (block_index % N_SEQ).astype(jnp.float32)
    return coefficient * (IMAGES * SEQ_LEN) ** 0.5 * growth ** (seq_rank / max(N_SEQ - 1, 1))


def draw_mom_qkv(key, part):
    key = jax.random.fold_in(key, 11)
    extent = (D, 3 * D)
    samples = jax.random.truncated_normal(key, -4.0, 4.0, extent, jnp.float32)
    growth = 3.0
    return samples * rising_scale(extent, 1, growth, 0.6)


def draw_mom_proj(key, part):
    key = jax.random.fold_in(key, 12)
    extent = (D, D)
    samples = jax.random.truncated_normal(key, -4.0, 4.0, extent, jnp.float32)
    growth = 3.0
    return samples * rising_scale(extent, 1, growth, 0.2)


def draw_mom_up(key, part):
    key = jax.random.fold_in(key, 13)
    extent = (D, FF)
    samples = jax.random.truncated_normal(key, -4.0, 4.0, extent, jnp.float32)
    growth = 3.0
    return samples * rising_scale(extent, 1, growth, 0.4)


def draw_mom_down(key, part):
    key = jax.random.fold_in(key, 14)
    extent = (FF, D)
    samples = jax.random.truncated_normal(key, -4.0, 4.0, extent, jnp.float32)
    growth = 3.0
    return samples * rising_scale(extent, 0, growth, 0.9)


def draw_vectors(key, part):
    key = jax.random.fold_in(key, 21)
    extent = (10, D)
    samples = jax.random.truncated_normal(key, -4.0, 4.0, extent, jnp.float32)
    row_index = lax.broadcasted_iota(jnp.int32, extent, 0)
    is_gain = (row_index == 0) | (row_index == 2)
    return jnp.where(is_gain, 1.0 + 0.1 * samples, 0.2 * samples)


def touch_ends(values, key, low, high):
    shape = values.shape
    spot = [jax.random.randint(jax.random.fold_in(key, axis), (), 0, shape[axis]) for axis in range(len(shape))]
    values = values.at[tuple(spot)].set(low)
    longest = shape.index(max(shape))
    spot[longest] = (spot[longest] + 1) % shape[longest]
    return values.at[tuple(spot)].set(high)


def block_levels(key, shape, split, smallest, top_value):
    def one(dim, blocks):
        draws = jax.random.uniform(jax.random.fold_in(jax.random.fold_in(key, 6), dim), (blocks,), jnp.float32, smallest / len(split), top_value / len(split))
        return jnp.repeat(jnp.exp(draws), shape[dim] // blocks).reshape((-1,) + (1,) * (len(shape) - dim - 1))

    gain = one(*split[0])
    for cut in split[1:]:
        gain = gain * one(*cut)
    return gain


def bell_draw(rng, shape, scale, reach, cuts=(), held_as=jnp.bfloat16):
    drawn = jax.random.normal(rng, shape, jnp.float32) * scale
    if len(cuts) > 0:
        drawn = block_levels(rng, shape, cuts, -0.22, 0.18) * drawn
    return jnp.clip(drawn, min=-reach, max=reach).astype(held_as)


def setup_inputs(seed: int = 0) -> dict:
    seeds = jax.random.split(jax.random.key(seed), 22)
    patches = bell_draw(seeds[0], (IMAGES, PATCHES, D), 1.0, 6.0, ((0, 8), (1, 4)))
    timesteps = touch_ends(jax.random.randint(seeds[1], (IMAGES,), 0, 1000), jax.random.fold_in(seeds[1], 1), 0, 999).astype(jnp.int32)
    labels = touch_ends(jax.random.randint(seeds[2], (IMAGES,), 0, CLASSES), jax.random.fold_in(seeds[2], 1), 0, CLASSES - 1).astype(jnp.int32)
    next_grad = bell_draw(seeds[3], (IMAGES, PATCHES, D), 0.7, 6.0, ((0, 8), (1, 4)))
    skip_grad = bell_draw(seeds[4], (IMAGES, PATCHES, D), 0.7, 6.0, ((0, 8), (1, 4)))
    next_extra = bell_draw(seeds[5], (IMAGES, EXTRA, D), 0.7, 6.0, ((0, 8),))
    skip_extra = bell_draw(seeds[6], (IMAGES, EXTRA, D), 0.7, 6.0, ((0, 8),))
    w_qkv = bell_draw(seeds[7], (D, 3 * D), D ** -0.5, 0.1875, ((1, 32),), jnp.float32)
    w_proj = bell_draw(seeds[8], (D, D), (D // 48) ** -0.5, 1.25, ((1, 32),), jnp.float32)
    w_up = bell_draw(seeds[9], (D, FF), D ** -0.5, 0.1875, ((1, 32),), jnp.float32)
    w_down = bell_draw(seeds[10], (FF, D), FF ** -0.5, 0.09375, ((0, 32),), jnp.float32)
    mom_qkv = draw_mom_qkv(jax.random.fold_in(seeds[21], 71), 0)
    mom_proj = draw_mom_proj(jax.random.fold_in(seeds[21], 71), 0)
    mom_up = draw_mom_up(jax.random.fold_in(seeds[21], 71), 0)
    mom_down = draw_mom_down(jax.random.fold_in(seeds[21], 71), 0)
    vectors = draw_vectors(jax.random.fold_in(seeds[21], 71), 0)
    vec_first = bell_draw(seeds[16], (10, D), (0.09 * (IMAGES * SEQ_LEN) ** 0.5), 64.0, ((1, 32),), jnp.float32)
    vec_second = jnp.clip(jnp.exp(math.log(73.872) - 1.3217559 * jax.random.uniform(seeds[17], (10, D), jnp.float32) ** block_levels(seeds[17], (10, D), ((1, 32),), -0.2, 0.2)), 19.6992, 73.872)
    table = bell_draw(seeds[18], (CLASSES, D), 1.0, 6.0, ((1, 32),), jnp.float32)
    table_first = bell_draw(seeds[19], (CLASSES, D), 0.17, 2.5, ((1, 32),), jnp.float32)
    table_second = jnp.clip(jnp.exp(math.log(0.009) - 1.4087672 * jax.random.uniform(seeds[20], (CLASSES, D), jnp.float32) ** block_levels(seeds[20], (CLASSES, D), ((1, 32),), -0.2, 0.2)), 0.0022, 0.009)
    return dict(patches=patches, timesteps=timesteps, labels=labels, next_grad=next_grad, skip_grad=skip_grad, next_extra=next_extra, skip_extra=skip_extra, w_qkv=w_qkv, w_proj=w_proj, w_up=w_up, w_down=w_down, mom_qkv=mom_qkv, mom_proj=mom_proj, mom_up=mom_up, mom_down=mom_down, vectors=vectors, vec_first=vec_first, vec_second=vec_second, table=table, table_first=table_first, table_second=table_second)


@jax.custom_vjp
def low(v):
    return lax.optimization_barrier(v.astype(jnp.bfloat16)).astype(jnp.float32)

@jax.custom_vjp
def low_back(v):
    return v

def low_keep(v):
    return (low(v), None)

def low_pass(kept, grad):
    return (grad,)

def back_keep(v):
    return (v, None)

def back_low(kept, grad):
    return (low(grad),)
low.defvjp(low_keep, low_pass)
low_back.defvjp(back_keep, back_low)
norm_eps = 1e-05
poly_first = 3.4445
poly_second = -4.775
poly_third = 2.0315
muon_momentum = 0.95
muon_rate = 1.5
muon_decay = 0.01
beta_one = 0.9
beta_two = 0.999
adam_rate = 1.0
adam_eps = 1e-08
highest = lax.Precision.HIGHEST

def standardize(values):
    average = lax.optimization_barrier(jnp.mean(values, axis=-1, keepdims=True))
    centred = values - average
    variance = lax.optimization_barrier(jnp.mean(centred * centred, axis=-1, keepdims=True))
    return centred * lax.rsqrt(variance + norm_eps)

def time_tokens(step_values, model_width):
    half_width = model_width // 2
    frequency = jnp.exp(-math.log(10000.0) * jnp.arange(half_width, dtype=jnp.float32) / half_width)
    angles = step_values.astype(jnp.float32)[:, None] * frequency[None, :]
    return jnp.concatenate([jnp.cos(angles), jnp.sin(angles)], axis=-1)

def forward(params, patch_group, label_group, time_group):
    w_qkv, w_proj, w_up, w_down, vectors, table = [low(member) for member in params]
    images = patch_group.shape[0]
    class_rows = table[label_group]
    extras = jnp.stack([time_tokens(time_group, D), class_rows], axis=1)
    tokens = jnp.concatenate([extras, patch_group], axis=1)
    normed = low(standardize(tokens) * vectors[0] + vectors[1])
    packed = low_back(low(jnp.einsum('gtd,de->gte', normed, w_qkv, precision=highest)))
    queries = packed[..., :D].reshape(images, SEQ_LEN, HEADS, HEAD_DIM)
    key_rows = packed[..., D:2 * D].reshape(images, SEQ_LEN, HEADS, HEAD_DIM)
    values = packed[..., 2 * D:].reshape(images, SEQ_LEN, HEADS, HEAD_DIM)
    scores = low_back(jnp.einsum('gqhe,gkhe->ghqk', queries, key_rows, precision=highest) * HEAD_DIM ** (-0.5))
    largest = lax.optimization_barrier(jnp.max(scores, axis=-1, keepdims=True))
    powers = jnp.exp(scores - largest)
    attention = powers / lax.optimization_barrier(jnp.sum(powers, axis=-1, keepdims=True))
    attended = jnp.einsum('ghqk,gkhe->gqhe', attention, values, precision=highest).reshape(images, SEQ_LEN, D)
    attended = low_back(low(attended))
    branch = low_back(jnp.einsum('gtd,de->gte', attended, w_proj, precision=highest) + vectors[4])
    middle = tokens + branch
    normed_two = low(standardize(middle) * vectors[2] + vectors[3])
    hidden = low_back(jnp.einsum('gtd,de->gte', normed_two, w_up, precision=highest) + vectors[6:].reshape(-1))
    activated = low(jax.nn.gelu(hidden, approximate=False))
    return middle + low_back(jnp.einsum('gtd,de->gte', activated, w_down, precision=highest) + vectors[5])

def orthogonalize(matrix):
    square_sum = jnp.sum(matrix * matrix)
    current = matrix / (jnp.sqrt(square_sum) + 1e-07)
    for sweep in range(NS_STEPS):
        gram_matrix = jnp.dot(current, current.T, precision=highest)
        square = jnp.dot(gram_matrix, gram_matrix, precision=highest)
        mixing = poly_second * gram_matrix + poly_third * square
        current = poly_first * current + jnp.dot(mixing, current, precision=highest)
    return current

def muon_step(weight, momentum, gradient, flipped):
    momentum_new = muon_momentum * momentum + gradient
    if flipped:
        ortho = orthogonalize(momentum_new.T).T
    else:
        ortho = orthogonalize(momentum_new)
    factor = math.sqrt(max(1.0, weight.shape[1] / weight.shape[0]))
    return (weight * (1.0 - muon_rate * muon_decay) - muon_rate * factor * ortho, momentum_new)

def adam_step(parameter, first_state, second, gradient):
    first_new = beta_one * first_state + (1.0 - beta_one) * gradient
    second_new = beta_two * second + (1.0 - beta_two) * gradient * gradient
    first_hat = first_new / (1.0 - beta_one ** STEP)
    second_hat = second_new / (1.0 - beta_two ** STEP)
    return (first_new, second_new, parameter - adam_rate * first_hat / (jnp.sqrt(second_hat) + adam_eps))

def reference(patches, timesteps, labels, next_grad, skip_grad, next_extra, skip_extra, w_qkv, w_proj, w_up, w_down, mom_qkv, mom_proj, mom_up, mom_down, vectors, vec_first, vec_second, table, table_first, table_second):
    weights = (w_qkv, w_proj, w_up, w_down, vectors, table)
    groups = IMAGES // 4

    def regroup(array):
        return array.reshape((groups, 4) + array.shape[1:])
    cotangent = jnp.concatenate([next_extra.astype(jnp.float32) + skip_extra.astype(jnp.float32), next_grad.astype(jnp.float32) + skip_grad.astype(jnp.float32)], axis=1)

    def one_group(totals, inputs):
        patch_group, label_group, time_group, cot_group = inputs

        def wrapped(params, patch_in):
            return forward(params, patch_in, label_group, time_group)
        output, pullback = jax.vjp(wrapped, weights, patch_group.astype(jnp.float32))
        param_grads, patch_grads = pullback(cot_group)
        totals = jax.tree.map(lambda summed, adding: summed + adding, totals, param_grads)
        return (totals, (output.astype(jnp.bfloat16), patch_grads.astype(jnp.bfloat16)))
    zeros = tuple((jnp.zeros_like(member) for member in weights))
    totals, (outputs, patch_grads) = lax.scan(one_group, zeros, (regroup(patches), regroup(labels), regroup(timesteps), regroup(cotangent)))
    outputs = outputs.reshape(IMAGES, SEQ_LEN, D)
    patch_grads = patch_grads.reshape(IMAGES, PATCHES, D)
    grad_qkv, grad_proj, grad_up, grad_down, grad_vec, grad_tab = totals
    w_qkv_new, mom_qkv_new = muon_step(w_qkv, mom_qkv, grad_qkv, False)
    w_proj_new, mom_proj_new = muon_step(w_proj, mom_proj, grad_proj, False)
    w_up_new, mom_up_new = muon_step(w_up, mom_up, grad_up, False)
    w_down_new, mom_down_new = muon_step(w_down, mom_down, grad_down, True)
    vec_first_new, vec_second_new, vectors_new = adam_step(vectors, vec_first, vec_second, grad_vec)
    table_first_new, table_second_new, table_new = adam_step(table, table_first, table_second, grad_tab)
    return (outputs[:, 2:], outputs[:, :2], patch_grads, w_qkv_new, w_proj_new, w_up_new, w_down_new, mom_qkv_new, mom_proj_new, mom_up_new, mom_down_new, vec_first_new, vec_second_new, vectors_new, table_first_new, table_second_new, table_new)
```

```python
import functools
import math

import jax
import jax.numpy as jnp
from jax import lax
from jax.experimental import pallas as pl
from jax.experimental.pallas import tpu as pltpu
from jax.sharding import PartitionSpec as P

HEADS = 16
STEP = 10
FIRST_STEPS = 3
LAST_STEPS = 2

norm_eps = 1e-05
poly_first = 3.4445
poly_second = -4.775
poly_third = 2.0315
muon_momentum = 0.95
muon_rate = 1.5
muon_decay = 0.01
beta_one = 0.9
beta_two = 0.999
adam_rate = 1.0
adam_eps = 1e-08
highest = lax.Precision.HIGHEST
BF = jnp.bfloat16
F32 = jnp.float32
LOG2E = math.log2(math.e)
MIB = 1024 * 1024


def dot_nt(former, latter):
    return lax.dot_general(former, latter, (((1,), (1,)), ((), ())), preferred_element_type=F32)


def dot_nn(former, latter):
    return lax.dot_general(former, latter, (((1,), (0,)), ((), ())), preferred_element_type=F32)


def dot_tn(former, latter):
    return lax.dot_general(former, latter, (((0,), (0,)), ((), ())), preferred_element_type=F32)


def in_vmem(count):
    return [pl.BlockSpec(memory_space=pltpu.VMEM)] * count


def shape_of(shape, dtype):
    return jax.ShapeDtypeStruct(shape, dtype)


def head_window(head, size, width):
    start = jnp.minimum((head * size) // 128, (width - 256) // 128) * 128
    return pl.multiple_of(start, 128), head * size - start


def attention_forward_kernel(groups, valid_ref, own_ref, *refs):
    others, (o_ref, lse_ref, lsex_ref, acc) = refs[: groups - 1], refs[groups - 1 :]
    rows = own_ref.shape[0] - 16
    width = own_ref.shape[1] // 3
    size = width // HEADS
    factor = size**-0.5 * LOG2E
    tables = [(own_ref, width, 2 * width)] + [(ref, 0, width) for ref in others]
    parts = []
    for group, (ref, key_at, value_at) in enumerate(tables):
        parts.append((ref, pl.ds(0, rows), key_at, value_at, None))
        parts.append((ref, pl.ds(rows, 16), key_at, value_at, valid_ref[group]))
    acc[...] = jnp.zeros_like(acc)
    tile_row = lax.broadcasted_iota(jnp.int32, (16, rows), 0)

    def one_head(head, carry):
        start, offset = head_window(head, size, width)
        lane = lax.broadcasted_iota(jnp.int32, (rows, 256), 1)
        mask = (lane >= offset) & (lane < offset + size)
        query = jnp.where(mask, own_ref[:rows, pl.ds(start, 256)], jnp.zeros((), BF))
        scores = []
        for ref, span, key_at, value_at, valid in parts:
            score = dot_nt(ref[span, pl.ds(pl.multiple_of(key_at + start, 128), 256)], query)
            if valid is not None:
                score = jnp.where(tile_row < valid, score, -1e30)
            scores.append(score)
        largest = functools.reduce(
            jnp.maximum, [jnp.max(score, axis=0, keepdims=True) for score in scores]
        )
        largest = largest * factor
        total = jnp.zeros((1, rows), F32)
        out = jnp.zeros((256, rows), F32)
        for score, (ref, span, key_at, value_at, valid) in zip(scores, parts):
            power = jnp.exp2(score * factor - largest)
            total = total + jnp.sum(power, axis=0, keepdims=True)
            values = ref[span, pl.ds(pl.multiple_of(value_at + start, 128), 256)]
            out = out + dot_tn(values, power.astype(BF))
        out = (out * (1.0 / total)).T
        acc[:, pl.ds(start, 256)] += jnp.where(mask, out, 0.0)
        lse_ref[pl.ds(head, 1), :] = largest + jnp.log2(total)
        return carry

    lax.fori_loop(0, HEADS, one_head, 0)
    o_ref[:rows, :] = acc[...].astype(BF)
    head_row = lax.broadcasted_iota(jnp.int32, (HEADS, width), 0)
    lane = lax.broadcasted_iota(jnp.int32, (HEADS, width), 1)
    diagonal = (lane >= head_row * size) & (lane < head_row * size + size)
    extra = jnp.broadcast_to(own_ref[rows : rows + 16, :width].astype(F32)[0:1], (HEADS, width))
    extra = jnp.where(diagonal, extra, 0.0).astype(BF)
    tile_lane = lax.broadcasted_iota(jnp.int32, (HEADS, 16), 1)
    scores = []
    for ref, span, key_at, value_at, valid in parts:
        score = dot_nt(extra, ref[span, key_at : key_at + width])
        if valid is not None:
            score = jnp.where(tile_lane < valid, score, -1e30)
        scores.append(score)
    largest = functools.reduce(
        jnp.maximum, [jnp.max(score, axis=1, keepdims=True) for score in scores]
    )
    largest = largest * factor
    total = jnp.zeros((HEADS, 1), F32)
    out = jnp.zeros((HEADS, width), F32)
    for score, (ref, span, key_at, value_at, valid) in zip(scores, parts):
        power = jnp.exp2(score * factor - largest)
        total = total + jnp.sum(power, axis=1, keepdims=True)
        out = out + dot_nn(power.astype(BF), ref[span, value_at : value_at + width])
    out = jnp.sum(jnp.where(diagonal, out * (1.0 / total), 0.0), axis=0, keepdims=True)
    first = lax.broadcasted_iota(jnp.int32, (16, width), 0) < valid_ref[0]
    o_ref[rows:, :] = jnp.where(first, jnp.broadcast_to(out, (16, width)), 0.0).astype(BF)
    lsex_ref[...] = jnp.broadcast_to(largest + jnp.log2(total), (HEADS, 128))


def attention_forward(valid, own, others):
    padded, wide = own.shape
    rows, width, groups = padded - 16, wide // 3, 1 + len(others)
    pairs = rows * groups * rows
    return pl.pallas_call(
        functools.partial(attention_forward_kernel, groups),
        out_shape=[
            shape_of((padded, width), BF),
            shape_of((HEADS, rows), F32),
            shape_of((HEADS, 128), F32),
        ],
        in_specs=[pl.BlockSpec(memory_space=pltpu.SMEM)] + in_vmem(groups),
        out_specs=in_vmem(3),
        scratch_shapes=[pltpu.VMEM((rows, width), F32)],
        compiler_params=pltpu.CompilerParams(vmem_limit_bytes=60 * MIB),
        cost_estimate=pl.CostEstimate(
            flops=16 * pairs * width,
            bytes_accessed=groups * padded * wide * 2,
            transcendentals=HEADS * pairs,
        ),
        name="attention_forward",
    )(valid, own, *others)


def attention_backward_kernel(groups, valid_ref, own_ref, *refs):
    others, refs = refs[: groups - 1], refs[groups - 1 :]
    o_ref, do_ref, lse_ref, lsex_ref = refs[:4]
    dq_ref, dkv_refs, refs = refs[4], refs[5 : 5 + groups], refs[5 + groups :]
    dq_acc, dk_acc, dv_acc, delta = refs
    rows = own_ref.shape[0] - 16
    padded = rows + 16
    width = own_ref.shape[1] // 3
    size = width // HEADS
    scale = size**-0.5
    factor = scale * LOG2E
    tables = [(own_ref, width, 2 * width)] + [(ref, 0, width) for ref in others]
    parts = []
    for group, (ref, key_at, value_at) in enumerate(tables):
        parts.append((ref, 0, rows, key_at, value_at, group, None))
        parts.append((ref, rows, 16, key_at, value_at, group, valid_ref[group]))
    head_row = lax.broadcasted_iota(jnp.int32, (HEADS, width), 0)
    lane = lax.broadcasted_iota(jnp.int32, (HEADS, width), 1)
    diagonal = (lane >= head_row * size) & (lane < head_row * size + size)
    ones = jnp.where(diagonal, 1.0, 0.0).astype(BF)
    product = do_ref[:rows, :].astype(F32) * o_ref[:rows, :].astype(F32)
    upper = product.astype(BF)
    lower = (product - upper.astype(F32)).astype(BF)
    delta[...] = dot_nt(ones, upper) + dot_nt(ones, lower)
    extra = jnp.broadcast_to(own_ref[rows:padded, :width].astype(F32)[0:1], (HEADS, width))
    extra = jnp.where(diagonal, extra, 0.0).astype(BF)
    extra_do = jnp.broadcast_to(do_ref[rows:padded, :].astype(F32)[0:1], (HEADS, width))
    extra_do = jnp.where(diagonal, extra_do, 0.0)
    extra_o = o_ref[rows:padded, :].astype(F32)[0:1]
    extra_delta = jnp.sum(extra_do * extra_o, axis=1, keepdims=True)
    extra_do = extra_do.astype(BF)
    extra_lse = lsex_ref[:, 0:1]
    tile_lane = lax.broadcasted_iota(jnp.int32, (HEADS, 16), 1)
    extra_dq = jnp.zeros((HEADS, width), F32)
    for ref, at, count, key_at, value_at, group, valid in parts:
        keys = ref[at : at + count, key_at : key_at + width]
        values = ref[at : at + count, value_at : value_at + width]
        prob = jnp.exp2(dot_nt(extra, keys) * factor - extra_lse)
        if valid is not None:
            prob = jnp.where(tile_lane < valid, prob, 0.0)
        score_grad = (prob * (dot_nt(extra_do, values) - extra_delta)).astype(BF)
        extra_dq = extra_dq + dot_nn(score_grad, keys)
        dk_acc[group, at : at + count, :] = dot_tn(score_grad, extra)
        dv_acc[group, at : at + count, :] = dot_tn(prob.astype(BF), extra_do)
    extra_dq = jnp.sum(jnp.where(diagonal, extra_dq, 0.0), axis=0, keepdims=True) * scale
    first = lax.broadcasted_iota(jnp.int32, (16, width), 0) < valid_ref[0]
    dq_ref[rows:, :] = jnp.where(first, jnp.broadcast_to(extra_dq, (16, width)), 0.0).astype(BF)
    dq_acc[...] = jnp.zeros_like(dq_acc)
    tile_row = lax.broadcasted_iota(jnp.int32, (16, rows), 0)

    def one_head(head, carry):
        start, offset = head_window(head, size, width)
        window = pl.ds(start, 256)
        lanes = lax.broadcasted_iota(jnp.int32, (rows, 256), 1)
        mask = (lanes >= offset) & (lanes < offset + size)
        zero = jnp.zeros((), BF)
        query = jnp.where(mask, own_ref[:rows, window], zero)
        out_grad = jnp.where(mask, do_ref[:rows, window], zero)
        lse = lse_ref[pl.ds(head, 1), :]
        row_delta = delta[pl.ds(head, 1), :]
        query_grad = jnp.zeros((256, rows), F32)
        for ref, at, count, key_at, value_at, group, valid in parts:
            keys = ref[at : at + count, pl.ds(pl.multiple_of(key_at + start, 128), 256)]
            values = ref[at : at + count, pl.ds(pl.multiple_of(value_at + start, 128), 256)]
            prob = jnp.exp2(dot_nt(keys, query) * factor - lse)
            if valid is not None:
                prob = jnp.where(tile_row < valid, prob, 0.0)
            score_grad = (prob * (dot_nt(values, out_grad) - row_delta)).astype(BF)
            dv_acc[group, at : at + count, window] += dot_nn(prob.astype(BF), out_grad)
            dk_acc[group, at : at + count, window] += dot_nn(score_grad, query)
            query_grad = query_grad + dot_tn(keys, score_grad)
        dq_acc[:, window] += jnp.where(mask, query_grad.T, 0.0)
        return carry

    lax.fori_loop(0, HEADS, one_head, 0)
    dq_ref[:rows, :] = (dq_acc[...] * scale).astype(BF)
    for group, dkv_ref in enumerate(dkv_refs):
        dkv_ref[:, :width] = (dk_acc[group] * scale).astype(dkv_ref.dtype)
        dkv_ref[:, width:] = dv_acc[group].astype(dkv_ref.dtype)


def attention_backward(valid, own, others, attended, attended_grad, lse, lse_extra):
    padded, wide = own.shape
    rows, width, groups = padded - 16, wide // 3, 1 + len(others)
    pairs = rows * groups * rows
    return pl.pallas_call(
        functools.partial(attention_backward_kernel, groups),
        out_shape=[shape_of((padded, width), BF)]
        + [shape_of((padded, 2 * width), BF) for _ in range(groups)],
        in_specs=[pl.BlockSpec(memory_space=pltpu.SMEM)] + in_vmem(groups + 4),
        out_specs=in_vmem(1 + groups),
        scratch_shapes=[
            pltpu.VMEM((rows, width), F32),
            pltpu.VMEM((groups, padded, width), F32),
            pltpu.VMEM((groups, padded, width), F32),
            pltpu.VMEM((HEADS, rows), F32),
        ],
        compiler_params=pltpu.CompilerParams(vmem_limit_bytes=60 * MIB),
        cost_estimate=pl.CostEstimate(
            flops=36 * pairs * width,
            bytes_accessed=2 * groups * padded * wide * 2,
            transcendentals=HEADS * pairs,
        ),
        name="attention_backward",
    )(valid, own, *others, attended, attended_grad, lse, lse_extra)


def mlp_kernel(
    units, unit, block, first_ref, bias_ref, rows_ref, n_own, n_other, dm_own, dm_other,
    out_own, out_other, dn_own, dn_other, gup_ref, gdown_ref, gbias_ref,
    out_acc, dn_acc, up_all, down_all, n_ref, dm_ref, sems,
):
    step = pl.program_id(0)

    @pl.when(step == 0)
    def _():
        copies = []
        for index in range(units):
            start = pl.multiple_of(first_ref[index], 16)
            for which, joined in enumerate((up_all, down_all)):
                copy = pltpu.make_async_copy(
                    rows_ref.at[pl.ds(start + which * unit, unit)],
                    joined.at[pl.ds(index * unit, unit)],
                    sems.at[2 * index + which],
                )
                copy.start()
                copies.append(copy)
        half = out_own.shape[0]
        for index, (source, joined, at) in enumerate(
            ((n_own, n_ref, 0), (n_other, n_ref, half), (dm_own, dm_ref, 0), (dm_other, dm_ref, half))
        ):
            copy = pltpu.make_async_copy(
                source, joined.at[pl.ds(at, half)], sems.at[2 * units + index]
            )
            copy.start()
            copies.append(copy)
        out_acc[...] = jnp.zeros_like(out_acc)
        dn_acc[...] = jnp.zeros_like(dn_acc)
        for copy in copies:
            copy.wait()

    span = pl.ds(pl.multiple_of(step * block, block), block)
    normed, dm, up, down = n_ref[...], dm_ref[...], up_all[span, :], down_all[span, :]
    hidden = dot_nt(normed, up) + bias_ref[...]
    below = 0.5 * (1.0 + lax.erf(hidden * (2.0**-0.5)))
    activated = (hidden * below).astype(BF)
    out_acc[...] += dot_nn(activated, down)
    gdown_ref[...] = dot_tn(activated, dm).astype(BF)
    slope = below + hidden * (jnp.exp(-0.5 * hidden * hidden) * (1.0 / math.sqrt(2 * math.pi)))
    hidden_grad = (dot_nt(dm, down) * slope).astype(BF)
    dn_acc[...] += dot_nn(hidden_grad, up)
    gup_ref[...] = dot_tn(hidden_grad, normed).astype(BF)
    gbias_ref[...] = jnp.sum(hidden_grad.astype(F32), axis=0, keepdims=True)
    half = out_own.shape[0]

    @pl.when(step == pl.num_programs(0) - 1)
    def _():
        out_own[...] = out_acc[:half, :]
        out_other[...] = out_acc[half:, :].astype(BF)
        dn_own[...] = dn_acc[:half, :]
        dn_other[...] = dn_acc[half:, :].astype(BF)


def mlp(normed, dm, bias, gathered, first_rows, block=384):
    half, width = normed[0].shape
    hidden = bias.shape[1]
    rows = 2 * half
    units = first_rows.shape[0]
    unit = hidden // units
    if unit % 16:
        wide = -(-unit // 16) * 16
        fill = ((0, 0), (0, wide - unit), (0, 0))
        gathered = jnp.pad(gathered.reshape(2 * units, unit, width), fill).reshape(-1, width)
        bias = jnp.pad(bias.reshape(units, unit), fill[:2]).reshape(1, -1)
        *outs, grad_up, grad_down, grad_bias = mlp(
            normed, dm, bias, gathered, first_rows // unit * wide, block
        )
        grads = [
            grad.reshape(units, wide, width)[:, :unit].reshape(hidden, width)
            for grad in (grad_up, grad_down)
        ]
        return *outs, *grads, grad_bias.reshape(units, wide)[:, :unit].reshape(1, hidden)
    whole = lambda step: (0, 0)
    part = lambda step: (step, 0)
    return pl.pallas_call(
        functools.partial(mlp_kernel, units, unit, block),
        grid=(hidden // block,),
        out_shape=[shape_of((half, width), dtype) for dtype in (F32, BF, F32, BF)]
        + [shape_of((hidden, width), BF)] * 2
        + [shape_of((1, hidden), F32)],
        in_specs=[
            pl.BlockSpec(memory_space=pltpu.SMEM),
            pl.BlockSpec((1, block), lambda step: (0, step)),
        ]
        + [pl.BlockSpec(memory_space=pl.ANY)] * 5,
        out_specs=[pl.BlockSpec((half, width), whole)] * 4
        + [pl.BlockSpec((block, width), part)] * 2
        + [pl.BlockSpec((1, block), lambda step: (0, step))],
        scratch_shapes=[pltpu.VMEM((rows, width), F32)] * 2
        + [pltpu.VMEM((hidden, width), BF)] * 2
        + [pltpu.VMEM((rows, width), BF)] * 2
        + [pltpu.SemaphoreType.DMA((2 * units + 4,))],
        compiler_params=pltpu.CompilerParams(vmem_limit_bytes=62 * MIB),
        cost_estimate=pl.CostEstimate(
            flops=12 * rows * width * hidden,
            bytes_accessed=8 * hidden * width + 16 * rows * width,
            transcendentals=2 * rows * hidden,
        ),
        name="mlp",
    )(first_rows.astype(jnp.int32), bias, gathered, *normed, *dm)


def column_blocks(width):
    return [(at, min(256, width - at)) for at in range(0, width, 256)]


def packed_rows(width, units):
    rows = sum((at + w) * w // 256 for at, w in column_blocks(width))
    return -(-rows // (16 * units)) * (16 * units)


def gram_into(slab, slab_t, out_ref):
    row = 0
    for at, w in column_blocks(slab.shape[1]):
        high = at + w
        value = dot_nn(slab_t[0:high, :], slab[:, at:high]).astype(BF)
        if w == 256:
            out_ref[row : row + high, :] = value
            row += high
        else:
            half = high // 2
            out_ref[row : row + half, 0:128] = value[:half]
            out_ref[row : row + half, 128:256] = value[half:]
            row += half
    out_ref[row:, :] = jnp.zeros((out_ref.shape[0] - row, 256), BF)


def unpack(packed, width, store):
    row = 0
    for at, w in column_blocks(width):
        high = at + w
        if w == 256:
            value = packed[row : row + high, :]
            row += high
        else:
            half = high // 2
            value = jnp.concatenate(
                [packed[row : row + half, 0:128], packed[row : row + half, 128:256]], axis=0
            )
            row += half
        store(at, w, value.astype(F32))


def store_both(ref, at, w, value):
    ref[0 : at + w, at : at + w] = value.astype(BF)
    if at:
        ref[at : at + w, 0:at] = value[0:at].T.astype(BF)


def on_diagonal(at, w):
    rows = lax.broadcasted_iota(jnp.int32, (at + w, w), 0)
    return rows == lax.broadcasted_iota(jnp.int32, (at + w, w), 1) + at


def symmetric_product(former, latter, width, done):
    for at, w in column_blocks(width):
        done(at, w, dot_nn(former[0 : at + w, :], latter[:, at : at + w]))


def deal(packed, offset_ref, kept, sent, sems):
    copies = []
    count, unit = kept.shape[0], kept.shape[1]
    for index in range(2 * count):
        start = pl.multiple_of(offset_ref[index], 16)
        out = kept if index < count else sent
        copy = pltpu.make_async_copy(
            packed.at[pl.ds(start, unit)], out.at[index % count], sems.at[index]
        )
        copy.start()
        copies.append(copy)
    for copy in copies:
        copy.wait()


def collect(pairs, offset_ref, packed, sems):
    copies = []
    unit = pairs[0].shape[1]
    for index, pair in enumerate(pairs):
        for side in (0, 1):
            at = side * len(pairs) + index
            start = pl.multiple_of(offset_ref[at], 16)
            copy = pltpu.make_async_copy(pair.at[side], packed.at[pl.ds(start, unit)], sems.at[at])
            copy.start()
            copies.append(copy)
    for copy in copies:
        copy.wait()


def gram_kernel(offset_ref, slab_ref, kept, sent, slab_t, packed, sems):
    slab_t[...] = slab_ref[...].T
    gram_into(slab_ref, slab_t, packed)
    deal(packed, offset_ref, kept, sent, sems)


SMEM = pl.BlockSpec(memory_space=pltpu.SMEM)
ANYWHERE = pl.BlockSpec(memory_space=pl.ANY)


def gram(slab, offsets):
    rows, width = slab.shape
    units = offsets.shape[0]
    size = packed_rows(width, units)
    part = shape_of((units // 2, size // units, 256), BF)
    return pl.pallas_call(
        gram_kernel,
        out_shape=[part, part],
        in_specs=[SMEM] + in_vmem(1),
        out_specs=[ANYWHERE] * 2,
        scratch_shapes=[
            pltpu.VMEM((width, rows), BF),
            pltpu.VMEM((size, 256), BF),
            pltpu.SemaphoreType.DMA((units,)),
        ],
        compiler_params=pltpu.CompilerParams(vmem_limit_bytes=50 * MIB),
        cost_estimate=pl.CostEstimate(
            flops=2 * rows * width * width,
            bytes_accessed=2 * rows * width + 2 * width * width,
            transcendentals=0,
        ),
        name="gram",
    )(offsets, slab)


def first_steps_kernel(count, offset_ref, slab_ref, *refs):
    pairs, refs = refs[:count], refs[count:]
    slab_out, kept, sent = refs[:3]
    gram_f, mix_f, prod_f, poly_f, gram_b, mix_b, prod_b, poly_b, slab_t, packed, sems = refs[3:]
    width = slab_ref.shape[1]
    collect(pairs, offset_ref, packed, sems)
    square = [jnp.zeros((1, 1), F32)]

    def add_diagonal(at, w, value):
        here = jnp.where(on_diagonal(at, w), value, 0.0)
        square[0] = square[0] + jnp.sum(here, keepdims=True).reshape(1, 1)

    unpack(packed, width, add_diagonal)
    inverse = 1.0 / (jnp.sqrt(square[0]) + 1e-07)

    def start(at, w, value):
        value = value * inverse * inverse
        gram_f[0 : at + w, at : at + w] = value
        store_both(gram_b, at, w, value)

    unpack(packed, width, start)
    lead = 1.0
    for step in range(FIRST_STEPS):
        def make_mix(at, w, value):
            span = (slice(0, at + w), slice(at, at + w))
            mix = poly_second * gram_f[span] + poly_third * value
            mix_f[span] = mix
            store_both(mix_b, at, w, mix)
            if step == 0:
                poly_f[span] = mix
                store_both(poly_b, at, w, mix)

        symmetric_product(gram_b, gram_b, width, make_mix)
        if step > 0:

            def join(at, w, value):
                span = (slice(0, at + w), slice(at, at + w))
                poly = poly_first * poly_f[span] + lead * mix_f[span] + value
                poly_f[span] = poly
                store_both(prod_b, at, w, poly)

            symmetric_product(mix_b, poly_b, width, join)
            poly_b, prod_b = prod_b, poly_b
        lead = lead * poly_first
        if step < FIRST_STEPS - 1:

            def keep(at, w, value):
                prod_f[0 : at + w, at : at + w] = value
                store_both(prod_b, at, w, value)

            symmetric_product(gram_b, mix_b, width, keep)

            def next_gram(at, w, value):
                span = (slice(0, at + w), slice(at, at + w))
                new = poly_first**2 * gram_f[span] + 2 * poly_first * prod_f[span] + value
                gram_f[span] = new
                store_both(gram_b, at, w, new)

            symmetric_product(prod_b, mix_b, width, next_gram)
    slab = slab_ref[...]
    moved = ((lead * slab.astype(F32) + dot_nn(slab, poly_b[...])) * inverse).astype(BF)
    slab_out[...] = moved
    slab_t[...] = moved.T
    gram_into(moved, slab_t, packed)
    deal(packed, offset_ref, kept, sent, sems)


def first_steps(pairs, slab, offsets):
    rows, width = slab.shape
    square = (width, width)
    units = offsets.shape[0]
    size = packed_rows(width, units)
    part = shape_of((units // 2, size // units, 256), BF)
    return pl.pallas_call(
        functools.partial(first_steps_kernel, len(pairs)),
        out_shape=[shape_of((rows, width), BF), part, part],
        in_specs=[SMEM] + in_vmem(1) + [ANYWHERE] * len(pairs),
        out_specs=in_vmem(1) + [ANYWHERE] * 2,
        scratch_shapes=[pltpu.VMEM(square, F32)] * 4
        + [pltpu.VMEM(square, BF)] * 4
        + [pltpu.VMEM((width, rows), BF), pltpu.VMEM((size, 256), BF)]
        + [pltpu.SemaphoreType.DMA((units,))],
        compiler_params=pltpu.CompilerParams(vmem_limit_bytes=60 * MIB),
        cost_estimate=pl.CostEstimate(
            flops=18 * width**3,
            bytes_accessed=4 * rows * width + 4 * width * width,
            transcendentals=0,
        ),
        name="first_steps",
    )(offsets, slab, *pairs)


def last_steps_kernel(count, offset_ref, slab_ref, *refs):
    pairs, refs = refs[:count], refs[count:]
    slab_out, gram_b, poly_b, prod_b, join_b, packed, sems = refs
    width = slab_ref.shape[1]
    collect(pairs, offset_ref, packed, sems)
    unpack(packed, width, lambda at, w, value: store_both(gram_b, at, w, value))
    for step in range(LAST_STEPS):

        def make_poly(at, w, value):
            held = gram_b[0 : at + w, at : at + w].astype(F32)
            poly = poly_second * held + poly_third * value
            poly = poly + jnp.where(on_diagonal(at, w), poly_first, 0.0)
            store_both(poly_b, at, w, poly)
            if step == 0:
                store_both(join_b, at, w, poly)

        symmetric_product(gram_b, gram_b, width, make_poly)
        if step > 0:
            symmetric_product(
                poly_b, join_b, width, lambda at, w, value: store_both(prod_b, at, w, value)
            )
            join_b, prod_b = prod_b, join_b
        if step < LAST_STEPS - 1:
            symmetric_product(
                gram_b, poly_b, width, lambda at, w, value: store_both(prod_b, at, w, value)
            )
            symmetric_product(
                prod_b, poly_b, width, lambda at, w, value: store_both(gram_b, at, w, value)
            )
    slab_out[...] = dot_nn(slab_ref[...], join_b[...]).astype(BF)


def last_steps(pairs, slab, offsets):
    rows, width = slab.shape
    units = offsets.shape[0]
    size = packed_rows(width, units)
    return pl.pallas_call(
        functools.partial(last_steps_kernel, len(pairs)),
        out_shape=shape_of((rows, width), BF),
        in_specs=[SMEM] + in_vmem(1) + [ANYWHERE] * len(pairs),
        out_specs=in_vmem(1)[0],
        scratch_shapes=[pltpu.VMEM((width, width), BF)] * 4
        + [pltpu.VMEM((size, 256), BF), pltpu.SemaphoreType.DMA((units,))],
        compiler_params=pltpu.CompilerParams(vmem_limit_bytes=60 * MIB),
        cost_estimate=pl.CostEstimate(
            flops=10 * width**3,
            bytes_accessed=4 * rows * width + 2 * width * width,
            transcendentals=0,
        ),
        name="last_steps",
    )(offsets, slab, *pairs)


def line_up_kernel(counts, place_ref, *refs):
    line, qkv, proj, small_at = counts
    blocks, (former, latter, held, joined) = refs[:line], refs[line:]
    for step, block in enumerate(blocks):
        held[step] = block[...]
    total = None
    for index in range(line):
        step = lax.rem(place_ref[0] - index + line, line)
        value = held[step].astype(F32)
        joined[index * qkv : (index + 1) * qkv, :] = value[:qkv]
        at = line * qkv + index * proj
        joined[at : at + proj, :] = value[qkv : qkv + proj]
        small = value[small_at:]
        total = small if total is None else total + small
    half = former.shape[0]
    rest = line * (qkv + proj) - half
    former[...] = joined[:half, :].astype(BF)
    latter[:rest, :] = joined[half:, :].astype(BF)
    latter[rest:, :] = total.astype(BF)


def line_up(blocks, place, qkv, proj):
    line = len(blocks)
    rows, width = blocks[0].shape
    small_at = -(-(qkv + proj) // 16) * 16
    half = line * (qkv + proj) // 2
    return pl.pallas_call(
        functools.partial(line_up_kernel, (line, qkv, proj, small_at)),
        out_shape=[
            shape_of((half, width), BF),
            shape_of((line * (qkv + proj) - half + rows - small_at, width), BF),
        ],
        in_specs=[SMEM] + in_vmem(line),
        out_specs=in_vmem(2),
        scratch_shapes=[
            pltpu.VMEM((line, rows, width), BF),
            pltpu.VMEM((line * (qkv + proj), width), F32),
        ],
        compiler_params=pltpu.CompilerParams(vmem_limit_bytes=40 * MIB),
        name="line_up",
    )(place.reshape(1), *blocks)


def packed_grad_kernel(offset_ref, query_ref, own_ref, arrived_ref, other_ref, packed, kept, sent, grad, sems):
    width = query_ref.shape[1]
    packed[:, :width] = query_ref[...]
    total = own_ref[...].astype(F32) + arrived_ref[...].astype(F32)
    packed[:, width:] = total.astype(BF)
    qkv_grad_kernel(offset_ref, packed, other_ref, kept, sent, grad, sems)


def packed_grad_of(query_grad, own, arrived, other_side, offsets):
    rows, width = query_grad.shape
    long = 3 * width
    units = offsets.shape[0]
    unit = long // units
    if unit % 16:
        total = (own.astype(F32) + arrived.astype(F32)).astype(BF)
        packed = jnp.concatenate([query_grad, total], axis=1)
        return packed, *qkv_grad(packed, other_side, offsets)
    part = shape_of((units // 2, unit, width), BF)
    return pl.pallas_call(
        packed_grad_kernel,
        out_shape=[shape_of((rows, long), BF), part, part],
        in_specs=[SMEM] + in_vmem(4),
        out_specs=in_vmem(1) + [ANYWHERE] * 2,
        scratch_shapes=[pltpu.VMEM((long, width), BF), pltpu.SemaphoreType.DMA((units,))],
        compiler_params=pltpu.CompilerParams(vmem_limit_bytes=50 * MIB),
        cost_estimate=pl.CostEstimate(
            flops=2 * rows * long * width,
            bytes_accessed=2 * rows * (2 * long + width) + 2 * long * width,
            transcendentals=0,
        ),
        name="packed_grad",
    )(offsets, query_grad, own, arrived, other_side)


def first_norm_kernel(packed_ref, weight_ref, standard_ref, inverse_ref, after_ref, gain_ref, low_ref, sums_ref):
    grad = dot_nn(packed_ref[...], weight_ref[...])
    standard = standard_ref[...]
    sums_ref[...] = jnp.zeros_like(sums_ref)
    sums_ref[0:1, :] = jnp.sum(grad * standard, axis=0, keepdims=True)
    sums_ref[1:2, :] = jnp.sum(grad, axis=0, keepdims=True)
    scaled = grad * gain_ref[...]
    average = jnp.mean(scaled, axis=1, keepdims=True)
    along = jnp.mean(scaled * standard, axis=1, keepdims=True)
    token = after_ref[...] + inverse_ref[...] * (scaled - average - standard * along)
    low_ref[...] = token.astype(BF)
    rows = token.shape[0] - 16
    sums_ref[8:16, :] = token[rows : rows + 8, :]


def first_norm_back(packed_grad, weight, standard, inverse, after, gain):
    rows, width = standard.shape
    long = weight.shape[0]
    low, sums = pl.pallas_call(
        first_norm_kernel,
        out_shape=[shape_of((rows, width), BF), shape_of((16, width), F32)],
        in_specs=in_vmem(6),
        out_specs=in_vmem(2),
        compiler_params=pltpu.CompilerParams(vmem_limit_bytes=60 * MIB),
        cost_estimate=pl.CostEstimate(
            flops=2 * rows * long * width,
            bytes_accessed=2 * rows * (long + 5 * width) + 2 * long * width,
            transcendentals=0,
        ),
        name="first_norm_back",
    )(packed_grad, weight, standard, inverse, after, gain)
    return low, sums[0:2], sums[8:9]


def qkv_grad_kernel(offset_ref, long_ref, other_ref, kept, sent, grad, sems):
    other = other_ref[...]
    for at, w in [(at, 384) for at in range(0, grad.shape[0], 384)]:
        grad[at : at + w, :] = dot_tn(long_ref[:, at : at + w], other).astype(BF)
    deal(grad, offset_ref, kept, sent, sems)


def qkv_grad(long_side, other_side, offsets):
    rows, long = long_side.shape
    width = other_side.shape[1]
    units = offsets.shape[0]
    unit = long // units
    if unit % 16:
        grad = dot_tn(long_side, other_side).astype(BF).reshape(units, unit, width)
        parts = [
            lax.dynamic_index_in_dim(grad, offsets[index] // unit, 0, False)
            for index in range(units)
        ]
        return jnp.stack(parts[: units // 2]), jnp.stack(parts[units // 2 :])
    part = shape_of((units // 2, unit, width), BF)
    return pl.pallas_call(
        qkv_grad_kernel,
        out_shape=[part, part],
        in_specs=[SMEM] + in_vmem(2),
        out_specs=[ANYWHERE] * 2,
        scratch_shapes=[pltpu.VMEM((long, width), BF), pltpu.SemaphoreType.DMA((units,))],
        compiler_params=pltpu.CompilerParams(vmem_limit_bytes=50 * MIB),
        cost_estimate=pl.CostEstimate(
            flops=2 * rows * long * width,
            bytes_accessed=2 * rows * (long + width) + 2 * long * width,
            transcendentals=0,
        ),
        name="qkv_grad",
    )(offsets, long_side, other_side)


def place_kernel(moves, count, outputs, offset_ref, *refs):
    pieces, outs, sems = refs[:count], refs[count : count + outputs], refs[count + outputs]
    copies = []
    for index, (piece, at, rows, out, _) in enumerate(moves):
        start = pl.multiple_of(offset_ref[index], 16)
        copy = pltpu.make_async_copy(
            pieces[piece].at[pl.ds(at, rows)], outs[out].at[pl.ds(start, rows)], sems.at[index]
        )
        copy.start()
        copies.append(copy)
    for copy in copies:
        copy.wait()


def place(pieces, moves, sizes):
    width = pieces[0].shape[1]
    if any(at % 16 or rows % 16 for _, at, rows, _, _ in moves):
        outs = [jnp.zeros((size, width), BF) for size in sizes]
        for piece, at, rows, out, offset in moves:
            part = pieces[piece][at : at + rows]
            outs[out] = lax.dynamic_update_slice_in_dim(outs[out], part, offset, 0)
        return outs
    offsets = jnp.stack([move[4] for move in moves]).astype(jnp.int32)
    static = [move[:4] + (None,) for move in moves]
    return pl.pallas_call(
        functools.partial(place_kernel, static, len(pieces), len(sizes)),
        out_shape=[shape_of((size, width), BF) for size in sizes],
        in_specs=[pl.BlockSpec(memory_space=pltpu.SMEM)]
        + [pl.BlockSpec(memory_space=pl.ANY)] * len(pieces),
        out_specs=in_vmem(len(sizes)),
        scratch_shapes=[pltpu.SemaphoreType.DMA((len(moves),))],
        compiler_params=pltpu.CompilerParams(vmem_limit_bytes=40 * MIB),
        cost_estimate=pl.CostEstimate(
            flops=0, bytes_accessed=4 * sum(sizes) * width, transcendentals=0
        ),
        name="place",
    )(offsets, *pieces)


def together_kernel(*refs):
    pass


def together(*arrays, cost=0):
    anywhere = pl.BlockSpec(memory_space=pl.ANY)
    return pl.pallas_call(
        together_kernel,
        out_shape=[shape_of(array.shape, array.dtype) for array in arrays],
        in_specs=[anywhere] * len(arrays),
        out_specs=[anywhere] * len(arrays),
        input_output_aliases={index: index for index in range(len(arrays))},
        cost_estimate=pl.CostEstimate(flops=cost, bytes_accessed=0, transcendentals=0),
        name="together",
    )(*arrays)


def beside(*arrays):
    got = together(*arrays, cost=10**11)
    return got if len(arrays) > 1 else got[0]


def shift(values, step, seq_count):
    return lax.ppermute(
        values, "seq", [(rank, (rank + step) % seq_count) for rank in range(seq_count)]
    )


def swap(values, bit, batch_count):
    return lax.ppermute(values, "batch", [(rank, rank ^ bit) for rank in range(batch_count)])


def line_gather(values, seq_count):
    return [values] + [shift(values, step, seq_count) for step in range(1, seq_count)]


def line_reduce(blocks, seq_count):
    total = blocks[0].astype(F32)
    for step in range(1, seq_count):
        total = total + shift(blocks[step], -step, seq_count).astype(F32)
    return total


def from_own(values, seq_count):
    rank = lax.axis_index("seq")
    blocks = values.reshape(seq_count, -1, values.shape[1])
    return [
        lax.dynamic_index_in_dim(blocks, (rank - step) % seq_count, 0, False)
        for step in range(seq_count)
    ]


def in_line(blocks, seq_count):
    stacked = jnp.stack(blocks)
    rank = lax.axis_index("seq")
    order = (rank - jnp.arange(seq_count, dtype=jnp.int32)) % seq_count
    return jnp.take(stacked, order, axis=0)


def plane_gather(block, bits, batch_count):
    blocks = {0: block}
    for bit in bits:
        for mask in list(blocks):
            blocks[mask ^ bit] = swap(blocks[mask], bit, batch_count)
    return blocks


def plane_reduce(blocks, bits, batch_count):
    blocks = dict(blocks)
    for bit in bits:
        kept = [mask for mask in blocks if not mask & bit]
        rows = blocks[0].shape[0]
        arrived = swap(jnp.concatenate([blocks[mask ^ bit] for mask in kept], axis=0), bit, batch_count)
        blocks = {
            mask: (
                blocks[mask].astype(F32) + arrived[index * rows : (index + 1) * rows].astype(F32)
            ).astype(BF)
            for index, mask in enumerate(kept)
        }
    return blocks[0]


def gather_small(values, batch_count, seq_count):
    return gather_batch(in_line(line_gather(values, seq_count), seq_count), batch_count)


def gather_batch(values, batch_count):
    joined = values[None]
    bit = 1
    while bit < batch_count:
        joined = jnp.concatenate([joined, swap(joined, bit, batch_count)], axis=0)
        bit *= 2
    order = lax.axis_index("batch") ^ jnp.arange(batch_count, dtype=jnp.int32)
    return jnp.take(joined, order, axis=0)


def standardize(values):
    average = jnp.mean(values, axis=-1, keepdims=True)
    centred = values - average
    variance = jnp.mean(centred * centred, axis=-1, keepdims=True)
    inverse = lax.rsqrt(variance + norm_eps)
    return centred * inverse, inverse


def standardize_back(grad, standard, inverse):
    average = jnp.mean(grad, axis=-1, keepdims=True)
    along = jnp.mean(grad * standard, axis=-1, keepdims=True)
    return inverse * (grad - average - standard * along)


def time_token(step_values, model_width):
    half_width = model_width // 2
    frequency = jnp.exp(-math.log(10000.0) * jnp.arange(half_width, dtype=F32) / half_width)
    angles = step_values.astype(F32)[:, None] * frequency[None, :]
    return jnp.concatenate([jnp.cos(angles), jnp.sin(angles)], axis=-1)


def adam_step(parameter, first_state, second, gradient):
    first_new = beta_one * first_state + (1.0 - beta_one) * gradient
    second_new = beta_two * second + (1.0 - beta_two) * gradient * gradient
    first_hat = first_new / (1.0 - beta_one**STEP)
    second_hat = second_new / (1.0 - beta_two**STEP)
    return (
        first_new,
        second_new,
        parameter - adam_rate * first_hat / (jnp.sqrt(second_hat) + adam_eps),
    )


def body(
    patches, timesteps, labels, next_grad, skip_grad, next_extra, skip_extra,
    w_qkv, w_proj, w_up, w_down, mom_qkv, mom_proj, mom_up, mom_down,
    vectors, vec_first, vec_second, table, table_first, table_second,
):
    images, patch_rows, width = patches.shape
    batch_count = lax.axis_size("batch")
    seq_count = lax.axis_size("seq")
    shards = batch_count * seq_count
    batch_rank = lax.axis_index("batch")
    seq_rank = lax.axis_index("seq")
    shard_rank = batch_rank * seq_count + seq_rank
    core = batch_rank % 2
    chips = seq_count // (2 * images)
    own_image = seq_rank // chips
    own_core, own_slot = own_image // images, own_image % images
    sub_rank = seq_rank % chips
    bits = [1 << level for level in range(1, (batch_count - 1).bit_length())]
    up_bits, down_bits = bits, bits[::-1]

    def route(matching):
        pairs = []
        for rank in range(batch_count):
            for place_z in range(seq_count):
                code = place_z ^ matching
                slot, rest = code // (2 * chips), code % (2 * chips)
                to_core, sub = rest // chips, rest % chips
                to_z = ((rank % 2) * images + slot) * chips + sub
                pairs.append((rank * seq_count + place_z, (rank - rank % 2 + to_core) * seq_count + to_z))
        return pairs

    piece_rows = images * patch_rows // seq_count

    def send(values):
        pieces = values.reshape(seq_count, piece_rows, width)
        return [
            lax.ppermute(
                lax.dynamic_index_in_dim(pieces, seq_rank ^ matching, 0, False),
                ("batch", "seq"),
                route(matching),
            )
            for matching in range(seq_count)
        ]

    def send_back(values):
        pieces = jnp.stack([array.reshape(seq_count, piece_rows, width) for array in values], axis=1)
        return [
            lax.ppermute(
                pieces[matching], ("batch", "seq"), [(to, at) for at, to in route(matching)]
            )
            for matching in range(seq_count)
        ]

    def join_back(moved, index):
        moved = jnp.stack([piece[index] for piece in moved])
        pieces = [
            lax.dynamic_index_in_dim(moved, seq_rank ^ code, 0, True) for code in range(seq_count)
        ]
        return jnp.concatenate(pieces, axis=0).reshape(images, patch_rows, width)

    rows = seq_count * piece_rows
    padded = rows + 16

    low_qkv = w_qkv.astype(BF).T
    low_proj = w_proj.astype(BF).T
    unit_width, qkv_width, proj_width = w_up.shape[1], low_qkv.shape[0], low_proj.shape[0]
    column_count = table.shape[1]
    class_count = table.shape[0]
    masks = [level << 1 for level in range(batch_count // 2)]
    offsets = batch_rank ^ jnp.array(masks + [mask ^ 1 for mask in masks], jnp.int32)

    own_mlp = jnp.concatenate([w_up.astype(BF).T, w_down.astype(BF)], axis=0)

    facts = lax.all_gather(jnp.stack([timesteps, labels]), "batch", axis=0)
    all_labels = facts[:, 1].reshape(-1)
    selector = (
        all_labels[:, None] == jnp.arange(class_count, dtype=jnp.int32)[None, :]
    ).astype(BF)
    class_part = dot_nn(selector, table.astype(BF)).astype(BF)
    small = jnp.concatenate([vectors.astype(BF), class_part], axis=0)
    small_rows = -(-small.shape[0] // 16) * 16
    small = lax.dynamic_update_slice(
        jnp.zeros((small_rows, width), BF), small, (0, shard_rank * column_count)
    )

    gap = -(qkv_width + proj_width) % 16
    load = [low_qkv, low_proj] + ([jnp.zeros((gap, width), BF)] if gap else []) + [small]
    line = line_gather(jnp.concatenate(load, axis=0), seq_count)
    former, latter = line_up(line, seq_rank, qkv_width, proj_width)
    former, latter, patches, own_mlp = together(former, latter, patches, own_mlp)

    same_core = [
        [rank * seq_count + at for rank in range(side, batch_count, 2) for at in range(seq_count)]
        for side in (0, 1)
    ]
    all_mlp = lax.all_gather(
        own_mlp, ("batch", "seq"), axis=0, tiled=True, axis_index_groups=same_core
    )
    qkv_rows, proj_rows = qkv_width * seq_count, proj_width * seq_count

    def spread_start(former, latter):
        return (
            {mask: swap(former, mask, batch_count) for mask in bits},
            {mask: swap(latter, mask, batch_count) for mask in bits},
        )

    def spread_rest(former, latter, arrived):
        former_got, latter_got = dict(arrived[0]), dict(arrived[1])
        former_got[0], latter_got[0] = former, latter
        for got, order in ((former_got, bits), (latter_got, bits[::-1])):
            for index, bit in enumerate(order):
                lower = order[:index]
                for mask in [m for m in list(got) if m and not m & bit]:
                    if all(not (mask & other) or other in lower for other in bits):
                        if (mask ^ bit) not in got:
                            got[mask ^ bit] = swap(got[mask], bit, batch_count)
        return former_got, latter_got

    def flat(groups):
        return [group[mask] for group in groups for mask in sorted(group)]

    def unflat(arrays, groups):
        arrays = list(arrays)
        return [{mask: arrays.pop(0) for mask in sorted(group)} for group in groups]

    arrived = spread_start(former, latter)
    moved_patches = send(patches)
    gathered = spread_rest(former, latter, arrived)
    grad_in = (next_grad.astype(F32) + skip_grad.astype(F32)).astype(BF)
    grad_in, *got = together(grad_in, *flat(gathered), *moved_patches)
    moved_grad = send(grad_in)
    moved_patches = jnp.concatenate(got[len(got) - seq_count :], axis=0)
    gathered = unflat(got[: len(got) - seq_count], gathered)
    pieces, moves, small = [], [], 0.0
    unit = former.shape[0]
    rest = qkv_rows - unit
    for group, blocks in enumerate(gathered):
        for mask in masks:
            for side in (0, 1):
                block = swap(blocks[mask], 1, batch_count) if side else blocks[mask]
                target = batch_rank ^ mask ^ side
                number = len(pieces)
                pieces.append(block)
                if group == 0:
                    moves.append((number, 0, unit, 0, target * qkv_rows))
                else:
                    moves.append((number, 0, rest, 0, target * qkv_rows + unit))
                    moves.append((number, rest, proj_rows, 1, target * proj_rows))
                    small = small + block[rest + proj_rows :].astype(F32)
    full_qkv, full_proj = place(pieces, moves, [qkv_rows * batch_count, proj_rows * batch_count])
    vec_values, class_rows = small[:10], small[10 : 10 + images * batch_count]
    home = batch_rank - core + own_core
    own_time = lax.dynamic_index_in_dim(facts[:, 0].reshape(-1), home * images + own_slot, 0, True)
    time_row = time_token(own_time, width)
    class_row = lax.dynamic_index_in_dim(class_rows, home * images + own_slot, 0, True)
    has_extra = sub_rank == 0
    extra_row = jnp.where(core == 0, time_row, class_row) * has_extra.astype(F32)
    row_index = lax.broadcasted_iota(jnp.int32, (padded, 1), 0)
    row_valid = (row_index < rows + has_extra.astype(jnp.int32)).astype(F32)
    first_row = lax.broadcasted_iota(jnp.int32, (16, 1), 0) == 0

    extra_tile = jnp.where(first_row, extra_row, 0.0)
    tokens = jnp.concatenate([moved_patches.astype(F32), extra_tile], axis=0)
    standard_one, inverse_one = standardize(tokens)
    normed = ((standard_one * vec_values[0] + vec_values[1]) * row_valid).astype(BF)
    packed = dot_nt(normed, full_qkv).astype(BF)

    def rotate(values, step, core_bit, back):
        pairs = []
        for rank in range(batch_count):
            for place_z in range(seq_count):
                base, sub = place_z - place_z % chips, place_z % chips
                source = (rank ^ core_bit) * seq_count + base + (sub + step) % chips
                here = rank * seq_count + place_z
                pairs.append((here, source) if back else (source, here))
        return lax.ppermute(values, ("batch", "seq"), pairs)

    peers = [(step, bit) for step in range(chips) for bit in (0, 1)][1:]
    sooner = seq_count // 2
    packed, *moved_grad[:sooner] = together(packed, *moved_grad[:sooner])
    own_kv = packed[:, width:]
    other_kv = [rotate(own_kv, step, bit, False) for step, bit in peers]
    valid = jnp.stack(
        [has_extra.astype(jnp.int32)]
        + [((sub_rank + step) % chips == 0).astype(jnp.int32) for step, bit in peers]
    )
    in_extra = (next_extra.astype(F32) + skip_extra.astype(F32)).astype(BF)
    in_extra_other = swap(in_extra, 1, batch_count)
    attended, lse, lse_extra = attention_forward(valid, packed, other_kv)
    attended, in_extra_other, *moved_grad = together(attended, in_extra_other, *moved_grad)
    in_extra = jnp.where(own_core == core, in_extra, in_extra_other)
    in_extra = lax.dynamic_index_in_dim(in_extra, own_slot, 0, False)
    in_extra = lax.dynamic_index_in_dim(in_extra, core, 0, True)
    in_extra = jnp.where(first_row & has_extra, in_extra, jnp.zeros_like(in_extra))
    incoming_low = jnp.concatenate([*moved_grad, in_extra], axis=0)
    incoming = incoming_low.astype(F32)
    other_incoming = swap(incoming_low, 1, batch_count)
    line_order = (seq_rank - jnp.arange(seq_count, dtype=jnp.int32)) % seq_count
    chip_order = (batch_rank ^ jnp.array(masks, jnp.int32)) >> 1
    first_rows = (chip_order[:, None] * seq_count + line_order[None, :]).reshape(-1) * (2 * unit_width)
    all_bias = vec_values[6:].reshape(batch_count // 2, 2, seq_count, unit_width)
    core_bias = lax.dynamic_index_in_dim(all_bias, core, 1, False)
    core_bias = jnp.take(jnp.take(core_bias, chip_order, axis=0), line_order, axis=1).reshape(1, -1)
    middle = tokens + (dot_nt(attended, full_proj) + vec_values[4]) * row_valid
    standard_two, inverse_two = standardize(middle)
    normed_two = ((standard_two * vec_values[2] + vec_values[3]) * row_valid).astype(BF)
    other_normed = swap(normed_two, 1, batch_count)
    out_own, out_other, dn_own, dn_other, grad_up, grad_down, grad_bias = mlp(
        (normed_two, other_normed), (incoming_low, other_incoming), core_bias, all_mlp, first_rows
    )

    def blocks_of(grad):
        parts = grad.reshape(len(masks), -1, width)
        return {mask: parts[index] for index, mask in enumerate(masks)}

    def sum_start(groups):
        moved = []
        for blocks, bit in zip(groups, (bits[-1], bits[0])):
            kept = [mask for mask in masks if not mask & bit]
            moved.append(swap(jnp.concatenate([blocks[mask ^ bit] for mask in kept], axis=0), bit, batch_count))
        return moved

    def sum_add(groups, moved):
        sums = []
        for blocks, arrived, bit in zip(groups, moved, (bits[-1], bits[0])):
            kept = [mask for mask in masks if not mask & bit]
            count = blocks[0].shape[0]
            sums.append(
                {
                    mask: (
                        blocks[mask].astype(F32)
                        + arrived[index * count : (index + 1) * count].astype(F32)
                    ).astype(BF)
                    for index, mask in enumerate(kept)
                }
            )
        return sums

    def sum_rest(groups):
        return [
            plane_reduce(blocks, order, batch_count)
            for blocks, order in zip(groups, (bits[::-1][1:], bits[1:]))
        ]

    def line_blocks(former, latter):
        joined = [values.reshape(seq_count, -1, width) for values in (former, latter)]
        return jnp.concatenate(joined, axis=1)

    mlp_groups = [blocks_of(grad_up), blocks_of(grad_down)]
    moved = sum_start(mlp_groups)
    normed_two_grad = dn_own + swap(dn_other, 1, batch_count).astype(F32)
    middle_grad = incoming + standardize_back(
        normed_two_grad * vec_values[2], standard_two, inverse_two
    )
    middle_low = middle_grad.astype(BF)

    attended_grad = dot_nn(middle_low, full_proj).astype(BF)
    out_arrived = swap(out_other, 1, batch_count)
    backward = attention_backward(valid, packed, other_kv, attended, attended_grad, lse, lse_extra)
    *backward, moved_up, moved_down, out_arrived, middle_low, attended, middle = together(
        *backward, *moved, out_arrived, middle_low, attended, middle
    )
    mlp_groups = sum_add(mlp_groups, [moved_up, moved_down])

    def halves(values):
        cut = values.shape[1] // 32 * 16
        cut = cut if cut else values.shape[1] // 2
        return [
            {mask: part[index] for index, mask in enumerate(masks)}
            for part in (values[:, :cut], values[:, cut:])
        ]

    def next_axis(groups, orders):
        moved = []
        for blocks, order in zip(groups, orders):
            kept = [mask for mask in blocks if not mask & order[0]]
            load = jnp.concatenate([blocks[mask ^ order[0]] for mask in kept], axis=0)
            moved.append(swap(load, order[0], batch_count))
        return moved

    def next_add(groups, orders, moved):
        sums = []
        for blocks, order, arrived in zip(groups, orders, moved):
            kept = [mask for mask in blocks if not mask & order[0]]
            count = blocks[0].shape[0]
            sums.append(
                plane_reduce(
                    {
                        mask: (
                            blocks[mask].astype(F32)
                            + arrived[index * count : (index + 1) * count].astype(F32)
                        ).astype(BF)
                        for index, mask in enumerate(kept)
                    },
                    order[1:],
                    batch_count,
                )
            )
        return sums

    orders = (bits[::-1][1:], bits[1:])
    mlp_moved = next_axis(mlp_groups, orders)
    query_grad, own_dkv = backward[0], backward[1]
    arrived = [rotate(term, step, bit, True) for (step, bit), term in zip(peers, backward[2:])]
    middle_low, attended = beside(middle_low, attended)
    proj_kept, proj_sent = qkv_grad(middle_low, attended, offsets * proj_rows)
    own_dkv, proj_kept, proj_sent, *arrived = together(own_dkv, proj_kept, proj_sent, *arrived)

    proj_arrived = swap(proj_sent, 1, batch_count)
    far_dkv = arrived[0]
    for term in arrived[1:]:
        far_dkv = (far_dkv.astype(F32) + term.astype(F32)).astype(BF)
    packed_grad, kept, sent = packed_grad_of(
        query_grad, own_dkv, far_dkv, normed, offsets * qkv_rows
    )
    packed_grad, kept, sent, proj_kept, proj_arrived, *mlp_moved = together(
        packed_grad, kept, sent, proj_kept, proj_arrived, *mlp_moved
    )

    arrived = swap(sent, 1, batch_count)
    proj_kept, proj_arrived, *mlp_moved = beside(proj_kept, proj_arrived, *mlp_moved)
    mlp_up, mlp_down = next_add(mlp_groups, orders, mlp_moved)
    joined = line_blocks(mlp_up, mlp_down)
    proj_groups = halves((proj_kept.astype(F32) + proj_arrived.astype(F32)).astype(BF))
    joined = [joined[step] for step in range(seq_count)]
    arrived, *joined = together(arrived, *joined)

    groups = halves((kept.astype(F32) + arrived.astype(F32)).astype(BF))
    moved = sum_start(groups)
    near_steps = (1, seq_count - 1)
    far_steps = tuple(range(2, seq_count - 1))
    near_line = [shift(joined[step], -step, seq_count) for step in near_steps]
    first_proj = sum_start(proj_groups)
    packed_grad = beside(packed_grad)
    token_low, norm_sums, extra_grad = first_norm_back(
        packed_grad, full_qkv, standard_one, inverse_one, middle_grad, vec_values[0:1]
    )
    far_line = [joined[step] for step in far_steps]
    moved_up, moved_down, token_low, norm_sums, extra_grad, *got = together(
        *moved, token_low, norm_sums, extra_grad, *near_line, *far_line, *first_proj
    )
    near_line, far_line, first_proj = got[:2], got[2:-2], got[-2:]
    far_line = [shift(part, -step, seq_count) for step, part in zip(far_steps, far_line)]
    bias_parts = jnp.take(grad_bias.reshape(len(masks), seq_count, -1), line_order, axis=1)
    bias_sum = jnp.zeros((batch_count // 2, seq_count, unit_width), F32)
    bias_sum = jnp.take(bias_parts, (batch_rank ^ jnp.arange(0, batch_count, 2)) >> 1, axis=0)
    bias_sum = jnp.where(
        jnp.arange(2, dtype=jnp.int32)[None, :, None, None] == core, bias_sum[:, None], 0.0
    )
    class_slots = jnp.arange(images * batch_count, dtype=jnp.int32) == home * images + own_slot
    holds_class = (core == 1) & has_extra
    class_grad = jnp.where((class_slots & holds_class)[:, None], extra_grad, 0.0)
    vec_grad = jnp.concatenate(
        [
            norm_sums,
            jnp.sum(normed_two_grad * standard_two, axis=0)[None],
            jnp.sum(normed_two_grad, axis=0)[None],
            jnp.sum(middle_low.astype(F32), axis=0)[None],
            jnp.sum(incoming_low.astype(F32), axis=0)[None],
            bias_sum.reshape(4, width),
            class_grad,
        ],
        axis=0,
    )
    sums = next_axis(sum_add(groups, [moved_up, moved_down]), orders)
    proj_groups = sum_add(proj_groups, first_proj)
    proj_up, proj_down = next_axis(proj_groups, orders)
    vec_far = swap(vec_grad, 1, batch_count)
    sums_up, sums_down, vec_far, proj_up, proj_down, *far_line = together(
        *sums, vec_far, proj_up, proj_down, *far_line
    )
    sums = next_add(sum_add(groups, [moved_up, moved_down]), orders, [sums_up, sums_down])
    proj_one, proj_two = next_add(proj_groups, orders, [proj_up, proj_down])
    vec_grad = vec_grad + vec_far

    qkv_parts = from_own(jnp.concatenate(sums, axis=0), seq_count)
    proj_parts = from_own(jnp.concatenate([proj_one, proj_two], axis=0), seq_count)
    late = [jnp.concatenate(parts, axis=0) for parts in zip(qkv_parts, proj_parts)]
    late = [late[0]] + [shift(late[step], -step, seq_count) for step in range(1, seq_count)]
    output = (middle + (out_own + out_arrived.astype(F32) + vec_values[5])).astype(BF)
    for bit in bits:
        vec_grad = vec_grad + swap(vec_grad, bit, batch_count)
    *late, vec_grad, output = together(*late, vec_grad, output)
    total_mlp = functools.reduce(
        jnp.add, [part.astype(F32) for part in (joined[0], *near_line, *far_line)]
    )
    share_up, share_down = total_mlp[:unit_width], total_mlp[unit_width:]

    turned = (mom_qkv.T, mom_proj.T, mom_up.T, mom_down)
    widest = unit_width
    spread = seq_count // 4
    home_plane = [spread * turn for turn in (1, 2, 3, 0)]
    plane_of = {plane: index for index, plane in enumerate(home_plane)}
    held = jnp.take(
        jnp.array([plane_of.get(plane - plane % spread) for plane in range(seq_count)], jnp.int32),
        (seq_rank + jnp.arange(seq_count, dtype=jnp.int32)) % seq_count,
    )

    late = functools.reduce(jnp.add, [part.astype(F32) for part in late])
    shares = (late[:qkv_width], late[qkv_width:], share_up, share_down)
    fresh = [muon_momentum * old + share for old, share in zip(turned, shares)]
    stacked = jnp.stack(
        [jnp.pad(new.astype(BF), ((0, widest - new.shape[0]), (0, 0))) for new in fresh]
    )
    small = lax.dynamic_slice_in_dim(vec_grad, batch_rank * (seq_count * column_count), seq_count * column_count, 1)
    small = jnp.transpose(small.reshape(-1, seq_count, column_count), (1, 0, 2)).reshape(seq_count, -1)
    small = jnp.pad(small, ((0, 0), (0, width - small.shape[1])))
    small_high = small.astype(BF)
    small_low = (small - small_high.astype(F32)).astype(BF)
    y_own = jnp.broadcast_to(output[rows : rows + 1], (seq_count, width))
    small = jnp.pad(jnp.stack([small_high, small_low, y_own], axis=1), ((0, 0), (0, 13), (0, 0)))
    slab = []
    for step in range(seq_count):
        part = lax.dynamic_index_in_dim(stacked, held[step], 0, False)
        rider = lax.dynamic_index_in_dim(small, (seq_rank + step) % seq_count, 0, False)
        part = jnp.concatenate([part, rider], axis=0)
        slab.append(shift(part, step, seq_count) if step else part)
    *slab, token_low, output = together(*slab, token_low, output)
    riders = [part[widest : widest + 3] for part in slab]
    slab = jnp.concatenate([part[:widest] for part in slab], axis=0)
    back_moved = send_back([output[:rows], token_low[:rows]])
    y_line = jnp.stack([part[2:3] for part in riders])
    y_far = swap(y_line, 1, batch_count)

    def plane_sum(kept, sent):
        chip = (kept.astype(F32) + swap(sent, 1, batch_count).astype(F32)).astype(BF)
        total = chip[0].astype(F32)
        for index, mask in enumerate(masks[1:]):
            total = total + swap(chip[index + 1], mask, batch_count).astype(F32)
        total = total.astype(BF)
        pair = jnp.stack([total, swap(total, 1, batch_count)])
        return [pair] + [swap(pair, mask, batch_count) for mask in masks[1:]]

    unit_offsets = offsets * (packed_rows(width, batch_count) // batch_count)
    slab, kept, sent = first_steps(plane_sum(*gram(slab, unit_offsets)), slab, unit_offsets)
    slab, kept, sent, y_far = together(slab, kept, sent, y_far)
    slab = last_steps(plane_sum(kept, sent), slab, unit_offsets)
    slab, *back_moved = together(slab, *back_moved)
    y_patches, dx_patches = join_back(back_moved, 0), join_back(back_moved, 1)
    back = slab.reshape(seq_count, widest, width)
    back = jnp.stack(
        [back[0]] + [shift(back[step], -step, seq_count) for step in range(1, seq_count)]
    )
    masters = (w_qkv, w_proj, w_up, w_down)
    ratios = (3.0, 1.0, 4.0, 0.25)
    updated = []
    for index in range(4):
        own_part = lax.dynamic_index_in_dim(
            back, (home_plane[index] - seq_rank) % seq_count, 0, False
        )[: fresh[index].shape[0]].astype(F32)
        if index < 3:
            own_part = own_part.T
        factor = math.sqrt(max(1.0, ratios[index]))
        updated.append(
            masters[index] * (1.0 - muon_rate * muon_decay) - muon_rate * factor * own_part
        )

    vec_sum = functools.reduce(
        jnp.add, [part[0].astype(F32) + part[1].astype(F32) for part in riders]
    )
    vec_sum = vec_sum[: vec_grad.shape[0] * column_count].reshape(-1, column_count)
    vec_sum, class_sums = vec_sum[:10], vec_sum[10:]
    chosen = (
        jnp.arange(class_count, dtype=jnp.int32)[:, None] == all_labels[None, :]
    ).astype(F32)
    table_sum = jnp.dot(chosen, class_sums, precision=highest, preferred_element_type=F32)
    y_rows = []
    for slot in range(images):
        turn = (seq_rank - (core * images + slot) * chips) % seq_count
        near = lax.dynamic_index_in_dim(y_line, turn, 0, False)
        far = lax.dynamic_index_in_dim(y_far, turn, 0, False)
        time_y = jnp.where(core == 0, near, far)
        class_y = jnp.where(core == 0, far, near)
        y_rows.append(jnp.concatenate([time_y, class_y], axis=0))
    y_rows = jnp.stack(y_rows)
    vec_new = adam_step(vectors, vec_first, vec_second, vec_sum)
    table_new = adam_step(table, table_first, table_second, table_sum)
    return (
        y_patches,
        y_rows,
        dx_patches,
        *updated,
        fresh[0].T,
        fresh[1].T,
        fresh[2].T,
        fresh[3],
        *vec_new,
        *table_new,
    )


def solution(mesh):
    tokens = P("batch", "seq", None)
    images = P("batch")
    extras = P("batch", None, None)
    columns = P(None, ("batch", "seq"))
    rows = P(("batch", "seq"), None)
    return jax.shard_map(
        body,
        mesh=mesh,
        in_specs=(
            tokens, images, images, tokens, tokens, extras, extras,
            columns, columns, columns, rows, columns, columns, columns, rows,
            columns, columns, columns, columns, columns, columns,
        ),
        out_specs=(
            tokens, extras, tokens, columns, columns, columns, rows,
            columns, columns, columns, rows, columns, columns, columns, columns, columns, columns,
        ),
        check_vma=False,
    )
```

```python
import functools
import math

import jax
import jax.numpy as jnp
from jax import lax
from jax.experimental import pallas as pl
from jax.experimental.pallas import tpu as pltpu
from jax.sharding import PartitionSpec as P

HEADS = 16
STEP = 10
FIRST_STEPS = 3
LAST_STEPS = 2

norm_eps = 1e-05
poly_first = 3.4445
poly_second = -4.775
poly_third = 2.0315
muon_momentum = 0.95
muon_rate = 1.5
muon_decay = 0.01
beta_one = 0.9
beta_two = 0.999
adam_rate = 1.0
adam_eps = 1e-08
highest = lax.Precision.HIGHEST
BF = jnp.bfloat16
F32 = jnp.float32
LOG2E = math.log2(math.e)
MIB = 1024 * 1024


def dot_nt(former, latter):
    return lax.dot_general(former, latter, (((1,), (1,)), ((), ())), preferred_element_type=F32)


def dot_nn(former, latter):
    return lax.dot_general(former, latter, (((1,), (0,)), ((), ())), preferred_element_type=F32)


def dot_tn(former, latter):
    return lax.dot_general(former, latter, (((0,), (0,)), ((), ())), preferred_element_type=F32)


def in_vmem(count):
    return [pl.BlockSpec(memory_space=pltpu.VMEM)] * count


def shape_of(shape, dtype):
    return jax.ShapeDtypeStruct(shape, dtype)


def head_window(head, size, width):
    start = jnp.minimum((head * size) // 128, (width - 256) // 128) * 128
    return pl.multiple_of(start, 128), head * size - start


def attention_forward_kernel(groups, valid_ref, own_ref, *refs):
    others, (o_ref, lse_ref, lsex_ref, acc) = refs[: groups - 1], refs[groups - 1 :]
    rows = own_ref.shape[0] - 16
    width = own_ref.shape[1] // 3
    size = width // HEADS
    factor = size**-0.5 * LOG2E
    tables = [(own_ref, width, 2 * width)] + [(ref, 0, width) for ref in others]
    parts = []
    for group, (ref, key_at, value_at) in enumerate(tables):
        parts.append((ref, pl.ds(0, rows), key_at, value_at, None))
        parts.append((ref, pl.ds(rows, 16), key_at, value_at, valid_ref[group]))
    acc[...] = jnp.zeros_like(acc)
    tile_row = lax.broadcasted_iota(jnp.int32, (16, rows), 0)

    def one_head(head, carry):
        start, offset = head_window(head, size, width)
        lane = lax.broadcasted_iota(jnp.int32, (rows, 256), 1)
        mask = (lane >= offset) & (lane < offset + size)
        query = jnp.where(mask, own_ref[:rows, pl.ds(start, 256)], jnp.zeros((), BF))
        scores = []
        for ref, span, key_at, value_at, valid in parts:
            score = dot_nt(ref[span, pl.ds(pl.multiple_of(key_at + start, 128), 256)], query)
            if valid is not None:
                score = jnp.where(tile_row < valid, score, -1e30)
            scores.append(score)
        largest = functools.reduce(
            jnp.maximum, [jnp.max(score, axis=0, keepdims=True) for score in scores]
        )
        largest = largest * factor
        total = jnp.zeros((1, rows), F32)
        out = jnp.zeros((256, rows), F32)
        for score, (ref, span, key_at, value_at, valid) in zip(scores, parts):
            power = jnp.exp2(score * factor - largest)
            total = total + jnp.sum(power, axis=0, keepdims=True)
            values = ref[span, pl.ds(pl.multiple_of(value_at + start, 128), 256)]
            out = out + dot_tn(values, power.astype(BF))
        out = (out * (1.0 / total)).T
        acc[:, pl.ds(start, 256)] += jnp.where(mask, out, 0.0)
        lse_ref[pl.ds(head, 1), :] = largest + jnp.log2(total)
        return carry

    lax.fori_loop(0, HEADS, one_head, 0, unroll=4)
    o_ref[:rows, :] = acc[...].astype(BF)
    head_row = lax.broadcasted_iota(jnp.int32, (HEADS, width), 0)
    lane = lax.broadcasted_iota(jnp.int32, (HEADS, width), 1)
    diagonal = (lane >= head_row * size) & (lane < head_row * size + size)
    extra = jnp.broadcast_to(own_ref[rows : rows + 16, :width].astype(F32)[0:1], (HEADS, width))
    extra = jnp.where(diagonal, extra, 0.0).astype(BF)
    tile_lane = lax.broadcasted_iota(jnp.int32, (HEADS, 16), 1)
    scores = []
    for ref, span, key_at, value_at, valid in parts:
        score = dot_nt(extra, ref[span, key_at : key_at + width])
        if valid is not None:
            score = jnp.where(tile_lane < valid, score, -1e30)
        scores.append(score)
    largest = functools.reduce(
        jnp.maximum, [jnp.max(score, axis=1, keepdims=True) for score in scores]
    )
    largest = largest * factor
    total = jnp.zeros((HEADS, 1), F32)
    out = jnp.zeros((HEADS, width), F32)
    for score, (ref, span, key_at, value_at, valid) in zip(scores, parts):
        power = jnp.exp2(score * factor - largest)
        total = total + jnp.sum(power, axis=1, keepdims=True)
        out = out + dot_nn(power.astype(BF), ref[span, value_at : value_at + width])
    out = jnp.sum(jnp.where(diagonal, out * (1.0 / total), 0.0), axis=0, keepdims=True)
    first = lax.broadcasted_iota(jnp.int32, (16, width), 0) < valid_ref[0]
    o_ref[rows:, :] = jnp.where(first, jnp.broadcast_to(out, (16, width)), 0.0).astype(BF)
    lsex_ref[...] = jnp.broadcast_to(largest + jnp.log2(total), (HEADS, 128))


def attention_forward(valid, own, others):
    padded, wide = own.shape
    rows, width, groups = padded - 16, wide // 3, 1 + len(others)
    pairs = rows * groups * rows
    return pl.pallas_call(
        functools.partial(attention_forward_kernel, groups),
        out_shape=[
            shape_of((padded, width), BF),
            shape_of((HEADS, rows), F32),
            shape_of((HEADS, 128), F32),
        ],
        in_specs=[pl.BlockSpec(memory_space=pltpu.SMEM)] + in_vmem(groups),
        out_specs=in_vmem(3),
        scratch_shapes=[pltpu.VMEM((rows, width), F32)],
        compiler_params=pltpu.CompilerParams(vmem_limit_bytes=60 * MIB),
        cost_estimate=pl.CostEstimate(
            flops=16 * pairs * width,
            bytes_accessed=groups * padded * wide * 2,
            transcendentals=HEADS * pairs,
        ),
        name="attention_forward",
    )(valid, own, *others)


def attention_backward_kernel(groups, valid_ref, own_ref, *refs):
    others, refs = refs[: groups - 1], refs[groups - 1 :]
    o_ref, do_ref, lse_ref, lsex_ref = refs[:4]
    dq_ref, dkv_refs, refs = refs[4], refs[5 : 5 + groups], refs[5 + groups :]
    dq_acc, dk_acc, dv_acc, delta = refs
    rows = own_ref.shape[0] - 16
    padded = rows + 16
    width = own_ref.shape[1] // 3
    size = width // HEADS
    scale = size**-0.5
    factor = scale * LOG2E
    tables = [(own_ref, width, 2 * width)] + [(ref, 0, width) for ref in others]
    parts = []
    for group, (ref, key_at, value_at) in enumerate(tables):
        parts.append((ref, 0, rows, key_at, value_at, group, None))
        parts.append((ref, rows, 16, key_at, value_at, group, valid_ref[group]))
    head_row = lax.broadcasted_iota(jnp.int32, (HEADS, width), 0)
    lane = lax.broadcasted_iota(jnp.int32, (HEADS, width), 1)
    diagonal = (lane >= head_row * size) & (lane < head_row * size + size)
    ones = jnp.where(diagonal, 1.0, 0.0).astype(BF)
    product = do_ref[:rows, :].astype(F32) * o_ref[:rows, :].astype(F32)
    upper = product.astype(BF)
    lower = (product - upper.astype(F32)).astype(BF)
    delta[...] = dot_nt(ones, upper) + dot_nt(ones, lower)
    extra = jnp.broadcast_to(own_ref[rows:padded, :width].astype(F32)[0:1], (HEADS, width))
    extra = jnp.where(diagonal, extra, 0.0).astype(BF)
    extra_do = jnp.broadcast_to(do_ref[rows:padded, :].astype(F32)[0:1], (HEADS, width))
    extra_do = jnp.where(diagonal, extra_do, 0.0)
    extra_o = o_ref[rows:padded, :].astype(F32)[0:1]
    extra_delta = jnp.sum(extra_do * extra_o, axis=1, keepdims=True)
    extra_do = extra_do.astype(BF)
    extra_lse = lsex_ref[:, 0:1]
    tile_lane = lax.broadcasted_iota(jnp.int32, (HEADS, 16), 1)
    extra_dq = jnp.zeros((HEADS, width), F32)
    for ref, at, count, key_at, value_at, group, valid in parts:
        keys = ref[at : at + count, key_at : key_at + width]
        values = ref[at : at + count, value_at : value_at + width]
        prob = jnp.exp2(dot_nt(extra, keys) * factor - extra_lse)
        if valid is not None:
            prob = jnp.where(tile_lane < valid, prob, 0.0)
        score_grad = (prob * (dot_nt(extra_do, values) - extra_delta)).astype(BF)
        extra_dq = extra_dq + dot_nn(score_grad, keys)
        dk_acc[group, at : at + count, :] = dot_tn(score_grad, extra)
        dv_acc[group, at : at + count, :] = dot_tn(prob.astype(BF), extra_do)
    extra_dq = jnp.sum(jnp.where(diagonal, extra_dq, 0.0), axis=0, keepdims=True) * scale
    first = lax.broadcasted_iota(jnp.int32, (16, width), 0) < valid_ref[0]
    dq_ref[rows:, :] = jnp.where(first, jnp.broadcast_to(extra_dq, (16, width)), 0.0).astype(BF)
    dq_acc[...] = jnp.zeros_like(dq_acc)
    tile_row = lax.broadcasted_iota(jnp.int32, (16, rows), 0)

    def one_head(head, carry):
        start, offset = head_window(head, size, width)
        window = pl.ds(start, 256)
        lanes = lax.broadcasted_iota(jnp.int32, (rows, 256), 1)
        mask = (lanes >= offset) & (lanes < offset + size)
        zero = jnp.zeros((), BF)
        query = jnp.where(mask, own_ref[:rows, window], zero)
        out_grad = jnp.where(mask, do_ref[:rows, window], zero)
        lse = lse_ref[pl.ds(head, 1), :]
        row_delta = delta[pl.ds(head, 1), :]
        query_grad = jnp.zeros((256, rows), F32)
        for ref, at, count, key_at, value_at, group, valid in parts:
            keys = ref[at : at + count, pl.ds(pl.multiple_of(key_at + start, 128), 256)]
            values = ref[at : at + count, pl.ds(pl.multiple_of(value_at + start, 128), 256)]
            prob = jnp.exp2(dot_nt(keys, query) * factor - lse)
            if valid is not None:
                prob = jnp.where(tile_row < valid, prob, 0.0)
            score_grad = (prob * (dot_nt(values, out_grad) - row_delta)).astype(BF)
            dv_acc[group, at : at + count, window] += dot_nn(prob.astype(BF), out_grad)
            dk_acc[group, at : at + count, window] += dot_nn(score_grad, query)
            query_grad = query_grad + dot_tn(keys, score_grad)
        dq_acc[:, window] += jnp.where(mask, query_grad.T, 0.0)
        return carry

    lax.fori_loop(0, HEADS, one_head, 0, unroll=4)
    dq_ref[:rows, :] = (dq_acc[...] * scale).astype(BF)
    for group, dkv_ref in enumerate(dkv_refs):
        dkv_ref[:, :width] = (dk_acc[group] * scale).astype(dkv_ref.dtype)
        dkv_ref[:, width:] = dv_acc[group].astype(dkv_ref.dtype)


def attention_backward(valid, own, others, attended, attended_grad, lse, lse_extra):
    padded, wide = own.shape
    rows, width, groups = padded - 16, wide // 3, 1 + len(others)
    pairs = rows * groups * rows
    return pl.pallas_call(
        functools.partial(attention_backward_kernel, groups),
        out_shape=[shape_of((padded, width), BF)]
        + [shape_of((padded, 2 * width), BF) for _ in range(groups)],
        in_specs=[pl.BlockSpec(memory_space=pltpu.SMEM)] + in_vmem(groups + 4),
        out_specs=in_vmem(1 + groups),
        scratch_shapes=[
            pltpu.VMEM((rows, width), F32),
            pltpu.VMEM((groups, padded, width), F32),
            pltpu.VMEM((groups, padded, width), F32),
            pltpu.VMEM((HEADS, rows), F32),
        ],
        compiler_params=pltpu.CompilerParams(vmem_limit_bytes=60 * MIB),
        cost_estimate=pl.CostEstimate(
            flops=36 * pairs * width,
            bytes_accessed=2 * groups * padded * wide * 2,
            transcendentals=HEADS * pairs,
        ),
        name="attention_backward",
    )(valid, own, *others, attended, attended_grad, lse, lse_extra)


def mlp_kernel(
    units, unit, block, first_ref, bias_ref, rows_ref, n_own, n_other, dm_own, dm_other,
    out_own, out_other, dn_own, dn_other, gup_ref, gdown_ref, gbias_ref,
    out_acc, dn_acc, up_all, down_all, n_ref, dm_ref, sems,
):
    step = pl.program_id(0)

    @pl.when(step == 0)
    def _():
        copies = []
        for index in range(units):
            start = pl.multiple_of(first_ref[index], 16)
            for which, joined in enumerate((up_all, down_all)):
                copy = pltpu.make_async_copy(
                    rows_ref.at[pl.ds(start + which * unit, unit)],
                    joined.at[pl.ds(index * unit, unit)],
                    sems.at[2 * index + which],
                )
                copy.start()
                copies.append(copy)
        half = out_own.shape[0]
        for index, (source, joined, at) in enumerate(
            ((n_own, n_ref, 0), (n_other, n_ref, half), (dm_own, dm_ref, 0), (dm_other, dm_ref, half))
        ):
            copy = pltpu.make_async_copy(
                source, joined.at[pl.ds(at, half)], sems.at[2 * units + index]
            )
            copy.start()
            copies.append(copy)
        out_acc[...] = jnp.zeros_like(out_acc)
        dn_acc[...] = jnp.zeros_like(dn_acc)
        for copy in copies:
            copy.wait()

    span = pl.ds(pl.multiple_of(step * block, block), block)
    normed, dm, up, down = n_ref[...], dm_ref[...], up_all[span, :], down_all[span, :]
    hidden = dot_nt(normed, up) + bias_ref[...]
    below = 0.5 * (1.0 + lax.erf(hidden * (2.0**-0.5)))
    activated = (hidden * below).astype(BF)
    out_acc[...] += dot_nn(activated, down)
    gdown_ref[...] = dot_tn(activated, dm).astype(BF)
    slope = below + hidden * (jnp.exp(-0.5 * hidden * hidden) * (1.0 / math.sqrt(2 * math.pi)))
    hidden_grad = (dot_nt(dm, down) * slope).astype(BF)
    dn_acc[...] += dot_nn(hidden_grad, up)
    gup_ref[...] = dot_tn(hidden_grad, normed).astype(BF)
    gbias_ref[...] = jnp.sum(hidden_grad.astype(F32), axis=0, keepdims=True)
    half = out_own.shape[0]

    @pl.when(step == pl.num_programs(0) - 1)
    def _():
        out_own[...] = out_acc[:half, :]
        out_other[...] = out_acc[half:, :].astype(BF)
        dn_own[...] = dn_acc[:half, :]
        dn_other[...] = dn_acc[half:, :].astype(BF)


def mlp(normed, dm, bias, gathered, first_rows, block=768):
    half, width = normed[0].shape
    hidden = bias.shape[1]
    rows = 2 * half
    units = first_rows.shape[0]
    unit = hidden // units
    if unit % 16:
        wide = -(-unit // 16) * 16
        fill = ((0, 0), (0, wide - unit), (0, 0))
        gathered = jnp.pad(gathered.reshape(2 * units, unit, width), fill).reshape(-1, width)
        bias = jnp.pad(bias.reshape(units, unit), fill[:2]).reshape(1, -1)
        *outs, grad_up, grad_down, grad_bias = mlp(
            normed, dm, bias, gathered, first_rows // unit * wide, block
        )
        grads = [
            grad.reshape(units, wide, width)[:, :unit].reshape(hidden, width)
            for grad in (grad_up, grad_down)
        ]
        return *outs, *grads, grad_bias.reshape(units, wide)[:, :unit].reshape(1, hidden)
    whole = lambda step: (0, 0)
    part = lambda step: (step, 0)
    return pl.pallas_call(
        functools.partial(mlp_kernel, units, unit, block),
        grid=(hidden // block,),
        out_shape=[shape_of((half, width), dtype) for dtype in (F32, BF, F32, BF)]
        + [shape_of((hidden, width), BF)] * 2
        + [shape_of((1, hidden), F32)],
        in_specs=[
            pl.BlockSpec(memory_space=pltpu.SMEM),
            pl.BlockSpec((1, block), lambda step: (0, step)),
        ]
        + [pl.BlockSpec(memory_space=pl.ANY)] * 5,
        out_specs=[pl.BlockSpec((half, width), whole)] * 4
        + [pl.BlockSpec((block, width), part)] * 2
        + [pl.BlockSpec((1, block), lambda step: (0, step))],
        scratch_shapes=[pltpu.VMEM((rows, width), F32)] * 2
        + [pltpu.VMEM((hidden, width), BF)] * 2
        + [pltpu.VMEM((rows, width), BF)] * 2
        + [pltpu.SemaphoreType.DMA((2 * units + 4,))],
        compiler_params=pltpu.CompilerParams(vmem_limit_bytes=62 * MIB),
        cost_estimate=pl.CostEstimate(
            flops=12 * rows * width * hidden,
            bytes_accessed=8 * hidden * width + 16 * rows * width,
            transcendentals=2 * rows * hidden,
        ),
        name="mlp",
    )(first_rows.astype(jnp.int32), bias, gathered, *normed, *dm)


def column_blocks(width):
    return [(at, min(256, width - at)) for at in range(0, width, 256)]


def packed_rows(width, units):
    rows = sum((at + w) * w // 256 for at, w in column_blocks(width))
    return -(-rows // (16 * units)) * (16 * units)


def gram_into(slab, slab_t, out_ref):
    row = 0
    for at, w in column_blocks(slab.shape[1]):
        high = at + w
        value = dot_nn(slab_t[0:high, :], slab[:, at:high]).astype(BF)
        if w == 256:
            out_ref[row : row + high, :] = value
            row += high
        else:
            half = high // 2
            out_ref[row : row + half, 0:128] = value[:half]
            out_ref[row : row + half, 128:256] = value[half:]
            row += half
    out_ref[row:, :] = jnp.zeros((out_ref.shape[0] - row, 256), BF)


def unpack(packed, width, store):
    row = 0
    for at, w in column_blocks(width):
        high = at + w
        if w == 256:
            value = packed[row : row + high, :]
            row += high
        else:
            half = high // 2
            value = jnp.concatenate(
                [packed[row : row + half, 0:128], packed[row : row + half, 128:256]], axis=0
            )
            row += half
        store(at, w, value.astype(F32))


def store_both(ref, at, w, value):
    ref[0 : at + w, at : at + w] = value.astype(BF)
    if at:
        ref[at : at + w, 0:at] = value[0:at].T.astype(BF)


def on_diagonal(at, w):
    rows = lax.broadcasted_iota(jnp.int32, (at + w, w), 0)
    return rows == lax.broadcasted_iota(jnp.int32, (at + w, w), 1) + at


def symmetric_product(former, latter, width, done):
    for at, w in column_blocks(width):
        done(at, w, dot_nn(former[0 : at + w, :], latter[:, at : at + w]))


def deal(packed, offset_ref, kept, sent, sems):
    copies = []
    count, unit = kept.shape[0], kept.shape[1]
    for index in range(2 * count):
        start = pl.multiple_of(offset_ref[index], 16)
        out = kept if index < count else sent
        copy = pltpu.make_async_copy(
            packed.at[pl.ds(start, unit)], out.at[index % count], sems.at[index]
        )
        copy.start()
        copies.append(copy)
    for copy in copies:
        copy.wait()


def collect(near, far, offset_ref, packed, sems):
    copies = []
    count, unit = far.shape[0], far.shape[1]
    for index in range(2 * count):
        start = pl.multiple_of(offset_ref[index], 16)
        source = near[index] if index < count else far.at[index - count]
        copy = pltpu.make_async_copy(source, packed.at[pl.ds(start, unit)], sems.at[index])
        copy.start()
        copies.append(copy)
    for copy in copies:
        copy.wait()


def gram_kernel(offset_ref, slab_ref, kept, sent, slab_t, packed, sems):
    slab_t[...] = slab_ref[...].T
    gram_into(slab_ref, slab_t, packed)
    deal(packed, offset_ref, kept, sent, sems)


SMEM = pl.BlockSpec(memory_space=pltpu.SMEM)
ANYWHERE = pl.BlockSpec(memory_space=pl.ANY)


def gram(slab, offsets):
    rows, width = slab.shape
    units = offsets.shape[0]
    size = packed_rows(width, units)
    part = shape_of((units // 2, size // units, 256), BF)
    return pl.pallas_call(
        gram_kernel,
        out_shape=[part, part],
        in_specs=[SMEM] + in_vmem(1),
        out_specs=[ANYWHERE] * 2,
        scratch_shapes=[
            pltpu.VMEM((width, rows), BF),
            pltpu.VMEM((size, 256), BF),
            pltpu.SemaphoreType.DMA((units,)),
        ],
        compiler_params=pltpu.CompilerParams(vmem_limit_bytes=50 * MIB),
        cost_estimate=pl.CostEstimate(
            flops=2 * rows * width * width,
            bytes_accessed=2 * rows * width + 2 * width * width,
            transcendentals=0,
        ),
        name="gram",
    )(offsets, slab)


def first_steps_kernel(count, offset_ref, slab_ref, *refs):
    pairs, refs = refs[:count], refs[count:]
    slab_out, kept, sent = refs[:3]
    gram_f, mix_f, prod_f, poly_f, gram_b, mix_b, prod_b, poly_b, slab_t, packed, sems = refs[3:]
    width = slab_ref.shape[1]
    collect(pairs[:-1], pairs[-1], offset_ref, packed, sems)
    square = [jnp.zeros((1, 1), F32)]

    def add_diagonal(at, w, value):
        here = jnp.where(on_diagonal(at, w), value, 0.0)
        square[0] = square[0] + jnp.sum(here, keepdims=True).reshape(1, 1)

    unpack(packed, width, add_diagonal)
    inverse = 1.0 / (jnp.sqrt(square[0]) + 1e-07)

    def start(at, w, value):
        value = value * inverse * inverse
        gram_f[0 : at + w, at : at + w] = value
        store_both(gram_b, at, w, value)

    unpack(packed, width, start)
    lead = 1.0
    for step in range(FIRST_STEPS):
        def make_mix(at, w, value):
            span = (slice(0, at + w), slice(at, at + w))
            mix = poly_second * gram_f[span] + poly_third * value
            mix_f[span] = mix
            store_both(mix_b, at, w, mix)
            if step == 0:
                poly_f[span] = mix
                store_both(poly_b, at, w, mix)

        symmetric_product(gram_b, gram_b, width, make_mix)
        if step > 0:

            def join(at, w, value):
                span = (slice(0, at + w), slice(at, at + w))
                poly = poly_first * poly_f[span] + lead * mix_f[span] + value
                poly_f[span] = poly
                store_both(prod_b, at, w, poly)

            symmetric_product(mix_b, poly_b, width, join)
            poly_b, prod_b = prod_b, poly_b
        lead = lead * poly_first
        if step < FIRST_STEPS - 1:

            def keep(at, w, value):
                prod_f[0 : at + w, at : at + w] = value
                store_both(prod_b, at, w, value)

            symmetric_product(gram_b, mix_b, width, keep)

            def next_gram(at, w, value):
                span = (slice(0, at + w), slice(at, at + w))
                new = poly_first**2 * gram_f[span] + 2 * poly_first * prod_f[span] + value
                gram_f[span] = new
                store_both(gram_b, at, w, new)

            symmetric_product(prod_b, mix_b, width, next_gram)
    slab = slab_ref[...]
    moved = ((lead * slab.astype(F32) + dot_nn(slab, poly_b[...])) * inverse).astype(BF)
    slab_out[...] = moved
    slab_t[...] = moved.T
    gram_into(moved, slab_t, packed)
    deal(packed, offset_ref, kept, sent, sems)


def first_steps(pairs, slab, offsets):
    rows, width = slab.shape
    square = (width, width)
    units = offsets.shape[0]
    size = packed_rows(width, units)
    part = shape_of((units // 2, size // units, 256), BF)
    return pl.pallas_call(
        functools.partial(first_steps_kernel, len(pairs)),
        out_shape=[shape_of((rows, width), BF), part, part],
        in_specs=[SMEM] + in_vmem(1) + [ANYWHERE] * len(pairs),
        out_specs=in_vmem(1) + [ANYWHERE] * 2,
        scratch_shapes=[pltpu.VMEM(square, F32)] * 4
        + [pltpu.VMEM(square, BF)] * 4
        + [pltpu.VMEM((width, rows), BF), pltpu.VMEM((size, 256), BF)]
        + [pltpu.SemaphoreType.DMA((units,))],
        compiler_params=pltpu.CompilerParams(vmem_limit_bytes=60 * MIB),
        cost_estimate=pl.CostEstimate(
            flops=18 * width**3,
            bytes_accessed=4 * rows * width + 4 * width * width,
            transcendentals=0,
        ),
        name="first_steps",
    )(offsets, slab, *pairs)


def last_steps_kernel(count, offset_ref, slab_ref, *refs):
    pairs, refs = refs[:count], refs[count:]
    slab_out, gram_b, poly_b, prod_b, join_b, packed, sems = refs
    width = slab_ref.shape[1]
    collect(pairs[:-1], pairs[-1], offset_ref, packed, sems)
    unpack(packed, width, lambda at, w, value: store_both(gram_b, at, w, value))
    for step in range(LAST_STEPS):

        def make_poly(at, w, value):
            held = gram_b[0 : at + w, at : at + w].astype(F32)
            poly = poly_second * held + poly_third * value
            poly = poly + jnp.where(on_diagonal(at, w), poly_first, 0.0)
            store_both(poly_b, at, w, poly)
            if step == 0:
                store_both(join_b, at, w, poly)

        symmetric_product(gram_b, gram_b, width, make_poly)
        if step > 0:
            symmetric_product(
                poly_b, join_b, width, lambda at, w, value: store_both(prod_b, at, w, value)
            )
            join_b, prod_b = prod_b, join_b
        if step < LAST_STEPS - 1:
            symmetric_product(
                gram_b, poly_b, width, lambda at, w, value: store_both(prod_b, at, w, value)
            )
            symmetric_product(
                prod_b, poly_b, width, lambda at, w, value: store_both(gram_b, at, w, value)
            )
    slab_out[...] = dot_nn(slab_ref[...], join_b[...]).astype(BF)


def last_steps(pairs, slab, offsets):
    rows, width = slab.shape
    units = offsets.shape[0]
    size = packed_rows(width, units)
    return pl.pallas_call(
        functools.partial(last_steps_kernel, len(pairs)),
        out_shape=shape_of((rows, width), BF),
        in_specs=[SMEM] + in_vmem(1) + [ANYWHERE] * len(pairs),
        out_specs=in_vmem(1)[0],
        scratch_shapes=[pltpu.VMEM((width, width), BF)] * 4
        + [pltpu.VMEM((size, 256), BF), pltpu.SemaphoreType.DMA((units,))],
        compiler_params=pltpu.CompilerParams(vmem_limit_bytes=60 * MIB),
        cost_estimate=pl.CostEstimate(
            flops=10 * width**3,
            bytes_accessed=4 * rows * width + 2 * width * width,
            transcendentals=0,
        ),
        name="last_steps",
    )(offsets, slab, *pairs)


def line_up_kernel(counts, place_ref, *refs):
    line, qkv, proj, small_at = counts
    blocks, (former, latter, held, joined) = refs[:line], refs[line:]
    for step, block in enumerate(blocks):
        held[step] = block[...]
    total = None
    for index in range(line):
        step = lax.rem(place_ref[0] - index + line, line)
        value = held[step].astype(F32)
        joined[index * qkv : (index + 1) * qkv, :] = value[:qkv]
        at = line * qkv + index * proj
        joined[at : at + proj, :] = value[qkv : qkv + proj]
        small = value[small_at:]
        total = small if total is None else total + small
    half = former.shape[0]
    rest = line * (qkv + proj) - half
    former[...] = joined[:half, :].astype(BF)
    latter[:rest, :] = joined[half:, :].astype(BF)
    latter[rest:, :] = total.astype(BF)


def line_up(blocks, place, qkv, proj):
    line = len(blocks)
    rows, width = blocks[0].shape
    small_at = -(-(qkv + proj) // 16) * 16
    half = line * (qkv + proj) // 2
    return pl.pallas_call(
        functools.partial(line_up_kernel, (line, qkv, proj, small_at)),
        out_shape=[
            shape_of((half, width), BF),
            shape_of((line * (qkv + proj) - half + rows - small_at, width), BF),
        ],
        in_specs=[SMEM] + in_vmem(line),
        out_specs=in_vmem(2),
        scratch_shapes=[
            pltpu.VMEM((line, rows, width), BF),
            pltpu.VMEM((line * (qkv + proj), width), F32),
        ],
        compiler_params=pltpu.CompilerParams(vmem_limit_bytes=40 * MIB),
        name="line_up",
    )(place.reshape(1), *blocks)


def packed_grad_kernel(offset_ref, query_ref, own_ref, arrived_ref, other_ref, packed, kept, sent, grad, sems):
    width = query_ref.shape[1]
    packed[:, :width] = query_ref[...]
    total = own_ref[...].astype(F32) + arrived_ref[...].astype(F32)
    packed[:, width:] = total.astype(BF)
    qkv_grad_kernel(offset_ref, packed, other_ref, kept, sent, grad, sems)


def packed_grad_of(query_grad, own, arrived, other_side, offsets):
    rows, width = query_grad.shape
    long = 3 * width
    units = offsets.shape[0]
    unit = long // units
    if unit % 16:
        total = (own.astype(F32) + arrived.astype(F32)).astype(BF)
        packed = jnp.concatenate([query_grad, total], axis=1)
        return packed, *qkv_grad(packed, other_side, offsets)
    part = shape_of((units // 2, unit, width), BF)
    return pl.pallas_call(
        packed_grad_kernel,
        out_shape=[shape_of((rows, long), BF), part, part],
        in_specs=[SMEM] + in_vmem(4),
        out_specs=in_vmem(1) + [ANYWHERE] * 2,
        scratch_shapes=[pltpu.VMEM((long, width), BF), pltpu.SemaphoreType.DMA((units,))],
        compiler_params=pltpu.CompilerParams(vmem_limit_bytes=50 * MIB),
        cost_estimate=pl.CostEstimate(
            flops=2 * rows * long * width,
            bytes_accessed=2 * rows * (2 * long + width) + 2 * long * width,
            transcendentals=0,
        ),
        name="packed_grad",
    )(offsets, query_grad, own, arrived, other_side)


def first_norm_kernel(packed_ref, weight_ref, standard_ref, inverse_ref, after_ref, gain_ref, low_ref, sums_ref):
    grad = dot_nn(packed_ref[...], weight_ref[...])
    standard = standard_ref[...]
    sums_ref[...] = jnp.zeros_like(sums_ref)
    sums_ref[0:1, :] = jnp.sum(grad * standard, axis=0, keepdims=True)
    sums_ref[1:2, :] = jnp.sum(grad, axis=0, keepdims=True)
    scaled = grad * gain_ref[...]
    average = jnp.mean(scaled, axis=1, keepdims=True)
    along = jnp.mean(scaled * standard, axis=1, keepdims=True)
    token = after_ref[...] + inverse_ref[...] * (scaled - average - standard * along)
    low_ref[...] = token.astype(BF)
    rows = token.shape[0] - 16
    sums_ref[8:16, :] = token[rows : rows + 8, :]


def first_norm_back(packed_grad, weight, standard, inverse, after, gain):
    rows, width = standard.shape
    long = weight.shape[0]
    low, sums = pl.pallas_call(
        first_norm_kernel,
        out_shape=[shape_of((rows, width), BF), shape_of((16, width), F32)],
        in_specs=in_vmem(6),
        out_specs=in_vmem(2),
        compiler_params=pltpu.CompilerParams(vmem_limit_bytes=60 * MIB),
        cost_estimate=pl.CostEstimate(
            flops=2 * rows * long * width,
            bytes_accessed=2 * rows * (long + 5 * width) + 2 * long * width,
            transcendentals=0,
        ),
        name="first_norm_back",
    )(packed_grad, weight, standard, inverse, after, gain)
    return low, sums[0:2], sums[8:9]


def qkv_grad_kernel(offset_ref, long_ref, other_ref, kept, sent, grad, sems):
    other = other_ref[...]
    for at, w in [(at, 384) for at in range(0, grad.shape[0], 384)]:
        grad[at : at + w, :] = dot_tn(long_ref[:, at : at + w], other).astype(BF)
    deal(grad, offset_ref, kept, sent, sems)


def qkv_grad(long_side, other_side, offsets):
    rows, long = long_side.shape
    width = other_side.shape[1]
    units = offsets.shape[0]
    unit = long // units
    if unit % 16:
        grad = dot_tn(long_side, other_side).astype(BF).reshape(units, unit, width)
        parts = [
            lax.dynamic_index_in_dim(grad, offsets[index] // unit, 0, False)
            for index in range(units)
        ]
        return jnp.stack(parts[: units // 2]), jnp.stack(parts[units // 2 :])
    part = shape_of((units // 2, unit, width), BF)
    return pl.pallas_call(
        qkv_grad_kernel,
        out_shape=[part, part],
        in_specs=[SMEM] + in_vmem(2),
        out_specs=[ANYWHERE] * 2,
        scratch_shapes=[pltpu.VMEM((long, width), BF), pltpu.SemaphoreType.DMA((units,))],
        compiler_params=pltpu.CompilerParams(vmem_limit_bytes=50 * MIB),
        cost_estimate=pl.CostEstimate(
            flops=2 * rows * long * width,
            bytes_accessed=2 * rows * (long + width) + 2 * long * width,
            transcendentals=0,
        ),
        name="qkv_grad",
    )(offsets, long_side, other_side)


def place_kernel(moves, count, outputs, offset_ref, *refs):
    pieces, outs, sems = refs[:count], refs[count : count + outputs], refs[count + outputs]
    copies = []
    for index, (piece, at, rows, out, _) in enumerate(moves):
        start = pl.multiple_of(offset_ref[index], 16)
        copy = pltpu.make_async_copy(
            pieces[piece].at[pl.ds(at, rows)], outs[out].at[pl.ds(start, rows)], sems.at[index]
        )
        copy.start()
        copies.append(copy)
    for copy in copies:
        copy.wait()


def place(pieces, moves, sizes):
    width = pieces[0].shape[1]
    if any(at % 16 or rows % 16 for _, at, rows, _, _ in moves):
        outs = [jnp.zeros((size, width), BF) for size in sizes]
        for piece, at, rows, out, offset in moves:
            part = pieces[piece][at : at + rows]
            outs[out] = lax.dynamic_update_slice_in_dim(outs[out], part, offset, 0)
        return outs
    offsets = jnp.stack([move[4] for move in moves]).astype(jnp.int32)
    static = [move[:4] + (None,) for move in moves]
    return pl.pallas_call(
        functools.partial(place_kernel, static, len(pieces), len(sizes)),
        out_shape=[shape_of((size, width), BF) for size in sizes],
        in_specs=[pl.BlockSpec(memory_space=pltpu.SMEM)]
        + [pl.BlockSpec(memory_space=pl.ANY)] * len(pieces),
        out_specs=in_vmem(len(sizes)),
        scratch_shapes=[pltpu.SemaphoreType.DMA((len(moves),))],
        compiler_params=pltpu.CompilerParams(vmem_limit_bytes=40 * MIB),
        cost_estimate=pl.CostEstimate(
            flops=0, bytes_accessed=4 * sum(sizes) * width, transcendentals=0
        ),
        name="place",
    )(offsets, *pieces)


def together_kernel(*refs):
    pass


def together(*arrays, cost=0):
    anywhere = pl.BlockSpec(memory_space=pl.ANY)
    return pl.pallas_call(
        together_kernel,
        out_shape=[shape_of(array.shape, array.dtype) for array in arrays],
        in_specs=[anywhere] * len(arrays),
        out_specs=[anywhere] * len(arrays),
        input_output_aliases={index: index for index in range(len(arrays))},
        cost_estimate=pl.CostEstimate(flops=cost, bytes_accessed=0, transcendentals=0),
        name="together",
    )(*arrays)


def beside(*arrays):
    got = together(*arrays, cost=10**11)
    return got if len(arrays) > 1 else got[0]


def shift(values, step, seq_count):
    return lax.ppermute(
        values, "seq", [(rank, (rank + step) % seq_count) for rank in range(seq_count)]
    )


def swap(values, bit, batch_count):
    return lax.ppermute(values, "batch", [(rank, rank ^ bit) for rank in range(batch_count)])


def line_gather(values, seq_count):
    return [values] + [shift(values, step, seq_count) for step in range(1, seq_count)]


def line_reduce(blocks, seq_count):
    total = blocks[0].astype(F32)
    for step in range(1, seq_count):
        total = total + shift(blocks[step], -step, seq_count).astype(F32)
    return total


def from_own(values, seq_count):
    rank = lax.axis_index("seq")
    blocks = values.reshape(seq_count, -1, values.shape[1])
    return [
        lax.dynamic_index_in_dim(blocks, (rank - step) % seq_count, 0, False)
        for step in range(seq_count)
    ]


def in_line(blocks, seq_count):
    stacked = jnp.stack(blocks)
    rank = lax.axis_index("seq")
    order = (rank - jnp.arange(seq_count, dtype=jnp.int32)) % seq_count
    return jnp.take(stacked, order, axis=0)


def plane_gather(block, bits, batch_count):
    blocks = {0: block}
    for bit in bits:
        for mask in list(blocks):
            blocks[mask ^ bit] = swap(blocks[mask], bit, batch_count)
    return blocks


def plane_reduce(blocks, bits, batch_count):
    blocks = dict(blocks)
    for bit in bits:
        kept = [mask for mask in blocks if not mask & bit]
        rows = blocks[0].shape[0]
        arrived = swap(jnp.concatenate([blocks[mask ^ bit] for mask in kept], axis=0), bit, batch_count)
        blocks = {
            mask: (
                blocks[mask].astype(F32) + arrived[index * rows : (index + 1) * rows].astype(F32)
            ).astype(BF)
            for index, mask in enumerate(kept)
        }
    return blocks[0]


def gather_small(values, batch_count, seq_count):
    return gather_batch(in_line(line_gather(values, seq_count), seq_count), batch_count)


def gather_batch(values, batch_count):
    joined = values[None]
    bit = 1
    while bit < batch_count:
        joined = jnp.concatenate([joined, swap(joined, bit, batch_count)], axis=0)
        bit *= 2
    order = lax.axis_index("batch") ^ jnp.arange(batch_count, dtype=jnp.int32)
    return jnp.take(joined, order, axis=0)


def standardize(values):
    average = jnp.mean(values, axis=-1, keepdims=True)
    centred = values - average
    variance = jnp.mean(centred * centred, axis=-1, keepdims=True)
    inverse = lax.rsqrt(variance + norm_eps)
    return centred * inverse, inverse


def standardize_back(grad, standard, inverse):
    average = jnp.mean(grad, axis=-1, keepdims=True)
    along = jnp.mean(grad * standard, axis=-1, keepdims=True)
    return inverse * (grad - average - standard * along)


def time_token(step_values, model_width):
    half_width = model_width // 2
    frequency = jnp.exp(-math.log(10000.0) * jnp.arange(half_width, dtype=F32) / half_width)
    angles = step_values.astype(F32)[:, None] * frequency[None, :]
    return jnp.concatenate([jnp.cos(angles), jnp.sin(angles)], axis=-1)


def adam_step(parameter, first_state, second, gradient):
    first_new = beta_one * first_state + (1.0 - beta_one) * gradient
    second_new = beta_two * second + (1.0 - beta_two) * gradient * gradient
    first_hat = first_new / (1.0 - beta_one**STEP)
    second_hat = second_new / (1.0 - beta_two**STEP)
    return (
        first_new,
        second_new,
        parameter - adam_rate * first_hat / (jnp.sqrt(second_hat) + adam_eps),
    )


def body(
    patches, timesteps, labels, next_grad, skip_grad, next_extra, skip_extra,
    w_qkv, w_proj, w_up, w_down, mom_qkv, mom_proj, mom_up, mom_down,
    vectors, vec_first, vec_second, table, table_first, table_second,
):
    images, patch_rows, width = patches.shape
    batch_count = lax.axis_size("batch")
    seq_count = lax.axis_size("seq")
    shards = batch_count * seq_count
    batch_rank = lax.axis_index("batch")
    seq_rank = lax.axis_index("seq")
    shard_rank = batch_rank * seq_count + seq_rank
    core = batch_rank % 2
    chips = seq_count // (2 * images)
    own_image = seq_rank // chips
    own_core, own_slot = own_image // images, own_image % images
    sub_rank = seq_rank % chips
    bits = [1 << level for level in range(1, (batch_count - 1).bit_length())]
    up_bits, down_bits = bits, bits[::-1]

    def route(matching):
        pairs = []
        for rank in range(batch_count):
            for place_z in range(seq_count):
                code = place_z ^ matching
                slot, rest = code // (2 * chips), code % (2 * chips)
                to_core, sub = rest // chips, rest % chips
                to_z = ((rank % 2) * images + slot) * chips + sub
                pairs.append((rank * seq_count + place_z, (rank - rank % 2 + to_core) * seq_count + to_z))
        return pairs

    piece_rows = images * patch_rows // seq_count

    def send(values):
        pieces = values.reshape(seq_count, piece_rows, width)
        return [
            lax.ppermute(
                lax.dynamic_index_in_dim(pieces, seq_rank ^ matching, 0, False),
                ("batch", "seq"),
                route(matching),
            )
            for matching in range(seq_count)
        ]

    def send_back(values):
        pieces = jnp.stack([array.reshape(seq_count, piece_rows, width) for array in values], axis=1)
        return [
            lax.ppermute(
                pieces[matching], ("batch", "seq"), [(to, at) for at, to in route(matching)]
            )
            for matching in range(seq_count)
        ]

    def join_back(moved, index):
        moved = jnp.stack([piece[index] for piece in moved])
        pieces = [
            lax.dynamic_index_in_dim(moved, seq_rank ^ code, 0, True) for code in range(seq_count)
        ]
        return jnp.concatenate(pieces, axis=0).reshape(images, patch_rows, width)

    rows = seq_count * piece_rows
    padded = rows + 16

    low_qkv = w_qkv.astype(BF).T
    low_proj = w_proj.astype(BF).T
    unit_width, qkv_width, proj_width = w_up.shape[1], low_qkv.shape[0], low_proj.shape[0]
    column_count = table.shape[1]
    class_count = table.shape[0]
    masks = [level << 1 for level in range(batch_count // 2)]
    offsets = batch_rank ^ jnp.array(masks + [mask ^ 1 for mask in masks], jnp.int32)

    own_mlp = jnp.concatenate([w_up.astype(BF).T, w_down.astype(BF)], axis=0)

    facts = lax.all_gather(jnp.stack([timesteps, labels]), "batch", axis=0)
    all_labels = facts[:, 1].reshape(-1)
    selector = (
        all_labels[:, None] == jnp.arange(class_count, dtype=jnp.int32)[None, :]
    ).astype(BF)
    class_part = dot_nn(selector, table.astype(BF)).astype(BF)
    small = jnp.concatenate([vectors.astype(BF), class_part], axis=0)
    small_rows = -(-small.shape[0] // 16) * 16
    small = lax.dynamic_update_slice(
        jnp.zeros((small_rows, width), BF), small, (0, shard_rank * column_count)
    )

    gap = -(qkv_width + proj_width) % 16
    load = [low_qkv, low_proj] + ([jnp.zeros((gap, width), BF)] if gap else []) + [small]
    line = line_gather(jnp.concatenate(load, axis=0), seq_count)
    former, latter = line_up(line, seq_rank, qkv_width, proj_width)
    former, latter, patches, own_mlp = together(former, latter, patches, own_mlp)

    same_core = [
        [rank * seq_count + at for rank in range(side, batch_count, 2) for at in range(seq_count)]
        for side in (0, 1)
    ]
    all_mlp = lax.all_gather(
        own_mlp, ("batch", "seq"), axis=0, tiled=True, axis_index_groups=same_core
    )
    qkv_rows, proj_rows = qkv_width * seq_count, proj_width * seq_count

    def spread_start(former, latter):
        return (
            {mask: swap(former, mask, batch_count) for mask in bits},
            {mask: swap(latter, mask, batch_count) for mask in bits},
        )

    def spread_rest(former, latter, arrived):
        former_got, latter_got = dict(arrived[0]), dict(arrived[1])
        former_got[0], latter_got[0] = former, latter
        for got, order in ((former_got, bits), (latter_got, bits[::-1])):
            for index, bit in enumerate(order):
                lower = order[:index]
                for mask in [m for m in list(got) if m and not m & bit]:
                    if all(not (mask & other) or other in lower for other in bits):
                        if (mask ^ bit) not in got:
                            got[mask ^ bit] = swap(got[mask], bit, batch_count)
        return former_got, latter_got

    def flat(groups):
        return [group[mask] for group in groups for mask in sorted(group)]

    def unflat(arrays, groups):
        arrays = list(arrays)
        return [{mask: arrays.pop(0) for mask in sorted(group)} for group in groups]

    arrived = spread_start(former, latter)
    moved_patches = send(patches)
    gathered = spread_rest(former, latter, arrived)
    grad_in = (next_grad.astype(F32) + skip_grad.astype(F32)).astype(BF)
    grad_in, *got = together(grad_in, *flat(gathered), *moved_patches)
    moved_patches = jnp.concatenate(got[len(got) - seq_count :], axis=0)
    gathered = unflat(got[: len(got) - seq_count], gathered)
    pieces, moves, small = [], [], 0.0
    unit = former.shape[0]
    rest = qkv_rows - unit
    for group, blocks in enumerate(gathered):
        for mask in masks:
            for side in (0, 1):
                block = swap(blocks[mask], 1, batch_count) if side else blocks[mask]
                target = batch_rank ^ mask ^ side
                number = len(pieces)
                pieces.append(block)
                if group == 0:
                    moves.append((number, 0, unit, 0, target * qkv_rows))
                else:
                    moves.append((number, 0, rest, 0, target * qkv_rows + unit))
                    moves.append((number, rest, proj_rows, 1, target * proj_rows))
                    small = small + block[rest + proj_rows :].astype(F32)
    full_qkv, full_proj = place(pieces, moves, [qkv_rows * batch_count, proj_rows * batch_count])
    vec_values, class_rows = small[:10], small[10 : 10 + images * batch_count]
    home = batch_rank - core + own_core
    own_time = lax.dynamic_index_in_dim(facts[:, 0].reshape(-1), home * images + own_slot, 0, True)
    time_row = time_token(own_time, width)
    class_row = lax.dynamic_index_in_dim(class_rows, home * images + own_slot, 0, True)
    has_extra = sub_rank == 0
    extra_row = jnp.where(core == 0, time_row, class_row) * has_extra.astype(F32)
    row_index = lax.broadcasted_iota(jnp.int32, (padded, 1), 0)
    row_valid = (row_index < rows + has_extra.astype(jnp.int32)).astype(F32)
    first_row = lax.broadcasted_iota(jnp.int32, (16, 1), 0) == 0

    extra_tile = jnp.where(first_row, extra_row, 0.0)
    tokens = jnp.concatenate([moved_patches.astype(F32), extra_tile], axis=0)
    standard_one, inverse_one = standardize(tokens)
    normed = ((standard_one * vec_values[0] + vec_values[1]) * row_valid).astype(BF)
    packed = dot_nt(normed, full_qkv).astype(BF)

    def rotate(values, step, core_bit, back):
        pairs = []
        for rank in range(batch_count):
            for place_z in range(seq_count):
                base, sub = place_z - place_z % chips, place_z % chips
                source = (rank ^ core_bit) * seq_count + base + (sub + step) % chips
                here = rank * seq_count + place_z
                pairs.append((here, source) if back else (source, here))
        return lax.ppermute(values, ("batch", "seq"), pairs)

    peers = [(step, bit) for step in range(chips) for bit in (0, 1)][1:]
    packed, grad_in = together(packed, grad_in)
    moved_grad = send(grad_in)
    own_kv = packed[:, width:]
    other_kv = [rotate(own_kv, step, bit, False) for step, bit in peers]
    valid = jnp.stack(
        [has_extra.astype(jnp.int32)]
        + [((sub_rank + step) % chips == 0).astype(jnp.int32) for step, bit in peers]
    )
    in_extra = (next_extra.astype(F32) + skip_extra.astype(F32)).astype(BF)
    in_extra_other = swap(in_extra, 1, batch_count)
    attended, lse, lse_extra = attention_forward(valid, packed, other_kv)
    attended, in_extra_other, *moved_grad = together(attended, in_extra_other, *moved_grad)
    in_extra = jnp.where(own_core == core, in_extra, in_extra_other)
    in_extra = lax.dynamic_index_in_dim(in_extra, own_slot, 0, False)
    in_extra = lax.dynamic_index_in_dim(in_extra, core, 0, True)
    in_extra = jnp.where(first_row & has_extra, in_extra, jnp.zeros_like(in_extra))
    incoming_low = jnp.concatenate([*moved_grad, in_extra], axis=0)
    incoming = incoming_low.astype(F32)
    other_incoming = swap(incoming_low, 1, batch_count)
    line_order = (seq_rank - jnp.arange(seq_count, dtype=jnp.int32)) % seq_count
    chip_order = (batch_rank ^ jnp.array(masks, jnp.int32)) >> 1
    first_rows = (chip_order[:, None] * seq_count + line_order[None, :]).reshape(-1) * (2 * unit_width)
    all_bias = vec_values[6:].reshape(batch_count // 2, 2, seq_count, unit_width)
    core_bias = lax.dynamic_index_in_dim(all_bias, core, 1, False)
    core_bias = jnp.take(jnp.take(core_bias, chip_order, axis=0), line_order, axis=1).reshape(1, -1)
    middle = tokens + (dot_nt(attended, full_proj) + vec_values[4]) * row_valid
    standard_two, inverse_two = standardize(middle)
    normed_two = ((standard_two * vec_values[2] + vec_values[3]) * row_valid).astype(BF)
    other_normed = swap(normed_two, 1, batch_count)
    out_own, out_other, dn_own, dn_other, grad_up, grad_down, grad_bias = mlp(
        (normed_two, other_normed), (incoming_low, other_incoming), core_bias, all_mlp, first_rows
    )

    def blocks_of(grad):
        parts = grad.reshape(len(masks), -1, width)
        return {mask: parts[index] for index, mask in enumerate(masks)}

    def sum_start(groups):
        moved = []
        for blocks, bit in zip(groups, (bits[-1], bits[0])):
            kept = [mask for mask in masks if not mask & bit]
            moved.append(swap(jnp.concatenate([blocks[mask ^ bit] for mask in kept], axis=0), bit, batch_count))
        return moved

    def sum_add(groups, moved):
        sums = []
        for blocks, arrived, bit in zip(groups, moved, (bits[-1], bits[0])):
            kept = [mask for mask in masks if not mask & bit]
            count = blocks[0].shape[0]
            sums.append(
                {
                    mask: (
                        blocks[mask].astype(F32)
                        + arrived[index * count : (index + 1) * count].astype(F32)
                    ).astype(BF)
                    for index, mask in enumerate(kept)
                }
            )
        return sums

    def sum_rest(groups):
        return [
            plane_reduce(blocks, order, batch_count)
            for blocks, order in zip(groups, (bits[::-1][1:], bits[1:]))
        ]

    def line_blocks(former, latter):
        joined = [values.reshape(seq_count, -1, width) for values in (former, latter)]
        return jnp.concatenate(joined, axis=1)

    mlp_groups = [blocks_of(grad_up), blocks_of(grad_down)]
    moved = sum_start(mlp_groups)
    normed_two_grad = dn_own + swap(dn_other, 1, batch_count).astype(F32)
    middle_grad = incoming + standardize_back(
        normed_two_grad * vec_values[2], standard_two, inverse_two
    )
    middle_low = middle_grad.astype(BF)

    attended_grad = dot_nn(middle_low, full_proj).astype(BF)
    out_arrived = swap(out_other, 1, batch_count)
    backward = attention_backward(valid, packed, other_kv, attended, attended_grad, lse, lse_extra)
    *backward, moved_up, moved_down, out_arrived, middle_low, attended, middle = together(
        *backward, *moved, out_arrived, middle_low, attended, middle
    )
    mlp_groups = sum_add(mlp_groups, [moved_up, moved_down])

    def halves(values):
        cut = values.shape[1] // 32 * 16
        cut = cut if cut else values.shape[1] // 2
        return [
            {mask: part[index] for index, mask in enumerate(masks)}
            for part in (values[:, :cut], values[:, cut:])
        ]

    def next_axis(groups, orders):
        moved = []
        for blocks, order in zip(groups, orders):
            kept = [mask for mask in blocks if not mask & order[0]]
            load = jnp.concatenate([blocks[mask ^ order[0]] for mask in kept], axis=0)
            moved.append(swap(load, order[0], batch_count))
        return moved

    def next_add(groups, orders, moved):
        sums = []
        for blocks, order, arrived in zip(groups, orders, moved):
            kept = [mask for mask in blocks if not mask & order[0]]
            count = blocks[0].shape[0]
            sums.append(
                plane_reduce(
                    {
                        mask: (
                            blocks[mask].astype(F32)
                            + arrived[index * count : (index + 1) * count].astype(F32)
                        ).astype(BF)
                        for index, mask in enumerate(kept)
                    },
                    order[1:],
                    batch_count,
                )
            )
        return sums

    orders = (bits[::-1][1:], bits[1:])
    mlp_moved = next_axis(mlp_groups, orders)
    query_grad, own_dkv = backward[0], backward[1]
    arrived = [rotate(term, step, bit, True) for (step, bit), term in zip(peers, backward[2:])]
    middle_low, attended = beside(middle_low, attended)
    proj_kept, proj_sent = qkv_grad(middle_low, attended, offsets * proj_rows)
    own_dkv, proj_kept, proj_sent, *arrived = together(own_dkv, proj_kept, proj_sent, *arrived)

    proj_arrived = swap(proj_sent, 1, batch_count)
    far_dkv = arrived[0]
    for term in arrived[1:]:
        far_dkv = (far_dkv.astype(F32) + term.astype(F32)).astype(BF)
    packed_grad, kept, sent = packed_grad_of(
        query_grad, own_dkv, far_dkv, normed, offsets * qkv_rows
    )
    packed_grad, kept, sent, proj_kept, proj_arrived, *mlp_moved = together(
        packed_grad, kept, sent, proj_kept, proj_arrived, *mlp_moved
    )

    arrived = swap(sent, 1, batch_count)
    proj_kept, proj_arrived, *mlp_moved = beside(proj_kept, proj_arrived, *mlp_moved)
    mlp_up, mlp_down = next_add(mlp_groups, orders, mlp_moved)
    joined = line_blocks(mlp_up, mlp_down)
    proj_groups = halves((proj_kept.astype(F32) + proj_arrived.astype(F32)).astype(BF))
    joined = [joined[step] for step in range(seq_count)]
    arrived, *joined = together(arrived, *joined)

    groups = halves((kept.astype(F32) + arrived.astype(F32)).astype(BF))
    moved = sum_start(groups)
    near_steps = (1, seq_count - 1)
    far_steps = tuple(range(2, seq_count - 1))
    near_line = [shift(joined[step], -step, seq_count) for step in near_steps]
    first_proj = sum_start(proj_groups)
    packed_grad = beside(packed_grad)
    token_low, norm_sums, extra_grad = first_norm_back(
        packed_grad, full_qkv, standard_one, inverse_one, middle_grad, vec_values[0:1]
    )
    far_line = [joined[step] for step in far_steps]
    moved_up, moved_down, token_low, norm_sums, extra_grad, *got = together(
        *moved, token_low, norm_sums, extra_grad, *near_line, *far_line, *first_proj
    )
    near_line, far_line, first_proj = got[:2], got[2:-2], got[-2:]
    far_line = [shift(part, -step, seq_count) for step, part in zip(far_steps, far_line)]
    bias_parts = jnp.take(grad_bias.reshape(len(masks), seq_count, -1), line_order, axis=1)
    bias_sum = jnp.zeros((batch_count // 2, seq_count, unit_width), F32)
    bias_sum = jnp.take(bias_parts, (batch_rank ^ jnp.arange(0, batch_count, 2)) >> 1, axis=0)
    bias_sum = jnp.where(
        jnp.arange(2, dtype=jnp.int32)[None, :, None, None] == core, bias_sum[:, None], 0.0
    )
    class_slots = jnp.arange(images * batch_count, dtype=jnp.int32) == home * images + own_slot
    holds_class = (core == 1) & has_extra
    class_grad = jnp.where((class_slots & holds_class)[:, None], extra_grad, 0.0)
    vec_grad = jnp.concatenate(
        [
            norm_sums,
            jnp.sum(normed_two_grad * standard_two, axis=0)[None],
            jnp.sum(normed_two_grad, axis=0)[None],
            jnp.sum(middle_low.astype(F32), axis=0)[None],
            jnp.sum(incoming_low.astype(F32), axis=0)[None],
            bias_sum.reshape(4, width),
            class_grad,
        ],
        axis=0,
    )
    sums = next_axis(sum_add(groups, [moved_up, moved_down]), orders)
    proj_groups = sum_add(proj_groups, first_proj)
    proj_up, proj_down = next_axis(proj_groups, orders)
    vec_far = swap(vec_grad, 1, batch_count)
    sums_up, sums_down, vec_far, proj_up, proj_down, *far_line = together(
        *sums, vec_far, proj_up, proj_down, *far_line
    )
    sums = next_add(sum_add(groups, [moved_up, moved_down]), orders, [sums_up, sums_down])
    proj_one, proj_two = next_add(proj_groups, orders, [proj_up, proj_down])
    vec_grad = vec_grad + vec_far

    qkv_parts = from_own(jnp.concatenate(sums, axis=0), seq_count)
    proj_parts = from_own(jnp.concatenate([proj_one, proj_two], axis=0), seq_count)
    late = [jnp.concatenate(parts, axis=0) for parts in zip(qkv_parts, proj_parts)]
    late = [late[0]] + [shift(late[step], -step, seq_count) for step in range(1, seq_count)]
    output = (middle + (out_own + out_arrived.astype(F32) + vec_values[5])).astype(BF)
    for bit in bits:
        vec_grad = vec_grad + swap(vec_grad, bit, batch_count)
    *late, vec_grad, output = together(*late, vec_grad, output)
    total_mlp = functools.reduce(
        jnp.add, [part.astype(F32) for part in (joined[0], *near_line, *far_line)]
    )
    share_up, share_down = total_mlp[:unit_width], total_mlp[unit_width:]

    turned = (mom_qkv.T, mom_proj.T, mom_up.T, mom_down)
    widest = unit_width
    spread = seq_count // 4
    home_plane = [spread * turn for turn in (1, 2, 3, 0)]
    plane_of = {plane: index for index, plane in enumerate(home_plane)}
    held = jnp.take(
        jnp.array([plane_of.get(plane - plane % spread) for plane in range(seq_count)], jnp.int32),
        (seq_rank + jnp.arange(seq_count, dtype=jnp.int32)) % seq_count,
    )

    late = functools.reduce(jnp.add, [part.astype(F32) for part in late])
    shares = (late[:qkv_width], late[qkv_width:], share_up, share_down)
    fresh = [muon_momentum * old + share for old, share in zip(turned, shares)]
    stacked = jnp.stack(
        [jnp.pad(new.astype(BF), ((0, widest - new.shape[0]), (0, 0))) for new in fresh]
    )
    small = lax.dynamic_slice_in_dim(vec_grad, batch_rank * (seq_count * column_count), seq_count * column_count, 1)
    small = jnp.transpose(small.reshape(-1, seq_count, column_count), (1, 0, 2)).reshape(seq_count, -1)
    small = jnp.pad(small, ((0, 0), (0, width - small.shape[1])))
    small_high = small.astype(BF)
    small_low = (small - small_high.astype(F32)).astype(BF)
    y_own = jnp.broadcast_to(output[rows : rows + 1], (seq_count, width))
    small = jnp.pad(jnp.stack([small_high, small_low, y_own], axis=1), ((0, 0), (0, 13), (0, 0)))
    slab = []
    for step in range(seq_count):
        part = lax.dynamic_index_in_dim(stacked, held[step], 0, False)
        rider = lax.dynamic_index_in_dim(small, (seq_rank + step) % seq_count, 0, False)
        part = jnp.concatenate([part, rider], axis=0)
        slab.append(shift(part, step, seq_count) if step else part)
    *slab, token_low, output = together(*slab, token_low, output)
    riders = [part[widest : widest + 3] for part in slab]
    slab = jnp.concatenate([part[:widest] for part in slab], axis=0)
    back_moved = send_back([output[:rows], token_low[:rows]])
    y_line = jnp.stack([part[2:3] for part in riders])
    y_far = swap(y_line, 1, batch_count)

    def plane_sum(kept, sent):
        chip = (kept.astype(F32) + swap(sent, 1, batch_count).astype(F32)).astype(BF)
        total = chip[0].astype(F32)
        for index, mask in enumerate(masks[1:]):
            total = total + swap(chip[index + 1], mask, batch_count).astype(F32)
        total = total.astype(BF)
        near = [total] + [swap(total, mask, batch_count) for mask in masks[1:]]
        return near + [swap(jnp.stack(near), 1, batch_count)]

    unit_offsets = offsets * (packed_rows(width, batch_count) // batch_count)
    slab, kept, sent = first_steps(plane_sum(*gram(slab, unit_offsets)), slab, unit_offsets)
    slab, kept, sent, y_far = together(slab, kept, sent, y_far)
    slab = last_steps(plane_sum(kept, sent), slab, unit_offsets)
    slab, *back_moved = together(slab, *back_moved)
    y_patches, dx_patches = join_back(back_moved, 0), join_back(back_moved, 1)
    back = slab.reshape(seq_count, widest, width)
    back = jnp.stack(
        [back[0]] + [shift(back[step], -step, seq_count) for step in range(1, seq_count)]
    )
    masters = (w_qkv, w_proj, w_up, w_down)
    ratios = (3.0, 1.0, 4.0, 0.25)
    updated = []
    for index in range(4):
        own_part = lax.dynamic_index_in_dim(
            back, (home_plane[index] - seq_rank) % seq_count, 0, False
        )[: fresh[index].shape[0]].astype(F32)
        if index < 3:
            own_part = own_part.T
        factor = math.sqrt(max(1.0, ratios[index]))
        updated.append(
            masters[index] * (1.0 - muon_rate * muon_decay) - muon_rate * factor * own_part
        )

    vec_sum = functools.reduce(
        jnp.add, [part[0].astype(F32) + part[1].astype(F32) for part in riders]
    )
    vec_sum = vec_sum[: vec_grad.shape[0] * column_count].reshape(-1, column_count)
    vec_sum, class_sums = vec_sum[:10], vec_sum[10:]
    chosen = (
        jnp.arange(class_count, dtype=jnp.int32)[:, None] == all_labels[None, :]
    ).astype(F32)
    table_sum = jnp.dot(chosen, class_sums, precision=highest, preferred_element_type=F32)
    y_rows = []
    for slot in range(images):
        turn = (seq_rank - (core * images + slot) * chips) % seq_count
        near = lax.dynamic_index_in_dim(y_line, turn, 0, False)
        far = lax.dynamic_index_in_dim(y_far, turn, 0, False)
        time_y = jnp.where(core == 0, near, far)
        class_y = jnp.where(core == 0, far, near)
        y_rows.append(jnp.concatenate([time_y, class_y], axis=0))
    y_rows = jnp.stack(y_rows)
    vec_new = adam_step(vectors, vec_first, vec_second, vec_sum)
    table_new = adam_step(table, table_first, table_second, table_sum)
    return (
        y_patches,
        y_rows,
        dx_patches,
        *updated,
        fresh[0].T,
        fresh[1].T,
        fresh[2].T,
        fresh[3],
        *vec_new,
        *table_new,
    )


def solution(mesh):
    tokens = P("batch", "seq", None)
    images = P("batch")
    extras = P("batch", None, None)
    columns = P(None, ("batch", "seq"))
    rows = P(("batch", "seq"), None)
    return jax.shard_map(
        body,
        mesh=mesh,
        in_specs=(
            tokens, images, images, tokens, tokens, extras, extras,
            columns, columns, columns, rows, columns, columns, columns, rows,
            columns, columns, columns, columns, columns, columns,
        ),
        out_specs=(
            tokens, extras, tokens, columns, columns, columns, rows,
            columns, columns, columns, rows, columns, columns, columns, columns, columns, columns,
        ),
        check_vma=False,
    )
```

```python
import functools
import math

import jax
import jax.numpy as jnp
from jax import lax
from jax.experimental import pallas as pl
from jax.experimental.pallas import tpu as pltpu
from jax.sharding import PartitionSpec as P

HEADS = 16
STEP = 10
FIRST_STEPS = 3
LAST_STEPS = 2

norm_eps = 1e-05
poly_first = 3.4445
poly_second = -4.775
poly_third = 2.0315
muon_momentum = 0.95
muon_rate = 1.5
muon_decay = 0.01
beta_one = 0.9
beta_two = 0.999
adam_rate = 1.0
adam_eps = 1e-08
highest = lax.Precision.HIGHEST
BF = jnp.bfloat16
F32 = jnp.float32
LOG2E = math.log2(math.e)
MIB = 1024 * 1024


def dot_nt(former, latter):
    return lax.dot_general(former, latter, (((1,), (1,)), ((), ())), preferred_element_type=F32)


def dot_nn(former, latter):
    return lax.dot_general(former, latter, (((1,), (0,)), ((), ())), preferred_element_type=F32)


def dot_tn(former, latter):
    return lax.dot_general(former, latter, (((0,), (0,)), ((), ())), preferred_element_type=F32)


def in_vmem(count):
    return [pl.BlockSpec(memory_space=pltpu.VMEM)] * count


def shape_of(shape, dtype):
    return jax.ShapeDtypeStruct(shape, dtype)


def head_window(head, size, width):
    start = jnp.minimum((head * size) // 128, (width - 256) // 128) * 128
    return pl.multiple_of(start, 128), head * size - start


def attention_forward_kernel(groups, valid_ref, own_ref, *refs):
    held, (o_ref, lse_ref, lsex_ref, acc) = refs[:groups], refs[groups:]
    rows = own_ref.shape[0] - 16
    width = own_ref.shape[1]
    size = width // HEADS
    factor = size**-0.5 * LOG2E
    tables = [(ref, 0, width) for ref in held]
    parts = []
    for group, (ref, key_at, value_at) in enumerate(tables):
        parts.append((ref, pl.ds(0, rows), key_at, value_at, None))
        parts.append((ref, pl.ds(rows, 16), key_at, value_at, valid_ref[group]))
    acc[...] = jnp.zeros_like(acc)
    tile_row = lax.broadcasted_iota(jnp.int32, (16, rows), 0)

    def one_head(head, carry):
        start, offset = head_window(head, size, width)
        lane = lax.broadcasted_iota(jnp.int32, (rows, 256), 1)
        mask = (lane >= offset) & (lane < offset + size)
        query = jnp.where(mask, own_ref[:rows, pl.ds(start, 256)], jnp.zeros((), BF))
        scores = []
        for ref, span, key_at, value_at, valid in parts:
            score = dot_nt(ref[span, pl.ds(pl.multiple_of(key_at + start, 128), 256)], query)
            if valid is not None:
                score = jnp.where(tile_row < valid, score, -1e30)
            scores.append(score)
        largest = functools.reduce(
            jnp.maximum, [jnp.max(score, axis=0, keepdims=True) for score in scores]
        )
        largest = largest * factor
        total = jnp.zeros((1, rows), F32)
        out = jnp.zeros((256, rows), F32)
        for score, (ref, span, key_at, value_at, valid) in zip(scores, parts):
            power = jnp.exp2(score * factor - largest)
            total = total + jnp.sum(power, axis=0, keepdims=True)
            values = ref[span, pl.ds(pl.multiple_of(value_at + start, 128), 256)]
            out = out + dot_tn(values, power.astype(BF))
        out = (out * (1.0 / total)).T
        acc[:, pl.ds(start, 256)] += jnp.where(mask, out, 0.0)
        lse_ref[pl.ds(head, 1), :] = largest + jnp.log2(total)
        return carry

    lax.fori_loop(0, HEADS, one_head, 0, unroll=4)
    o_ref[:rows, :] = acc[...].astype(BF)
    head_row = lax.broadcasted_iota(jnp.int32, (HEADS, width), 0)
    lane = lax.broadcasted_iota(jnp.int32, (HEADS, width), 1)
    diagonal = (lane >= head_row * size) & (lane < head_row * size + size)
    extra = jnp.broadcast_to(own_ref[rows : rows + 16, :width].astype(F32)[0:1], (HEADS, width))
    extra = jnp.where(diagonal, extra, 0.0).astype(BF)
    tile_lane = lax.broadcasted_iota(jnp.int32, (HEADS, 16), 1)
    scores = []
    for ref, span, key_at, value_at, valid in parts:
        score = dot_nt(extra, ref[span, key_at : key_at + width])
        if valid is not None:
            score = jnp.where(tile_lane < valid, score, -1e30)
        scores.append(score)
    largest = functools.reduce(
        jnp.maximum, [jnp.max(score, axis=1, keepdims=True) for score in scores]
    )
    largest = largest * factor
    total = jnp.zeros((HEADS, 1), F32)
    out = jnp.zeros((HEADS, width), F32)
    for score, (ref, span, key_at, value_at, valid) in zip(scores, parts):
        power = jnp.exp2(score * factor - largest)
        total = total + jnp.sum(power, axis=1, keepdims=True)
        out = out + dot_nn(power.astype(BF), ref[span, value_at : value_at + width])
    out = jnp.sum(jnp.where(diagonal, out * (1.0 / total), 0.0), axis=0, keepdims=True)
    first = lax.broadcasted_iota(jnp.int32, (16, width), 0) < valid_ref[0]
    o_ref[rows:, :] = jnp.where(first, jnp.broadcast_to(out, (16, width)), 0.0).astype(BF)
    lsex_ref[...] = jnp.broadcast_to(largest + jnp.log2(total), (HEADS, 128))


def attention_forward(valid, query, held):
    padded, width = query.shape
    rows, groups = padded - 16, len(held)
    pairs = rows * groups * rows
    return pl.pallas_call(
        functools.partial(attention_forward_kernel, groups),
        out_shape=[
            shape_of((padded, width), BF),
            shape_of((HEADS, rows), F32),
            shape_of((HEADS, 128), F32),
        ],
        in_specs=[pl.BlockSpec(memory_space=pltpu.SMEM)] + in_vmem(1 + groups),
        out_specs=in_vmem(3),
        scratch_shapes=[pltpu.VMEM((rows, width), F32)],
        compiler_params=pltpu.CompilerParams(vmem_limit_bytes=60 * MIB),
        cost_estimate=pl.CostEstimate(
            flops=16 * pairs * width,
            bytes_accessed=groups * padded * width * 6,
            transcendentals=HEADS * pairs,
        ),
        name="attention_forward",
    )(valid, query, *held)


def attention_backward_kernel(groups, valid_ref, own_ref, *refs):
    held, refs = refs[:groups], refs[groups:]
    o_ref, do_ref, lse_ref, lsex_ref = refs[:4]
    dq_ref, dkv_refs, refs = refs[4], refs[5 : 5 + groups], refs[5 + groups :]
    dq_acc, dk_acc, dv_acc, delta = refs
    rows = own_ref.shape[0] - 16
    padded = rows + 16
    width = own_ref.shape[1]
    size = width // HEADS
    scale = size**-0.5
    factor = scale * LOG2E
    tables = [(ref, 0, width) for ref in held]
    parts = []
    for group, (ref, key_at, value_at) in enumerate(tables):
        parts.append((ref, 0, rows, key_at, value_at, group, None))
        parts.append((ref, rows, 16, key_at, value_at, group, valid_ref[group]))
    head_row = lax.broadcasted_iota(jnp.int32, (HEADS, width), 0)
    lane = lax.broadcasted_iota(jnp.int32, (HEADS, width), 1)
    diagonal = (lane >= head_row * size) & (lane < head_row * size + size)
    ones = jnp.where(diagonal, 1.0, 0.0).astype(BF)
    product = do_ref[:rows, :].astype(F32) * o_ref[:rows, :].astype(F32)
    upper = product.astype(BF)
    lower = (product - upper.astype(F32)).astype(BF)
    delta[...] = dot_nt(ones, upper) + dot_nt(ones, lower)
    extra = jnp.broadcast_to(own_ref[rows:padded, :width].astype(F32)[0:1], (HEADS, width))
    extra = jnp.where(diagonal, extra, 0.0).astype(BF)
    extra_do = jnp.broadcast_to(do_ref[rows:padded, :].astype(F32)[0:1], (HEADS, width))
    extra_do = jnp.where(diagonal, extra_do, 0.0)
    extra_o = o_ref[rows:padded, :].astype(F32)[0:1]
    extra_delta = jnp.sum(extra_do * extra_o, axis=1, keepdims=True)
    extra_do = extra_do.astype(BF)
    extra_lse = lsex_ref[:, 0:1]
    tile_lane = lax.broadcasted_iota(jnp.int32, (HEADS, 16), 1)
    extra_dq = jnp.zeros((HEADS, width), F32)
    for ref, at, count, key_at, value_at, group, valid in parts:
        keys = ref[at : at + count, key_at : key_at + width]
        values = ref[at : at + count, value_at : value_at + width]
        prob = jnp.exp2(dot_nt(extra, keys) * factor - extra_lse)
        if valid is not None:
            prob = jnp.where(tile_lane < valid, prob, 0.0)
        score_grad = (prob * (dot_nt(extra_do, values) - extra_delta)).astype(BF)
        extra_dq = extra_dq + dot_nn(score_grad, keys)
        dk_acc[group, at : at + count, :] = dot_tn(score_grad, extra)
        dv_acc[group, at : at + count, :] = dot_tn(prob.astype(BF), extra_do)
    extra_dq = jnp.sum(jnp.where(diagonal, extra_dq, 0.0), axis=0, keepdims=True) * scale
    first = lax.broadcasted_iota(jnp.int32, (16, width), 0) < valid_ref[0]
    dq_ref[rows:, :] = jnp.where(first, jnp.broadcast_to(extra_dq, (16, width)), 0.0).astype(BF)
    dq_acc[...] = jnp.zeros_like(dq_acc)
    tile_row = lax.broadcasted_iota(jnp.int32, (16, rows), 0)

    def one_head(head, carry):
        start, offset = head_window(head, size, width)
        window = pl.ds(start, 256)
        lanes = lax.broadcasted_iota(jnp.int32, (rows, 256), 1)
        mask = (lanes >= offset) & (lanes < offset + size)
        zero = jnp.zeros((), BF)
        query = jnp.where(mask, own_ref[:rows, window], zero)
        out_grad = jnp.where(mask, do_ref[:rows, window], zero)
        lse = lse_ref[pl.ds(head, 1), :]
        row_delta = delta[pl.ds(head, 1), :]
        query_grad = jnp.zeros((256, rows), F32)
        for ref, at, count, key_at, value_at, group, valid in parts:
            keys = ref[at : at + count, pl.ds(pl.multiple_of(key_at + start, 128), 256)]
            values = ref[at : at + count, pl.ds(pl.multiple_of(value_at + start, 128), 256)]
            prob = jnp.exp2(dot_nt(keys, query) * factor - lse)
            if valid is not None:
                prob = jnp.where(tile_row < valid, prob, 0.0)
            score_grad = (prob * (dot_nt(values, out_grad) - row_delta)).astype(BF)
            dv_acc[group, at : at + count, window] += dot_nn(prob.astype(BF), out_grad)
            dk_acc[group, at : at + count, window] += dot_nn(score_grad, query)
            query_grad = query_grad + dot_tn(keys, score_grad)
        dq_acc[:, window] += jnp.where(mask, query_grad.T, 0.0)
        return carry

    lax.fori_loop(0, HEADS, one_head, 0, unroll=4)
    dq_ref[:rows, :] = (dq_acc[...] * scale).astype(BF)
    for group, dkv_ref in enumerate(dkv_refs):
        dkv_ref[:, :width] = (dk_acc[group] * scale).astype(dkv_ref.dtype)
        dkv_ref[:, width:] = dv_acc[group].astype(dkv_ref.dtype)


def attention_backward(valid, query, held, attended, attended_grad, lse, lse_extra):
    padded, width = query.shape
    rows, groups = padded - 16, len(held)
    pairs = rows * groups * rows
    return pl.pallas_call(
        functools.partial(attention_backward_kernel, groups),
        out_shape=[shape_of((padded, width), BF)]
        + [shape_of((padded, 2 * width), BF) for _ in range(groups)],
        in_specs=[pl.BlockSpec(memory_space=pltpu.SMEM)] + in_vmem(groups + 5),
        out_specs=in_vmem(1 + groups),
        scratch_shapes=[
            pltpu.VMEM((rows, width), F32),
            pltpu.VMEM((groups, padded, width), F32),
            pltpu.VMEM((groups, padded, width), F32),
            pltpu.VMEM((HEADS, rows), F32),
        ],
        compiler_params=pltpu.CompilerParams(vmem_limit_bytes=60 * MIB),
        cost_estimate=pl.CostEstimate(
            flops=36 * pairs * width,
            bytes_accessed=2 * groups * padded * width * 6,
            transcendentals=HEADS * pairs,
        ),
        name="attention_backward",
    )(valid, query, *held, attended, attended_grad, lse, lse_extra)


def mlp_kernel(
    units, unit, block, first_ref, bias_ref, rows_ref, n_own, n_other, dm_own, dm_other,
    out_own, out_other, dn_own, dn_other, gup_ref, gdown_ref, gbias_ref,
    out_acc, dn_acc, up_all, down_all, n_ref, dm_ref, sems,
):
    step = pl.program_id(0)

    @pl.when(step == 0)
    def _():
        copies = []
        for index in range(units):
            start = pl.multiple_of(first_ref[index], 16)
            for which, joined in enumerate((up_all, down_all)):
                copy = pltpu.make_async_copy(
                    rows_ref.at[pl.ds(start + which * unit, unit)],
                    joined.at[pl.ds(index * unit, unit)],
                    sems.at[2 * index + which],
                )
                copy.start()
                copies.append(copy)
        half = out_own.shape[0]
        for index, (source, joined, at) in enumerate(
            ((n_own, n_ref, 0), (n_other, n_ref, half), (dm_own, dm_ref, 0), (dm_other, dm_ref, half))
        ):
            copy = pltpu.make_async_copy(
                source, joined.at[pl.ds(at, half)], sems.at[2 * units + index]
            )
            copy.start()
            copies.append(copy)
        out_acc[...] = jnp.zeros_like(out_acc)
        dn_acc[...] = jnp.zeros_like(dn_acc)
        for copy in copies:
            copy.wait()

    span = pl.ds(pl.multiple_of(step * block, block), block)
    normed, dm, up, down = n_ref[...], dm_ref[...], up_all[span, :], down_all[span, :]
    hidden = dot_nt(normed, up) + bias_ref[...]
    below = 0.5 * (1.0 + lax.erf(hidden * (2.0**-0.5)))
    activated = (hidden * below).astype(BF)
    out_acc[...] += dot_nn(activated, down)
    gdown_ref[...] = dot_tn(activated, dm).astype(BF)
    slope = below + hidden * (jnp.exp(-0.5 * hidden * hidden) * (1.0 / math.sqrt(2 * math.pi)))
    hidden_grad = (dot_nt(dm, down) * slope).astype(BF)
    dn_acc[...] += dot_nn(hidden_grad, up)
    gup_ref[...] = dot_tn(hidden_grad, normed).astype(BF)
    gbias_ref[...] = jnp.sum(hidden_grad.astype(F32), axis=0, keepdims=True)
    half = out_own.shape[0]

    @pl.when(step == pl.num_programs(0) - 1)
    def _():
        out_own[...] = out_acc[:half, :]
        out_other[...] = out_acc[half:, :].astype(BF)
        dn_own[...] = dn_acc[:half, :]
        dn_other[...] = dn_acc[half:, :].astype(BF)


def mlp(normed, dm, bias, gathered, first_rows, block=768):
    half, width = normed[0].shape
    hidden = bias.shape[1]
    rows = 2 * half
    units = first_rows.shape[0]
    unit = hidden // units
    if unit % 16:
        wide = -(-unit // 16) * 16
        fill = ((0, 0), (0, wide - unit), (0, 0))
        gathered = jnp.pad(gathered.reshape(2 * units, unit, width), fill).reshape(-1, width)
        bias = jnp.pad(bias.reshape(units, unit), fill[:2]).reshape(1, -1)
        *outs, grad_up, grad_down, grad_bias = mlp(
            normed, dm, bias, gathered, first_rows // unit * wide, block
        )
        grads = [
            grad.reshape(units, wide, width)[:, :unit].reshape(hidden, width)
            for grad in (grad_up, grad_down)
        ]
        return *outs, *grads, grad_bias.reshape(units, wide)[:, :unit].reshape(1, hidden)
    whole = lambda step: (0, 0)
    part = lambda step: (step, 0)
    return pl.pallas_call(
        functools.partial(mlp_kernel, units, unit, block),
        grid=(hidden // block,),
        out_shape=[shape_of((half, width), dtype) for dtype in (F32, BF, F32, BF)]
        + [shape_of((hidden, width), BF)] * 2
        + [shape_of((1, hidden), F32)],
        in_specs=[
            pl.BlockSpec(memory_space=pltpu.SMEM),
            pl.BlockSpec((1, block), lambda step: (0, step)),
        ]
        + [pl.BlockSpec(memory_space=pl.ANY)] * 5,
        out_specs=[pl.BlockSpec((half, width), whole)] * 4
        + [pl.BlockSpec((block, width), part)] * 2
        + [pl.BlockSpec((1, block), lambda step: (0, step))],
        scratch_shapes=[pltpu.VMEM((rows, width), F32)] * 2
        + [pltpu.VMEM((hidden, width), BF)] * 2
        + [pltpu.VMEM((rows, width), BF)] * 2
        + [pltpu.SemaphoreType.DMA((2 * units + 4,))],
        compiler_params=pltpu.CompilerParams(vmem_limit_bytes=62 * MIB),
        cost_estimate=pl.CostEstimate(
            flops=12 * rows * width * hidden,
            bytes_accessed=8 * hidden * width + 16 * rows * width,
            transcendentals=2 * rows * hidden,
        ),
        name="mlp",
    )(first_rows.astype(jnp.int32), bias, gathered, *normed, *dm)


def column_blocks(width):
    return [(at, min(256, width - at)) for at in range(0, width, 256)]


def packed_rows(width, units):
    rows = sum((at + w) * w // 256 for at, w in column_blocks(width))
    return -(-rows // (16 * units)) * (16 * units)


def gram_into(slab, slab_t, out_ref):
    row = 0
    for at, w in column_blocks(slab.shape[1]):
        high = at + w
        value = dot_nn(slab_t[0:high, :], slab[:, at:high]).astype(BF)
        if w == 256:
            out_ref[row : row + high, :] = value
            row += high
        else:
            half = high // 2
            out_ref[row : row + half, 0:128] = value[:half]
            out_ref[row : row + half, 128:256] = value[half:]
            row += half
    out_ref[row:, :] = jnp.zeros((out_ref.shape[0] - row, 256), BF)


def unpack(packed, width, store):
    row = 0
    for at, w in column_blocks(width):
        high = at + w
        if w == 256:
            value = packed[row : row + high, :]
            row += high
        else:
            half = high // 2
            value = jnp.concatenate(
                [packed[row : row + half, 0:128], packed[row : row + half, 128:256]], axis=0
            )
            row += half
        store(at, w, value.astype(F32))


def store_both(ref, at, w, value):
    ref[0 : at + w, at : at + w] = value.astype(BF)
    if at:
        ref[at : at + w, 0:at] = value[0:at].T.astype(BF)


def on_diagonal(at, w):
    rows = lax.broadcasted_iota(jnp.int32, (at + w, w), 0)
    return rows == lax.broadcasted_iota(jnp.int32, (at + w, w), 1) + at


def symmetric_product(former, latter, width, done):
    for at, w in column_blocks(width):
        done(at, w, dot_nn(former[0 : at + w, :], latter[:, at : at + w]))


def deal(packed, offset_ref, kept, sent, sems):
    copies = []
    count, unit = kept.shape[0], kept.shape[1]
    for index in range(2 * count):
        start = pl.multiple_of(offset_ref[index], 16)
        out = kept if index < count else sent
        copy = pltpu.make_async_copy(
            packed.at[pl.ds(start, unit)], out.at[index % count], sems.at[index]
        )
        copy.start()
        copies.append(copy)
    for copy in copies:
        copy.wait()


def collect(near, far, offset_ref, packed, sems):
    copies = []
    count, unit = far.shape[0], far.shape[1]
    for index in range(2 * count):
        start = pl.multiple_of(offset_ref[index], 16)
        source = near[index] if index < count else far.at[index - count]
        copy = pltpu.make_async_copy(source, packed.at[pl.ds(start, unit)], sems.at[index])
        copy.start()
        copies.append(copy)
    for copy in copies:
        copy.wait()


def gram_kernel(offset_ref, slab_ref, kept, sent, slab_t, packed, sems):
    slab_t[...] = slab_ref[...].T
    gram_into(slab_ref, slab_t, packed)
    deal(packed, offset_ref, kept, sent, sems)


SMEM = pl.BlockSpec(memory_space=pltpu.SMEM)
ANYWHERE = pl.BlockSpec(memory_space=pl.ANY)


def gram(slab, offsets):
    rows, width = slab.shape
    units = offsets.shape[0]
    size = packed_rows(width, units)
    part = shape_of((units // 2, size // units, 256), BF)
    return pl.pallas_call(
        gram_kernel,
        out_shape=[part, part],
        in_specs=[SMEM] + in_vmem(1),
        out_specs=[ANYWHERE] * 2,
        scratch_shapes=[
            pltpu.VMEM((width, rows), BF),
            pltpu.VMEM((size, 256), BF),
            pltpu.SemaphoreType.DMA((units,)),
        ],
        compiler_params=pltpu.CompilerParams(vmem_limit_bytes=50 * MIB),
        cost_estimate=pl.CostEstimate(
            flops=2 * rows * width * width,
            bytes_accessed=2 * rows * width + 2 * width * width,
            transcendentals=0,
        ),
        name="gram",
    )(offsets, slab)


def first_steps_kernel(count, offset_ref, slab_ref, *refs):
    pairs, refs = refs[:count], refs[count:]
    slab_out, kept, sent = refs[:3]
    gram_f, mix_f, prod_f, poly_f, gram_b, mix_b, prod_b, poly_b, slab_t, packed, sems = refs[3:]
    width = slab_ref.shape[1]
    collect(pairs[:-1], pairs[-1], offset_ref, packed, sems)
    square = [jnp.zeros((1, 1), F32)]

    def add_diagonal(at, w, value):
        here = jnp.where(on_diagonal(at, w), value, 0.0)
        square[0] = square[0] + jnp.sum(here, keepdims=True).reshape(1, 1)

    unpack(packed, width, add_diagonal)
    inverse = 1.0 / (jnp.sqrt(square[0]) + 1e-07)

    def start(at, w, value):
        value = value * inverse * inverse
        gram_f[0 : at + w, at : at + w] = value
        store_both(gram_b, at, w, value)

    unpack(packed, width, start)
    lead = 1.0
    for step in range(FIRST_STEPS):
        def make_mix(at, w, value):
            span = (slice(0, at + w), slice(at, at + w))
            mix = poly_second * gram_f[span] + poly_third * value
            mix_f[span] = mix
            store_both(mix_b, at, w, mix)
            if step == 0:
                poly_f[span] = mix
                store_both(poly_b, at, w, mix)

        symmetric_product(gram_b, gram_b, width, make_mix)
        if step > 0:

            def join(at, w, value):
                span = (slice(0, at + w), slice(at, at + w))
                poly = poly_first * poly_f[span] + lead * mix_f[span] + value
                poly_f[span] = poly
                store_both(prod_b, at, w, poly)

            symmetric_product(mix_b, poly_b, width, join)
            poly_b, prod_b = prod_b, poly_b
        lead = lead * poly_first
        if step < FIRST_STEPS - 1:

            def keep(at, w, value):
                prod_f[0 : at + w, at : at + w] = value
                store_both(prod_b, at, w, value)

            symmetric_product(gram_b, mix_b, width, keep)

            def next_gram(at, w, value):
                span = (slice(0, at + w), slice(at, at + w))
                new = poly_first**2 * gram_f[span] + 2 * poly_first * prod_f[span] + value
                gram_f[span] = new
                store_both(gram_b, at, w, new)

            symmetric_product(prod_b, mix_b, width, next_gram)
    slab = slab_ref[...]
    moved = ((lead * slab.astype(F32) + dot_nn(slab, poly_b[...])) * inverse).astype(BF)
    slab_out[...] = moved
    slab_t[...] = moved.T
    gram_into(moved, slab_t, packed)
    deal(packed, offset_ref, kept, sent, sems)


def first_steps(pairs, slab, offsets):
    rows, width = slab.shape
    square = (width, width)
    units = offsets.shape[0]
    size = packed_rows(width, units)
    part = shape_of((units // 2, size // units, 256), BF)
    return pl.pallas_call(
        functools.partial(first_steps_kernel, len(pairs)),
        out_shape=[shape_of((rows, width), BF), part, part],
        in_specs=[SMEM] + in_vmem(1) + [ANYWHERE] * len(pairs),
        out_specs=in_vmem(1) + [ANYWHERE] * 2,
        scratch_shapes=[pltpu.VMEM(square, F32)] * 4
        + [pltpu.VMEM(square, BF)] * 4
        + [pltpu.VMEM((width, rows), BF), pltpu.VMEM((size, 256), BF)]
        + [pltpu.SemaphoreType.DMA((units,))],
        compiler_params=pltpu.CompilerParams(vmem_limit_bytes=60 * MIB),
        cost_estimate=pl.CostEstimate(
            flops=18 * width**3,
            bytes_accessed=4 * rows * width + 4 * width * width,
            transcendentals=0,
        ),
        name="first_steps",
    )(offsets, slab, *pairs)


def last_steps_kernel(count, offset_ref, slab_ref, *refs):
    pairs, refs = refs[:count], refs[count:]
    slab_out, gram_b, poly_b, prod_b, join_b, packed, sems = refs
    width = slab_ref.shape[1]
    collect(pairs[:-1], pairs[-1], offset_ref, packed, sems)
    unpack(packed, width, lambda at, w, value: store_both(gram_b, at, w, value))
    for step in range(LAST_STEPS):

        def make_poly(at, w, value):
            held = gram_b[0 : at + w, at : at + w].astype(F32)
            poly = poly_second * held + poly_third * value
            poly = poly + jnp.where(on_diagonal(at, w), poly_first, 0.0)
            store_both(poly_b, at, w, poly)
            if step == 0:
                store_both(join_b, at, w, poly)

        symmetric_product(gram_b, gram_b, width, make_poly)
        if step > 0:
            symmetric_product(
                poly_b, join_b, width, lambda at, w, value: store_both(prod_b, at, w, value)
            )
            join_b, prod_b = prod_b, join_b
        if step < LAST_STEPS - 1:
            symmetric_product(
                gram_b, poly_b, width, lambda at, w, value: store_both(prod_b, at, w, value)
            )
            symmetric_product(
                prod_b, poly_b, width, lambda at, w, value: store_both(gram_b, at, w, value)
            )
    slab_out[...] = dot_nn(slab_ref[...], join_b[...]).astype(BF)


def last_steps(pairs, slab, offsets):
    rows, width = slab.shape
    units = offsets.shape[0]
    size = packed_rows(width, units)
    return pl.pallas_call(
        functools.partial(last_steps_kernel, len(pairs)),
        out_shape=shape_of((rows, width), BF),
        in_specs=[SMEM] + in_vmem(1) + [ANYWHERE] * len(pairs),
        out_specs=in_vmem(1)[0],
        scratch_shapes=[pltpu.VMEM((width, width), BF)] * 4
        + [pltpu.VMEM((size, 256), BF), pltpu.SemaphoreType.DMA((units,))],
        compiler_params=pltpu.CompilerParams(vmem_limit_bytes=60 * MIB),
        cost_estimate=pl.CostEstimate(
            flops=10 * width**3,
            bytes_accessed=4 * rows * width + 2 * width * width,
            transcendentals=0,
        ),
        name="last_steps",
    )(offsets, slab, *pairs)


def line_up_kernel(counts, place_ref, *refs):
    line, qkv, proj, small_at, folds, columns = counts
    blocks, (former, latter, held, joined) = refs[:line], refs[line:]
    for step, block in enumerate(blocks):
        held[step] = block[...]
    total = None
    for index in range(line):
        step = lax.rem(place_ref[0] - index + line, line)
        value = held[step].astype(F32)
        joined[index * qkv : (index + 1) * qkv, :] = value[:qkv]
        at = line * qkv + index * proj
        joined[at : at + proj, :] = value[qkv : qkv + proj]
        small = jnp.concatenate(
            [value[small_at:, 128 * fold : 128 * (fold + 1)] for fold in range(folds)], axis=0
        )
        small = jnp.concatenate(
            [small, jnp.zeros((16 * folds, value.shape[1] - 128), F32)], axis=1
        )
        small = pltpu.roll(small, (place_ref[1] * line + index) * columns, 1)
        total = small if total is None else total + small
    half = former.shape[0]
    rest = line * (qkv + proj) - half
    former[...] = joined[:half, :].astype(BF)
    latter[:rest, :] = joined[half:, :].astype(BF)
    latter[rest:, :] = total.astype(BF)


def line_up(blocks, place, qkv, proj, folds, columns):
    line = len(blocks)
    rows, width = blocks[0].shape
    small_at = -(-(qkv + proj) // 16) * 16
    half = line * (qkv + proj) // 2
    return pl.pallas_call(
        functools.partial(line_up_kernel, (line, qkv, proj, small_at, folds, columns)),
        out_shape=[
            shape_of((half, width), BF),
            shape_of((line * (qkv + proj) - half + 16 * folds, width), BF),
        ],
        in_specs=[SMEM] + in_vmem(line),
        out_specs=in_vmem(2),
        scratch_shapes=[
            pltpu.VMEM((line, rows, width), BF),
            pltpu.VMEM((line * (qkv + proj), width), F32),
        ],
        compiler_params=pltpu.CompilerParams(vmem_limit_bytes=40 * MIB),
        name="line_up",
    )(place, *blocks)


def packed_grad_kernel(offset_ref, query_ref, own_ref, arrived_ref, other_ref, packed, kept, sent, grad, sems):
    width = query_ref.shape[1]
    packed[:, :width] = query_ref[...]
    total = own_ref[...].astype(F32) + arrived_ref[...].astype(F32)
    packed[:, width:] = total.astype(BF)
    qkv_grad_kernel(offset_ref, packed, other_ref, kept, sent, grad, sems)


def packed_grad_of(query_grad, own, arrived, other_side, offsets):
    rows, width = query_grad.shape
    long = 3 * width
    units = offsets.shape[0]
    unit = long // units
    if unit % 16:
        total = (own.astype(F32) + arrived.astype(F32)).astype(BF)
        packed = jnp.concatenate([query_grad, total], axis=1)
        return packed, *qkv_grad(packed, other_side, offsets)
    part = shape_of((units // 2, unit, width), BF)
    return pl.pallas_call(
        packed_grad_kernel,
        out_shape=[shape_of((rows, long), BF), part, part],
        in_specs=[SMEM] + in_vmem(4),
        out_specs=in_vmem(1) + [ANYWHERE] * 2,
        scratch_shapes=[pltpu.VMEM((long, width), BF), pltpu.SemaphoreType.DMA((units,))],
        compiler_params=pltpu.CompilerParams(vmem_limit_bytes=50 * MIB),
        cost_estimate=pl.CostEstimate(
            flops=2 * rows * long * width,
            bytes_accessed=2 * rows * (2 * long + width) + 2 * long * width,
            transcendentals=0,
        ),
        name="packed_grad",
    )(offsets, query_grad, own, arrived, other_side)


def first_norm_kernel(packed_ref, weight_ref, standard_ref, inverse_ref, after_ref, gain_ref, low_ref, sums_ref):
    grad = dot_nn(packed_ref[...], weight_ref[...])
    standard = standard_ref[...]
    sums_ref[...] = jnp.zeros_like(sums_ref)
    sums_ref[0:1, :] = jnp.sum(grad * standard, axis=0, keepdims=True)
    sums_ref[1:2, :] = jnp.sum(grad, axis=0, keepdims=True)
    scaled = grad * gain_ref[...]
    average = jnp.mean(scaled, axis=1, keepdims=True)
    along = jnp.mean(scaled * standard, axis=1, keepdims=True)
    token = after_ref[...] + inverse_ref[...] * (scaled - average - standard * along)
    low_ref[...] = token.astype(BF)
    rows = token.shape[0] - 16
    sums_ref[8:16, :] = token[rows : rows + 8, :]


def first_norm_back(packed_grad, weight, standard, inverse, after, gain):
    rows, width = standard.shape
    long = weight.shape[0]
    low, sums = pl.pallas_call(
        first_norm_kernel,
        out_shape=[shape_of((rows, width), BF), shape_of((16, width), F32)],
        in_specs=in_vmem(6),
        out_specs=in_vmem(2),
        compiler_params=pltpu.CompilerParams(vmem_limit_bytes=60 * MIB),
        cost_estimate=pl.CostEstimate(
            flops=2 * rows * long * width,
            bytes_accessed=2 * rows * (long + 5 * width) + 2 * long * width,
            transcendentals=0,
        ),
        name="first_norm_back",
    )(packed_grad, weight, standard, inverse, after, gain)
    return low, sums[0:2], sums[8:9]


def qkv_grad_kernel(offset_ref, long_ref, other_ref, kept, sent, grad, sems):
    other = other_ref[...]
    for at, w in [(at, 384) for at in range(0, grad.shape[0], 384)]:
        grad[at : at + w, :] = dot_tn(long_ref[:, at : at + w], other).astype(BF)
    deal(grad, offset_ref, kept, sent, sems)


def qkv_grad(long_side, other_side, offsets):
    rows, long = long_side.shape
    width = other_side.shape[1]
    units = offsets.shape[0]
    unit = long // units
    if unit % 16:
        grad = dot_tn(long_side, other_side).astype(BF).reshape(units, unit, width)
        parts = [
            lax.dynamic_index_in_dim(grad, offsets[index] // unit, 0, False)
            for index in range(units)
        ]
        return jnp.stack(parts[: units // 2]), jnp.stack(parts[units // 2 :])
    part = shape_of((units // 2, unit, width), BF)
    return pl.pallas_call(
        qkv_grad_kernel,
        out_shape=[part, part],
        in_specs=[SMEM] + in_vmem(2),
        out_specs=[ANYWHERE] * 2,
        scratch_shapes=[pltpu.VMEM((long, width), BF), pltpu.SemaphoreType.DMA((units,))],
        compiler_params=pltpu.CompilerParams(vmem_limit_bytes=50 * MIB),
        cost_estimate=pl.CostEstimate(
            flops=2 * rows * long * width,
            bytes_accessed=2 * rows * (long + width) + 2 * long * width,
            transcendentals=0,
        ),
        name="qkv_grad",
    )(offsets, long_side, other_side)


def place_kernel(moves, count, outputs, offset_ref, *refs):
    pieces, outs, sems = refs[:count], refs[count : count + outputs], refs[count + outputs]
    copies = []
    for index, (piece, at, rows, out, _) in enumerate(moves):
        start = pl.multiple_of(offset_ref[index], 16)
        copy = pltpu.make_async_copy(
            pieces[piece].at[pl.ds(at, rows)], outs[out].at[pl.ds(start, rows)], sems.at[index]
        )
        copy.start()
        copies.append(copy)
    for copy in copies:
        copy.wait()


def place(pieces, moves, sizes):
    width = pieces[0].shape[1]
    if any(at % 16 or rows % 16 for _, at, rows, _, _ in moves):
        outs = [jnp.zeros((size, width), BF) for size in sizes]
        for piece, at, rows, out, offset in moves:
            part = pieces[piece][at : at + rows]
            outs[out] = lax.dynamic_update_slice_in_dim(outs[out], part, offset, 0)
        return outs
    offsets = jnp.stack([move[4] for move in moves]).astype(jnp.int32)
    static = [move[:4] + (None,) for move in moves]
    return pl.pallas_call(
        functools.partial(place_kernel, static, len(pieces), len(sizes)),
        out_shape=[shape_of((size, width), BF) for size in sizes],
        in_specs=[pl.BlockSpec(memory_space=pltpu.SMEM)]
        + [pl.BlockSpec(memory_space=pl.ANY)] * len(pieces),
        out_specs=in_vmem(len(sizes)),
        scratch_shapes=[pltpu.SemaphoreType.DMA((len(moves),))],
        compiler_params=pltpu.CompilerParams(vmem_limit_bytes=40 * MIB),
        cost_estimate=pl.CostEstimate(
            flops=0, bytes_accessed=4 * sum(sizes) * width, transcendentals=0
        ),
        name="place",
    )(offsets, *pieces)


def together_kernel(*refs):
    pass


def together(*arrays, cost=0):
    anywhere = pl.BlockSpec(memory_space=pl.ANY)
    return pl.pallas_call(
        together_kernel,
        out_shape=[shape_of(array.shape, array.dtype) for array in arrays],
        in_specs=[anywhere] * len(arrays),
        out_specs=[anywhere] * len(arrays),
        input_output_aliases={index: index for index in range(len(arrays))},
        cost_estimate=pl.CostEstimate(flops=cost, bytes_accessed=0, transcendentals=0),
        name="together",
    )(*arrays)


def beside(*arrays):
    got = together(*arrays, cost=10**11)
    return got if len(arrays) > 1 else got[0]


def shift(values, step, seq_count):
    return lax.ppermute(
        values, "seq", [(rank, (rank + step) % seq_count) for rank in range(seq_count)]
    )


def swap(values, bit, batch_count):
    return lax.ppermute(values, "batch", [(rank, rank ^ bit) for rank in range(batch_count)])


def line_gather(values, seq_count):
    return [values] + [shift(values, step, seq_count) for step in range(1, seq_count)]


def line_reduce(blocks, seq_count):
    total = blocks[0].astype(F32)
    for step in range(1, seq_count):
        total = total + shift(blocks[step], -step, seq_count).astype(F32)
    return total


def from_own(values, seq_count):
    rank = lax.axis_index("seq")
    blocks = values.reshape(seq_count, -1, values.shape[1])
    return [
        lax.dynamic_index_in_dim(blocks, (rank - step) % seq_count, 0, False)
        for step in range(seq_count)
    ]


def in_line(blocks, seq_count):
    stacked = jnp.stack(blocks)
    rank = lax.axis_index("seq")
    order = (rank - jnp.arange(seq_count, dtype=jnp.int32)) % seq_count
    return jnp.take(stacked, order, axis=0)


def plane_gather(block, bits, batch_count):
    blocks = {0: block}
    for bit in bits:
        for mask in list(blocks):
            blocks[mask ^ bit] = swap(blocks[mask], bit, batch_count)
    return blocks


def plane_reduce(blocks, bits, batch_count):
    blocks = dict(blocks)
    for bit in bits:
        kept = [mask for mask in blocks if not mask & bit]
        rows = blocks[0].shape[0]
        arrived = swap(jnp.concatenate([blocks[mask ^ bit] for mask in kept], axis=0), bit, batch_count)
        blocks = {
            mask: (
                blocks[mask].astype(F32) + arrived[index * rows : (index + 1) * rows].astype(F32)
            ).astype(BF)
            for index, mask in enumerate(kept)
        }
    return blocks[0]


def gather_small(values, batch_count, seq_count):
    return gather_batch(in_line(line_gather(values, seq_count), seq_count), batch_count)


def gather_batch(values, batch_count):
    joined = values[None]
    bit = 1
    while bit < batch_count:
        joined = jnp.concatenate([joined, swap(joined, bit, batch_count)], axis=0)
        bit *= 2
    order = lax.axis_index("batch") ^ jnp.arange(batch_count, dtype=jnp.int32)
    return jnp.take(joined, order, axis=0)


def standardize(values):
    average = jnp.mean(values, axis=-1, keepdims=True)
    centred = values - average
    variance = jnp.mean(centred * centred, axis=-1, keepdims=True)
    inverse = lax.rsqrt(variance + norm_eps)
    return centred * inverse, inverse


def standardize_back(grad, standard, inverse):
    average = jnp.mean(grad, axis=-1, keepdims=True)
    along = jnp.mean(grad * standard, axis=-1, keepdims=True)
    return inverse * (grad - average - standard * along)


def time_token(step_values, model_width):
    half_width = model_width // 2
    frequency = jnp.exp(-math.log(10000.0) * jnp.arange(half_width, dtype=F32) / half_width)
    angles = step_values.astype(F32)[:, None] * frequency[None, :]
    return jnp.concatenate([jnp.cos(angles), jnp.sin(angles)], axis=-1)


def adam_step(parameter, first_state, second, gradient):
    first_new = beta_one * first_state + (1.0 - beta_one) * gradient
    second_new = beta_two * second + (1.0 - beta_two) * gradient * gradient
    first_hat = first_new / (1.0 - beta_one**STEP)
    second_hat = second_new / (1.0 - beta_two**STEP)
    return (
        first_new,
        second_new,
        parameter - adam_rate * first_hat / (jnp.sqrt(second_hat) + adam_eps),
    )


def body(
    patches, timesteps, labels, next_grad, skip_grad, next_extra, skip_extra,
    w_qkv, w_proj, w_up, w_down, mom_qkv, mom_proj, mom_up, mom_down,
    vectors, vec_first, vec_second, table, table_first, table_second,
):
    images, patch_rows, width = patches.shape
    batch_count = lax.axis_size("batch")
    seq_count = lax.axis_size("seq")
    shards = batch_count * seq_count
    batch_rank = lax.axis_index("batch")
    seq_rank = lax.axis_index("seq")
    shard_rank = batch_rank * seq_count + seq_rank
    core = batch_rank % 2
    chips = seq_count // (2 * images)
    own_image = seq_rank // chips
    own_core, own_slot = own_image // images, own_image % images
    sub_rank = seq_rank % chips
    bits = [1 << level for level in range(1, (batch_count - 1).bit_length())]
    up_bits, down_bits = bits, bits[::-1]

    def route(matching):
        pairs = []
        for rank in range(batch_count):
            for place_z in range(seq_count):
                code = place_z ^ matching
                slot, rest = code // (2 * chips), code % (2 * chips)
                to_core, sub = rest // chips, rest % chips
                to_z = ((rank % 2) * images + slot) * chips + sub
                pairs.append((rank * seq_count + place_z, (rank - rank % 2 + to_core) * seq_count + to_z))
        return pairs

    piece_rows = images * patch_rows // seq_count

    def send(values):
        pieces = values.reshape(seq_count, piece_rows, width)
        return [
            lax.ppermute(
                lax.dynamic_index_in_dim(pieces, seq_rank ^ matching, 0, False),
                ("batch", "seq"),
                route(matching),
            )
            for matching in range(seq_count)
        ]

    def send_back(values):
        pieces = jnp.stack([array.reshape(seq_count, piece_rows, width) for array in values], axis=1)
        return [
            lax.ppermute(
                pieces[matching], ("batch", "seq"), [(to, at) for at, to in route(matching)]
            )
            for matching in range(seq_count)
        ]

    def join_back(moved, index):
        moved = jnp.stack([piece[index] for piece in moved])
        pieces = [
            lax.dynamic_index_in_dim(moved, seq_rank ^ code, 0, True) for code in range(seq_count)
        ]
        return jnp.concatenate(pieces, axis=0).reshape(images, patch_rows, width)

    rows = seq_count * piece_rows
    padded = rows + 16

    low_qkv = w_qkv.astype(BF).T
    low_proj = w_proj.astype(BF).T
    unit_width, qkv_width, proj_width = w_up.shape[1], low_qkv.shape[0], low_proj.shape[0]
    column_count = table.shape[1]
    class_count = table.shape[0]
    masks = [level << 1 for level in range(batch_count // 2)]
    offsets = batch_rank ^ jnp.array(masks + [mask ^ 1 for mask in masks], jnp.int32)

    own_mlp = jnp.concatenate([w_up.astype(BF).T, w_down.astype(BF)], axis=0)

    facts = lax.all_gather(jnp.stack([timesteps, labels]), "batch", axis=0)
    all_labels = facts[:, 1].reshape(-1)
    selector = (
        all_labels[:, None] == jnp.arange(class_count, dtype=jnp.int32)[None, :]
    ).astype(BF)
    class_part = dot_nn(selector, table.astype(BF)).astype(BF)
    small = jnp.concatenate([vectors.astype(BF), class_part], axis=0)
    small_rows = -(-small.shape[0] // 16) * 16
    small = jnp.pad(small, ((0, small_rows - small.shape[0]), (0, 128 - column_count)))
    small = jnp.transpose(small.reshape(-1, 16, 128), (1, 0, 2)).reshape(16, -1)
    small = jnp.pad(small, ((0, 0), (0, width - small.shape[1])))

    gap = -(qkv_width + proj_width) % 16
    load = [low_qkv, low_proj] + ([jnp.zeros((gap, width), BF)] if gap else []) + [small]
    line = line_gather(jnp.concatenate(load, axis=0), seq_count)
    former, latter = line_up(
        line, jnp.stack([seq_rank, batch_rank]), qkv_width, proj_width, small_rows // 16, column_count
    )
    former, latter, patches, own_mlp = together(former, latter, patches, own_mlp)

    same_core = [
        [rank * seq_count + at for rank in range(side, batch_count, 2) for at in range(seq_count)]
        for side in (0, 1)
    ]
    all_mlp = lax.all_gather(
        own_mlp, ("batch", "seq"), axis=0, tiled=True, axis_index_groups=same_core
    )
    qkv_rows, proj_rows = qkv_width * seq_count, proj_width * seq_count

    def spread_start(former, latter):
        return (
            {mask: swap(former, mask, batch_count) for mask in bits},
            {mask: swap(latter, mask, batch_count) for mask in bits},
        )

    def spread_rest(former, latter, arrived):
        former_got, latter_got = dict(arrived[0]), dict(arrived[1])
        former_got[0], latter_got[0] = former, latter
        for got, order in ((former_got, bits), (latter_got, bits[::-1])):
            for index, bit in enumerate(order):
                lower = order[:index]
                for mask in [m for m in list(got) if m and not m & bit]:
                    if all(not (mask & other) or other in lower for other in bits):
                        if (mask ^ bit) not in got:
                            got[mask ^ bit] = swap(got[mask], bit, batch_count)
        return former_got, latter_got

    def flat(groups):
        return [group[mask] for group in groups for mask in sorted(group)]

    def unflat(arrays, groups):
        arrays = list(arrays)
        return [{mask: arrays.pop(0) for mask in sorted(group)} for group in groups]

    arrived = spread_start(former, latter)
    moved_patches = send(patches)
    gathered = spread_rest(former, latter, arrived)
    grad_in = (next_grad.astype(F32) + skip_grad.astype(F32)).astype(BF)
    grad_in, *got = together(grad_in, *flat(gathered), *moved_patches)
    moved_patches = jnp.concatenate(got[len(got) - seq_count :], axis=0)
    gathered = unflat(got[: len(got) - seq_count], gathered)
    pieces, moves, small = [], [], 0.0
    unit = former.shape[0]
    rest = qkv_rows - unit
    for group, blocks in enumerate(gathered):
        for mask in masks:
            for side in (0, 1):
                block = swap(blocks[mask], 1, batch_count) if side else blocks[mask]
                target = batch_rank ^ mask ^ side
                number = len(pieces)
                pieces.append(block)
                if group == 0:
                    moves.append((number, 0, unit, 0, target * qkv_rows))
                else:
                    moves.append((number, 0, rest, 0, target * qkv_rows + unit))
                    moves.append((number, rest, proj_rows, 1, target * proj_rows))
                    small = small + block[rest + proj_rows :].astype(F32)
    full_qkv, full_proj = place(pieces, moves, [qkv_rows * batch_count, proj_rows * batch_count])
    vec_values, class_rows = small[:10], small[10 : 10 + images * batch_count]
    home = batch_rank - core + own_core
    own_time = lax.dynamic_index_in_dim(facts[:, 0].reshape(-1), home * images + own_slot, 0, True)
    time_row = time_token(own_time, width)
    class_row = lax.dynamic_index_in_dim(class_rows, home * images + own_slot, 0, True)
    has_extra = sub_rank == 0
    extra_row = jnp.where(core == 0, time_row, class_row) * has_extra.astype(F32)
    row_index = lax.broadcasted_iota(jnp.int32, (padded, 1), 0)
    row_valid = (row_index < rows + has_extra.astype(jnp.int32)).astype(F32)
    first_row = lax.broadcasted_iota(jnp.int32, (16, 1), 0) == 0

    extra_tile = jnp.where(first_row, extra_row, 0.0)
    tokens = jnp.concatenate([moved_patches.astype(F32), extra_tile], axis=0)
    standard_one, inverse_one = standardize(tokens)
    normed = ((standard_one * vec_values[0] + vec_values[1]) * row_valid).astype(BF)
    own_kv = dot_nt(normed, full_qkv[width:]).astype(BF)
    query = dot_nt(normed, full_qkv[:width]).astype(BF)

    def rotate(values, step, core_bit, back):
        pairs = []
        for rank in range(batch_count):
            for place_z in range(seq_count):
                base, sub = place_z - place_z % chips, place_z % chips
                source = (rank ^ core_bit) * seq_count + base + (sub + step) % chips
                here = rank * seq_count + place_z
                pairs.append((here, source) if back else (source, here))
        return lax.ppermute(values, ("batch", "seq"), pairs)

    peers = [(step, bit) for step in range(chips) for bit in (0, 1)][1:]
    own_kv, grad_in = together(own_kv, grad_in)
    moved_grad = send(grad_in)
    other_kv = [rotate(own_kv, step, bit, False) for step, bit in peers]
    valid = jnp.stack(
        [has_extra.astype(jnp.int32)]
        + [((sub_rank + step) % chips == 0).astype(jnp.int32) for step, bit in peers]
    )
    in_extra = (next_extra.astype(F32) + skip_extra.astype(F32)).astype(BF)
    in_extra_other = swap(in_extra, 1, batch_count)
    attended, lse, lse_extra = attention_forward(valid, query, [own_kv, *other_kv])
    attended, in_extra_other, *moved_grad = together(attended, in_extra_other, *moved_grad)
    in_extra = jnp.where(own_core == core, in_extra, in_extra_other)
    in_extra = lax.dynamic_index_in_dim(in_extra, own_slot, 0, False)
    in_extra = lax.dynamic_index_in_dim(in_extra, core, 0, True)
    in_extra = jnp.where(first_row & has_extra, in_extra, jnp.zeros_like(in_extra))
    incoming_low = jnp.concatenate([*moved_grad, in_extra], axis=0)
    incoming = incoming_low.astype(F32)
    other_incoming = swap(incoming_low, 1, batch_count)
    line_order = (seq_rank - jnp.arange(seq_count, dtype=jnp.int32)) % seq_count
    chip_order = (batch_rank ^ jnp.array(masks, jnp.int32)) >> 1
    first_rows = (chip_order[:, None] * seq_count + line_order[None, :]).reshape(-1) * (2 * unit_width)
    all_bias = vec_values[6:].reshape(batch_count // 2, 2, seq_count, unit_width)
    core_bias = lax.dynamic_index_in_dim(all_bias, core, 1, False)
    core_bias = jnp.take(jnp.take(core_bias, chip_order, axis=0), line_order, axis=1).reshape(1, -1)
    middle = tokens + (dot_nt(attended, full_proj) + vec_values[4]) * row_valid
    standard_two, inverse_two = standardize(middle)
    normed_two = ((standard_two * vec_values[2] + vec_values[3]) * row_valid).astype(BF)
    other_normed = swap(normed_two, 1, batch_count)
    out_own, out_other, dn_own, dn_other, grad_up, grad_down, grad_bias = mlp(
        (normed_two, other_normed), (incoming_low, other_incoming), core_bias, all_mlp, first_rows
    )

    def blocks_of(grad):
        parts = grad.reshape(len(masks), -1, width)
        return {mask: parts[index] for index, mask in enumerate(masks)}

    def sum_start(groups):
        moved = []
        for blocks, bit in zip(groups, (bits[-1], bits[0])):
            kept = [mask for mask in masks if not mask & bit]
            moved.append(swap(jnp.concatenate([blocks[mask ^ bit] for mask in kept], axis=0), bit, batch_count))
        return moved

    def sum_add(groups, moved):
        sums = []
        for blocks, arrived, bit in zip(groups, moved, (bits[-1], bits[0])):
            kept = [mask for mask in masks if not mask & bit]
            count = blocks[0].shape[0]
            sums.append(
                {
                    mask: (
                        blocks[mask].astype(F32)
                        + arrived[index * count : (index + 1) * count].astype(F32)
                    ).astype(BF)
                    for index, mask in enumerate(kept)
                }
            )
        return sums

    def sum_rest(groups):
        return [
            plane_reduce(blocks, order, batch_count)
            for blocks, order in zip(groups, (bits[::-1][1:], bits[1:]))
        ]

    def line_blocks(former, latter):
        joined = [values.reshape(seq_count, -1, width) for values in (former, latter)]
        return jnp.concatenate(joined, axis=1)

    mlp_groups = [blocks_of(grad_up), blocks_of(grad_down)]
    moved = sum_start(mlp_groups)
    normed_two_grad = dn_own + swap(dn_other, 1, batch_count).astype(F32)
    middle_grad = incoming + standardize_back(
        normed_two_grad * vec_values[2], standard_two, inverse_two
    )
    middle_low = middle_grad.astype(BF)

    attended_grad = dot_nn(middle_low, full_proj).astype(BF)
    out_arrived = swap(out_other, 1, batch_count)
    backward = attention_backward(valid, query, [own_kv, *other_kv], attended, attended_grad, lse, lse_extra)
    *backward, moved_up, moved_down, out_arrived, middle_low, attended, middle = together(
        *backward, *moved, out_arrived, middle_low, attended, middle
    )
    mlp_groups = sum_add(mlp_groups, [moved_up, moved_down])

    def halves(values):
        cut = values.shape[1] // 32 * 16
        cut = cut if cut else values.shape[1] // 2
        return [
            {mask: part[index] for index, mask in enumerate(masks)}
            for part in (values[:, :cut], values[:, cut:])
        ]

    def next_axis(groups, orders):
        moved = []
        for blocks, order in zip(groups, orders):
            kept = [mask for mask in blocks if not mask & order[0]]
            load = jnp.concatenate([blocks[mask ^ order[0]] for mask in kept], axis=0)
            moved.append(swap(load, order[0], batch_count))
        return moved

    def next_add(groups, orders, moved):
        sums = []
        for blocks, order, arrived in zip(groups, orders, moved):
            kept = [mask for mask in blocks if not mask & order[0]]
            count = blocks[0].shape[0]
            sums.append(
                plane_reduce(
                    {
                        mask: (
                            blocks[mask].astype(F32)
                            + arrived[index * count : (index + 1) * count].astype(F32)
                        ).astype(BF)
                        for index, mask in enumerate(kept)
                    },
                    order[1:],
                    batch_count,
                )
            )
        return sums

    orders = (bits[::-1][1:], bits[1:])
    mlp_moved = next_axis(mlp_groups, orders)
    query_grad, own_dkv = backward[0], backward[1]
    arrived = [rotate(term, step, bit, True) for (step, bit), term in zip(peers, backward[2:])]
    middle_low, attended = beside(middle_low, attended)
    proj_kept, proj_sent = qkv_grad(middle_low, attended, offsets * proj_rows)
    own_dkv, proj_kept, proj_sent, *arrived = together(own_dkv, proj_kept, proj_sent, *arrived)

    proj_arrived = swap(proj_sent, 1, batch_count)
    far_dkv = arrived[0]
    for term in arrived[1:]:
        far_dkv = (far_dkv.astype(F32) + term.astype(F32)).astype(BF)
    packed_grad, kept, sent = packed_grad_of(
        query_grad, own_dkv, far_dkv, normed, offsets * qkv_rows
    )
    packed_grad, kept, sent, proj_kept, proj_arrived, *mlp_moved = together(
        packed_grad, kept, sent, proj_kept, proj_arrived, *mlp_moved
    )

    arrived = swap(sent, 1, batch_count)
    proj_kept, proj_arrived, *mlp_moved = beside(proj_kept, proj_arrived, *mlp_moved)
    mlp_up, mlp_down = next_add(mlp_groups, orders, mlp_moved)
    joined = line_blocks(mlp_up, mlp_down)
    proj_groups = halves((proj_kept.astype(F32) + proj_arrived.astype(F32)).astype(BF))
    joined = [joined[step] for step in range(seq_count)]
    arrived, *joined = together(arrived, *joined)

    groups = halves((kept.astype(F32) + arrived.astype(F32)).astype(BF))
    moved = sum_start(groups)
    near_steps = (1, seq_count - 1)
    far_steps = tuple(range(2, seq_count - 1))
    near_line = [shift(joined[step], -step, seq_count) for step in near_steps]
    first_proj = sum_start(proj_groups)
    packed_grad = beside(packed_grad)
    token_low, norm_sums, extra_grad = first_norm_back(
        packed_grad, full_qkv, standard_one, inverse_one, middle_grad, vec_values[0:1]
    )
    far_line = [joined[step] for step in far_steps]
    moved_up, moved_down, token_low, norm_sums, extra_grad, *got = together(
        *moved, token_low, norm_sums, extra_grad, *near_line, *far_line, *first_proj
    )
    near_line, far_line, first_proj = got[:2], got[2:-2], got[-2:]
    far_line = [shift(part, -step, seq_count) for step, part in zip(far_steps, far_line)]
    bias_parts = jnp.take(grad_bias.reshape(len(masks), seq_count, -1), line_order, axis=1)
    bias_sum = jnp.zeros((batch_count // 2, seq_count, unit_width), F32)
    bias_sum = jnp.take(bias_parts, (batch_rank ^ jnp.arange(0, batch_count, 2)) >> 1, axis=0)
    bias_sum = jnp.where(
        jnp.arange(2, dtype=jnp.int32)[None, :, None, None] == core, bias_sum[:, None], 0.0
    )
    class_slots = jnp.arange(images * batch_count, dtype=jnp.int32) == home * images + own_slot
    holds_class = (core == 1) & has_extra
    class_grad = jnp.where((class_slots & holds_class)[:, None], extra_grad, 0.0)
    vec_grad = jnp.concatenate(
        [
            norm_sums,
            jnp.sum(normed_two_grad * standard_two, axis=0)[None],
            jnp.sum(normed_two_grad, axis=0)[None],
            jnp.sum(middle_low.astype(F32), axis=0)[None],
            jnp.sum(incoming_low.astype(F32), axis=0)[None],
            bias_sum.reshape(4, width),
            class_grad,
        ],
        axis=0,
    )
    sums = next_axis(sum_add(groups, [moved_up, moved_down]), orders)
    proj_groups = sum_add(proj_groups, first_proj)
    proj_up, proj_down = next_axis(proj_groups, orders)
    vec_far = swap(vec_grad, 1, batch_count)
    sums_up, sums_down, vec_far, proj_up, proj_down, *far_line = together(
        *sums, vec_far, proj_up, proj_down, *far_line
    )
    sums = next_add(sum_add(groups, [moved_up, moved_down]), orders, [sums_up, sums_down])
    proj_one, proj_two = next_add(proj_groups, orders, [proj_up, proj_down])
    vec_grad = vec_grad + vec_far

    qkv_parts = from_own(jnp.concatenate(sums, axis=0), seq_count)
    proj_parts = from_own(jnp.concatenate([proj_one, proj_two], axis=0), seq_count)
    late = [jnp.concatenate(parts, axis=0) for parts in zip(qkv_parts, proj_parts)]
    late = [late[0]] + [shift(late[step], -step, seq_count) for step in range(1, seq_count)]
    output = (middle + (out_own + out_arrived.astype(F32) + vec_values[5])).astype(BF)
    for bit in bits:
        vec_grad = vec_grad + swap(vec_grad, bit, batch_count)
    *late, vec_grad, output = together(*late, vec_grad, output)
    total_mlp = functools.reduce(
        jnp.add, [part.astype(F32) for part in (joined[0], *near_line, *far_line)]
    )
    share_up, share_down = total_mlp[:unit_width], total_mlp[unit_width:]

    turned = (mom_qkv.T, mom_proj.T, mom_up.T, mom_down)
    widest = unit_width
    spread = seq_count // 4
    home_plane = [spread * turn for turn in (1, 2, 3, 0)]
    plane_of = {plane: index for index, plane in enumerate(home_plane)}
    held = jnp.take(
        jnp.array([plane_of.get(plane - plane % spread) for plane in range(seq_count)], jnp.int32),
        (seq_rank + jnp.arange(seq_count, dtype=jnp.int32)) % seq_count,
    )

    late = functools.reduce(jnp.add, [part.astype(F32) for part in late])
    shares = (late[:qkv_width], late[qkv_width:], share_up, share_down)
    fresh = [muon_momentum * old + share for old, share in zip(turned, shares)]
    stacked = jnp.stack(
        [jnp.pad(new.astype(BF), ((0, widest - new.shape[0]), (0, 0))) for new in fresh]
    )
    small = lax.dynamic_slice_in_dim(vec_grad, batch_rank * (seq_count * column_count), seq_count * column_count, 1)
    small = jnp.transpose(small.reshape(-1, seq_count, column_count), (1, 0, 2)).reshape(seq_count, -1)
    small = jnp.pad(small, ((0, 0), (0, width - small.shape[1])))
    small_high = small.astype(BF)
    small_low = (small - small_high.astype(F32)).astype(BF)
    y_own = jnp.broadcast_to(output[rows : rows + 1], (seq_count, width))
    small = jnp.pad(jnp.stack([small_high, small_low, y_own], axis=1), ((0, 0), (0, 13), (0, 0)))
    slab = []
    for step in range(seq_count):
        part = lax.dynamic_index_in_dim(stacked, held[step], 0, False)
        rider = lax.dynamic_index_in_dim(small, (seq_rank + step) % seq_count, 0, False)
        part = jnp.concatenate([part, rider], axis=0)
        slab.append(shift(part, step, seq_count) if step else part)
    *slab, token_low, output = together(*slab, token_low, output)
    riders = [part[widest : widest + 3] for part in slab]
    slab = jnp.concatenate([part[:widest] for part in slab], axis=0)
    back_moved = send_back([output[:rows], token_low[:rows]])
    y_line = jnp.stack([part[2:3] for part in riders])
    y_far = swap(y_line, 1, batch_count)

    def plane_sum(kept, sent):
        chip = (kept.astype(F32) + swap(sent, 1, batch_count).astype(F32)).astype(BF)
        total = chip[0].astype(F32)
        for index, mask in enumerate(masks[1:]):
            total = total + swap(chip[index + 1], mask, batch_count).astype(F32)
        total = total.astype(BF)
        near = [total] + [swap(total, mask, batch_count) for mask in masks[1:]]
        return near + [swap(jnp.stack(near), 1, batch_count)]

    unit_offsets = offsets * (packed_rows(width, batch_count) // batch_count)
    slab, kept, sent = first_steps(plane_sum(*gram(slab, unit_offsets)), slab, unit_offsets)
    slab, kept, sent, y_far = together(slab, kept, sent, y_far)
    slab = last_steps(plane_sum(kept, sent), slab, unit_offsets)
    slab, *back_moved = together(slab, *back_moved)
    y_patches, dx_patches = join_back(back_moved, 0), join_back(back_moved, 1)
    back = slab.reshape(seq_count, widest, width)
    back = jnp.stack(
        [back[0]] + [shift(back[step], -step, seq_count) for step in range(1, seq_count)]
    )
    masters = (w_qkv, w_proj, w_up, w_down)
    ratios = (3.0, 1.0, 4.0, 0.25)
    updated = []
    for index in range(4):
        own_part = lax.dynamic_index_in_dim(
            back, (home_plane[index] - seq_rank) % seq_count, 0, False
        )[: fresh[index].shape[0]].astype(F32)
        if index < 3:
            own_part = own_part.T
        factor = math.sqrt(max(1.0, ratios[index]))
        updated.append(
            masters[index] * (1.0 - muon_rate * muon_decay) - muon_rate * factor * own_part
        )

    vec_sum = functools.reduce(
        jnp.add, [part[0].astype(F32) + part[1].astype(F32) for part in riders]
    )
    vec_sum = vec_sum[: vec_grad.shape[0] * column_count].reshape(-1, column_count)
    vec_sum, class_sums = vec_sum[:10], vec_sum[10:]
    chosen = (
        jnp.arange(class_count, dtype=jnp.int32)[:, None] == all_labels[None, :]
    ).astype(F32)
    table_sum = jnp.dot(chosen, class_sums, precision=highest, preferred_element_type=F32)
    y_rows = []
    for slot in range(images):
        turn = (seq_rank - (core * images + slot) * chips) % seq_count
        near = lax.dynamic_index_in_dim(y_line, turn, 0, False)
        far = lax.dynamic_index_in_dim(y_far, turn, 0, False)
        time_y = jnp.where(core == 0, near, far)
        class_y = jnp.where(core == 0, far, near)
        y_rows.append(jnp.concatenate([time_y, class_y], axis=0))
    y_rows = jnp.stack(y_rows)
    vec_new = adam_step(vectors, vec_first, vec_second, vec_sum)
    table_new = adam_step(table, table_first, table_second, table_sum)
    return (
        y_patches,
        y_rows,
        dx_patches,
        *updated,
        fresh[0].T,
        fresh[1].T,
        fresh[2].T,
        fresh[3],
        *vec_new,
        *table_new,
    )


def solution(mesh):
    tokens = P("batch", "seq", None)
    images = P("batch")
    extras = P("batch", None, None)
    columns = P(None, ("batch", "seq"))
    rows = P(("batch", "seq"), None)
    return jax.shard_map(
        body,
        mesh=mesh,
        in_specs=(
            tokens, images, images, tokens, tokens, extras, extras,
            columns, columns, columns, rows, columns, columns, columns, rows,
            columns, columns, columns, columns, columns, columns,
        ),
        out_specs=(
            tokens, extras, tokens, columns, columns, columns, rows,
            columns, columns, columns, rows, columns, columns, columns, columns, columns, columns,
        ),
        check_vma=False,
    )
```
